32 devices in a mesh: section: 4 (over x, core), mp: 8 (over z, y).
Axes of the slice: x: 2, y: 2, z: 4, core: 2. Of those that a mesh axis runs over, the one named last changes fastest.
Arguments:
- queries: bfloat16 [4096, 4096], P(('section', 'mp')), may hold values from -6 to 6
- keys: bfloat16 [1024, 512], P(('section', 'mp')), may hold values from -6 to 6
- values: bfloat16 [1024, 512], P(('section', 'mp')), may hold values from -6 to 6
- seg_image: int32 [4096], P(('section', 'mp')), may hold values from 0 to 3, as said below
- tile_counts: int32 [4], replicated, may hold values from 1 to 4, as said below
- gate: float32 [1], replicated, may hold values from 0.4 to 1.5
- cotangent: bfloat16 [4096, 4096], P(('section', 'mp')), may hold values from -6 to 6
Outputs:
- gated: bfloat16 [4096, 4096], P(('section', 'mp'))
- grad_queries: bfloat16 [4096, 4096], P(('section', 'mp'))
- grad_keys: float32 [1024, 512], P(('section', 'mp'))
- grad_values: float32 [1024, 512], P(('section', 'mp'))
- grad_gate: float32 [1], replicated
The draws below stay inside these ranges and needn't reach their ends.
Inputs may be any that keep to these rules, and one draw needn't show every extreme that they name: `seg_image`: within the 128 tokens of one device, a leading run attends one image and the rest attend one image, possibly the same. Image i holds 64 * tile_counts[i] real tokens at the start of its 256 slots.
All inputs are finite; a program needn't handle non-finite values.
Results may differ from the reference program's by a relative error of at most 0.029.
Values may be sent and summed in bfloat16 or wider, within the bound.
No kernel may reach another device: no remote copies, remote signals or barrier semaphores. Data moves between devices by JAX's collectives and lax.ppermute only.
A program may use at most 64 MiB of HBM per device.

```python
import jax
import jax.numpy as jnp
from jax import lax

HEADS = 32
KV_HEADS = 4
HD = 128
TXT_DEV = 128
TILE_TOK = 64
MAX_TILES = 4
NIMG = 4
IMG_TOK = 256
KEYS = 1024
TEXT = 4096


def shared_signs(key):
    flips = jax.random.bernoulli(key, 0.5, (KV_HEADS * HD,))
    return jnp.where(flips, 1.0, -1.0).astype(jnp.float32)


def base_field(key, shape):
    return jnp.clip(jax.random.normal(key, shape, jnp.float32), -6.0, 6.0)


def draw_queries(key, part):
    signs = shared_signs(key)
    key = jax.random.fold_in(key, 31)
    base = base_field(key, (TEXT, HEADS * HD))
    group = HEADS // KV_HEADS
    lined = jnp.broadcast_to(signs.reshape(KV_HEADS, 1, HD), (KV_HEADS, group, HD)).reshape(HEADS * HD)
    places = jnp.arange(TEXT, dtype=jnp.int32)
    strength = 4.0 + 0.5 * (places // TXT_DEV % 5).astype(jnp.float32)
    planted = places % TXT_DEV == 0
    return jnp.where(planted[:, None], strength[:, None] * lined[None, :], base).astype(jnp.bfloat16)


def draw_keys(key, part):
    signs = shared_signs(key)
    key = jax.random.fold_in(key, 37)
    base = base_field(key, (KEYS, KV_HEADS * HD))
    slots = jnp.arange(KEYS, dtype=jnp.int32) % IMG_TOK
    first_row = jnp.where(slots == 0, 6.0, 0.0).astype(jnp.float32)
    second_row = jnp.where(slots == 1, 5.96875, 0.0).astype(jnp.float32)
    planted = slots < 2
    return jnp.where(planted[:, None], (first_row + second_row)[:, None] * signs[None, :], base).astype(jnp.bfloat16)


def draw_seg_image(key, part):
    key = jax.random.fold_in(key, 11)
    blocks = TEXT // TXT_DEV
    key_b, key_s = jax.random.split(key)
    first = jnp.arange(blocks, dtype=jnp.int32) % NIMG
    second = jax.random.randint(key_b, (blocks,), 0, NIMG, dtype=jnp.int32)
    split = jax.random.randint(key_s, (blocks,), 1, TXT_DEV, dtype=jnp.int32)
    place = jnp.arange(TXT_DEV, dtype=jnp.int32)
    ids = jnp.where(place[None, :] < split[:, None], first[:, None], second[:, None])
    return ids.reshape(TEXT).astype(jnp.int32)


def draw_tile_counts(key, part):
    key = jax.random.fold_in(key, 23)
    key_c, key_p = jax.random.split(key)
    counts = jax.random.randint(key_c, (NIMG,), 1, MAX_TILES + 1, dtype=jnp.int32)
    order = jax.random.permutation(key_p, NIMG)
    counts = counts.at[order[0]].set(MAX_TILES)
    counts = counts.at[order[1]].set(1)
    return counts.astype(jnp.int32)


def steps_of(rng, dims, cuts, least, top_value):
    gain = 1.0
    for dim, blocks in cuts:
        draws = jax.random.uniform(jax.random.fold_in(jax.random.fold_in(rng, 6), dim), (blocks,), jnp.float32, least / len(cuts), top_value / len(cuts))
        gain = gain * jnp.repeat(jnp.exp(draws), dims[dim] // blocks).reshape((-1,) + (1,) * (len(dims) - 1 - dim))
    return gain


def scatter_about(own_key, dims, scale, most, shards=(), held_as=jnp.bfloat16):
    gain = steps_of(own_key, dims, shards, -0.22, 0.18) if shards else 1.0
    drawn = jax.random.normal(own_key, dims, jnp.float32) * scale * gain
    return jnp.minimum(jnp.maximum(drawn, -most), most).astype(held_as)


def setup_inputs(seed: int = 0) -> dict:
    arg_keys = jax.random.split(jax.random.key(seed), 8)
    return {
        "queries": draw_queries(jax.random.fold_in(arg_keys[7], 71), 0),
        "keys": draw_keys(jax.random.fold_in(arg_keys[7], 71), 0),
        "values": scatter_about(arg_keys[2], (KEYS, KV_HEADS * HD), 1.0, 6.0, ((0, 32),)),
        "seg_image": draw_seg_image(jax.random.fold_in(arg_keys[7], 71), 0),
        "tile_counts": draw_tile_counts(jax.random.fold_in(arg_keys[7], 71), 0),
        "gate": jnp.clip(jax.random.uniform(arg_keys[5], (1,), jnp.float32, 0.4, 1.5), 0.4, 1.5),
        "cotangent": scatter_about(arg_keys[6], (TEXT, HEADS * HD), 1.0, 6.0, ((0, 32),)),
    }


def attend(q, k, v, dy, valid, tg, scale):
    qf = q.astype(jnp.float32)
    kf = k.astype(jnp.float32)
    vf = v.astype(jnp.float32)
    s = jnp.einsum('tkgd,nkd->kgtn', qf, kf) * scale
    s = jnp.where(valid, s, -1e30)
    top = jnp.max(s, axis=-1, keepdims=True)
    e = jnp.where(valid, jnp.exp(s - top), 0.0)
    p = e / jnp.sum(e, axis=-1, keepdims=True)
    p16 = p.astype(jnp.bfloat16).astype(jnp.float32)
    o = jnp.einsum('kgtn,nkd->tkgd', p16, vf)
    y = (tg * o).astype(jnp.bfloat16)
    do16 = (tg * dy.astype(jnp.float32)).astype(jnp.bfloat16).astype(jnp.float32)
    dp = jnp.einsum('tkgd,nkd->kgtn', do16, vf)
    delta = jnp.einsum('tkgd,tkgd->kgt', do16, o)
    ds16 = (scale * p * (dp - delta[..., None])).astype(jnp.bfloat16).astype(jnp.float32)
    dq = jnp.einsum('kgtn,nkd->tkgd', ds16, kf).astype(jnp.bfloat16)
    dk = jnp.einsum('kgtn,tkgd->nkd', ds16, qf)
    dv = jnp.einsum('kgtn,tkgd->nkd', p16, do16)
    gterm = jnp.sum(dy.astype(jnp.float32) * o)
    return y, dq, dk, dv, gterm


def reference(queries, keys, values, seg_image, tile_counts, gate, cotangent):
    tg = jnp.tanh(gate[0])
    group = HEADS // KV_HEADS
    scale = 1.0 / (HD ** 0.5)
    blocks = TEXT // TXT_DEV
    qb = queries.reshape(blocks, TXT_DEV, KV_HEADS, group, HD)
    db = cotangent.reshape(blocks, TXT_DEV, KV_HEADS, group, HD)
    sb = seg_image.reshape(blocks, TXT_DEV)
    keys3 = keys.reshape(KEYS, KV_HEADS, HD)
    values3 = values.reshape(KEYS, KV_HEADS, HD)
    slot_pos = jnp.arange(IMG_TOK, dtype=jnp.int32)

    def step(carry, xs):
        dk_acc, dv_acc, gsum = carry
        q, dy, seg = xs
        first = seg[0].astype(jnp.int32)
        last = seg[TXT_DEV - 1].astype(jnp.int32)
        start_a = (first * IMG_TOK).astype(jnp.int32)
        start_b = (last * IMG_TOK).astype(jnp.int32)
        k_sel = jnp.concatenate([lax.dynamic_slice_in_dim(keys3, start_a, IMG_TOK, 0), lax.dynamic_slice_in_dim(keys3, start_b, IMG_TOK, 0)], 0)
        v_sel = jnp.concatenate([lax.dynamic_slice_in_dim(values3, start_a, IMG_TOK, 0), lax.dynamic_slice_in_dim(values3, start_b, IMG_TOK, 0)], 0)
        key_image = jnp.concatenate([jnp.full((IMG_TOK,), 1, jnp.int32) * first, jnp.full((IMG_TOK,), 1, jnp.int32) * last])
        key_pos = jnp.concatenate([slot_pos, slot_pos])
        keep = jnp.concatenate([jnp.ones((IMG_TOK,), bool), jnp.full((IMG_TOK,), True) & (last != first)])
        limit = tile_counts[key_image] * TILE_TOK
        valid = (key_image[None, :] == seg[:, None]) & (key_pos < limit)[None, :] & keep[None, :]
        y, dq, dk, dv, gterm = attend(q, k_sel, v_sel, dy, valid, tg, scale)
        dk_acc = lax.dynamic_update_slice_in_dim(dk_acc, lax.dynamic_slice_in_dim(dk_acc, start_a, IMG_TOK, 0) + dk[:IMG_TOK], start_a, 0)
        dk_acc = lax.dynamic_update_slice_in_dim(dk_acc, lax.dynamic_slice_in_dim(dk_acc, start_b, IMG_TOK, 0) + dk[IMG_TOK:], start_b, 0)
        dv_acc = lax.dynamic_update_slice_in_dim(dv_acc, lax.dynamic_slice_in_dim(dv_acc, start_a, IMG_TOK, 0) + dv[:IMG_TOK], start_a, 0)
        dv_acc = lax.dynamic_update_slice_in_dim(dv_acc, lax.dynamic_slice_in_dim(dv_acc, start_b, IMG_TOK, 0) + dv[IMG_TOK:], start_b, 0)
        return (dk_acc, dv_acc, gsum + gterm), (y, dq)

    zeros = jnp.zeros((KEYS, KV_HEADS, HD), jnp.float32)
    (dk_acc, dv_acc, gsum), (ys, dqs) = lax.scan(step, (zeros, zeros, jnp.zeros((), jnp.float32)), (qb, db, sb))
    gated = ys.reshape(TEXT, HEADS * HD)
    grad_queries = dqs.reshape(TEXT, HEADS * HD)
    grad_gate = ((1.0 - tg * tg) * gsum).reshape(1)
    return gated, grad_queries, dk_acc.reshape(KEYS, KV_HEADS * HD), dv_acc.reshape(KEYS, KV_HEADS * HD), grad_gate
```

```python
import functools

import jax
import jax.numpy as jnp
from jax import lax
from jax.experimental import pallas as pl
from jax.experimental.pallas import tpu as pltpu
from jax.sharding import PartitionSpec as P

KV_HEADS = 4
TILE_TOK = 64
IMG_TOK = 256
AXES = ("section", "mp")
NEG = -1e30
LOG2E = 1.4426950408889634

NT = (((1,), (1,)), ((), ()))
NN = (((1,), (0,)), ((), ()))
TN = (((0,), (0,)), ((), ()))


def mm(a, b, dims):
    return lax.dot_general(a, b, dims, preferred_element_type=jnp.float32)


def attend_kernel(
    folded,
    seg_s,
    cnt_s,
    gate_s,
    seg_v,
    q_ref,
    dy_ref,
    own,
    other,
    y_ref,
    dq_ref,
    part_own,
    part_other,
    g_ref,
    kv,
    acc,
    qc,
    dc,
    p16,
    ds16,
    bias,
    rowsel,
    sems,
):
    step = pl.program_id(0)
    last = pl.num_programs(0) - 1
    tokens = q_ref.shape[0]
    slots, width = kv.shape[1], kv.shape[2] // 2
    hd = width // KV_HEADS
    group = q_ref.shape[1] // hd
    scale = 1.0 / hd**0.5
    section = lax.axis_index("section")
    core, xpos = section % 2, section // 2
    img_a, img_b = seg_s[0], seg_s[tokens - 1]

    def place(img):
        return ((img % 2) ^ core), ((img // 2) ^ xpos)

    def fetch(i, img, start):
        par, dx = place(img)

        @pl.when(par == 0)
        def _():
            c = pltpu.make_async_copy(own.at[dx], kv.at[i], sems.at[i])
            c.start() if start else c.wait()

        @pl.when(par != 0)
        def _():
            c = pltpu.make_async_copy(other.at[dx], kv.at[i], sems.at[i])
            c.start() if start else c.wait()

    in_a = seg_v[...] == img_a
    tg = jnp.tanh(jnp.full((1, hd), gate_s[0], jnp.float32))

    @pl.when(step == 0)
    def _():
        fetch(0, img_a, True)
        fetch(1, img_b, True)
        acc[...] = jnp.zeros_like(acc)
        g_ref[...] = jnp.zeros_like(g_ref)
        n = lax.broadcasted_iota(jnp.int32, (slots, tokens), 0)
        if folded:
            zpos = lax.axis_index("mp") // 2
            per = slots // 8
            tile = ((n // per) % 4) ^ zpos
        else:
            tile = n // TILE_TOK
        limit = jnp.where(in_a, cnt_s[img_a], cnt_s[img_b])
        bias[...] = jnp.where(tile < limit, 0.0, NEG)
        rowsel[...] = jnp.broadcast_to(in_a.astype(jnp.float32), (hd, tokens)).T
        fetch(0, img_a, False)
        fetch(1, img_b, False)

    rows_a = rowsel[...] > 0.5
    kcols = pl.ds(pl.multiple_of(step * hd, hd), hd)
    vcols = pl.ds(pl.multiple_of(width + step * hd, hd), hd)
    kcat = jnp.concatenate([kv[0, :, kcols], kv[1, :, kcols]], axis=1)
    vcat = jnp.concatenate([kv[0, :, vcols], kv[1, :, vcols]], axis=1)
    kcat_t = kcat.astype(jnp.float32).T.astype(jnp.bfloat16)
    vcat_t = vcat.astype(jnp.float32).T.astype(jnp.bfloat16)
    zero = jnp.zeros((tokens, hd), jnp.bfloat16)
    for g in range(group):
        cols = slice(g * hd, (g + 1) * hd)
        rows = slice(g * tokens, (g + 1) * tokens)
        q = q_ref[:, cols]
        dy = dy_ref[:, cols].astype(jnp.float32)
        do = (tg * dy).astype(jnp.bfloat16)
        qc[rows, :hd] = jnp.where(rows_a, q, zero)
        qc[rows, hd:] = jnp.where(rows_a, zero, q)
        dc[rows, :hd] = jnp.where(rows_a, do, zero)
        dc[rows, hd:] = jnp.where(rows_a, zero, do)

    pair = 2
    gsum = jnp.zeros((tokens, hd), jnp.float32)
    in_a2 = jnp.concatenate([in_a] * pair, axis=1)
    for h in range(0, group, pair):
        rows = slice(h * tokens, (h + pair) * tokens)
        s = mm(kcat, qc[rows, :], NT)
        s = s + jnp.concatenate([bias[...]] * pair, axis=1)
        top = jnp.max(s, axis=0, keepdims=True)
        e = jnp.exp2((s - top) * (scale * LOG2E))
        p = e * (1.0 / jnp.sum(e, axis=0, keepdims=True))
        ph = p.astype(jnp.bfloat16)
        p16[:, rows] = ph
        dp = mm(vcat, dc[rows, :], NT)
        delta = jnp.sum(ph.astype(jnp.float32) * dp, axis=0, keepdims=True)
        dsh = (scale * p * (dp - delta)).astype(jnp.bfloat16)
        ds16[:, rows] = dsh
        o = mm(vcat_t, ph, NN)
        o = jnp.where(in_a2, o[:hd], o[hd:])
        dq = mm(kcat_t, dsh, NN)
        dq = jnp.where(in_a2, dq[:hd], dq[hd:])
        for j in range(pair):
            cols = slice((h + j) * hd, (h + j + 1) * hd)
            toks = slice(j * tokens, (j + 1) * tokens)
            ot = o[:, toks].T
            y_ref[:, cols] = (tg * ot).astype(jnp.bfloat16)
            gsum = gsum + dy_ref[:, cols].astype(jnp.float32) * ot
            dq_ref[:, cols] = dq[:, toks].T.astype(jnp.bfloat16)
    g_ref[...] += jnp.sum(gsum.reshape(tokens // 8, 8, hd), axis=0)
    dk = mm(ds16[...], qc[...], NN)
    dv = mm(p16[...], dc[...], NN)
    par_a, dx_a = place(img_a)
    par_b, dx_b = place(img_b)
    at_a, at_b = par_a * 2 + dx_a, par_b * 2 + dx_b
    acc[at_b, :, kcols] = dk[:, hd:].astype(jnp.bfloat16)
    acc[at_b, :, vcols] = dv[:, hd:].astype(jnp.bfloat16)
    acc[at_a, :, kcols] = dk[:, :hd].astype(jnp.bfloat16)
    acc[at_a, :, vcols] = dv[:, :hd].astype(jnp.bfloat16)

    @pl.when(step == last)
    def _():
        c1 = pltpu.make_async_copy(acc.at[pl.ds(2, 2)], part_other, sems.at[2])
        c0 = pltpu.make_async_copy(acc.at[pl.ds(0, 2)], part_own, sems.at[3])
        c1.start()
        c0.start()
        c1.wait()
        c0.wait()


def attend(folded, seg, counts, gate, q, dy, own, other):
    tokens, feats = q.shape
    slots, width2 = own.shape[1], own.shape[2]
    hd = width2 // 2 // KV_HEADS
    block = feats // KV_HEADS
    rows = block // hd * tokens
    smem = pl.BlockSpec(memory_space=pltpu.SMEM)
    hbm = pl.BlockSpec(memory_space=pl.ANY)
    cut = pl.BlockSpec((tokens, block), lambda i: (0, i))
    flops = 12 * KV_HEADS * rows * slots * hd * 2
    return pl.pallas_call(
        functools.partial(attend_kernel, folded),
        grid=(KV_HEADS,),
        in_specs=[
            smem,
            smem,
            smem,
            pl.BlockSpec((1, tokens), lambda i: (0, 0)),
            cut,
            cut,
            hbm,
            hbm,
        ],
        out_specs=[cut, cut, hbm, hbm, pl.BlockSpec((8, hd), lambda i: (0, 0))],
        out_shape=[
            jax.ShapeDtypeStruct(q.shape, jnp.bfloat16),
            jax.ShapeDtypeStruct(q.shape, jnp.bfloat16),
            jax.ShapeDtypeStruct(own.shape, jnp.bfloat16),
            jax.ShapeDtypeStruct(own.shape, jnp.bfloat16),
            jax.ShapeDtypeStruct((8, hd), jnp.float32),
        ],
        scratch_shapes=[
            pltpu.VMEM((2, slots, width2), jnp.bfloat16),
            pltpu.VMEM((4, slots, width2), jnp.bfloat16),
            pltpu.VMEM((rows, 2 * hd), jnp.bfloat16),
            pltpu.VMEM((rows, 2 * hd), jnp.bfloat16),
            pltpu.VMEM((slots, rows), jnp.bfloat16),
            pltpu.VMEM((slots, rows), jnp.bfloat16),
            pltpu.VMEM((slots, tokens), jnp.float32),
            pltpu.VMEM((tokens, hd), jnp.float32),
            pltpu.SemaphoreType.DMA((4,)),
        ],
        compiler_params=pltpu.CompilerParams(
            dimension_semantics=("arbitrary",), vmem_limit_bytes=32 * 1024 * 1024
        ),
        cost_estimate=pl.CostEstimate(
            flops=flops,
            bytes_accessed=8 * q.size + 8 * own.size,
            transcendentals=KV_HEADS * rows * slots,
        ),
    )(seg, counts, gate, seg.reshape(1, tokens), q, dy, own, other)


def local(mp, queries, keys, values, seg_image, tile_counts, gate, cotangent):
    f32, bf16 = jnp.float32, jnp.bfloat16
    width = keys.shape[1]
    mine = keys.shape[0]
    folded = mp == 8

    def send_z(x, k):
        perm = [(m, ((m // 2) ^ k) * 2 + m % 2) for m in range(mp)]
        return lax.ppermute(x, "mp", perm)

    def send_xy(x, dx, dy):
        perm = []
        for s in range(4):
            for m in range(mp):
                perm.append((s * mp + m, (s ^ (2 * dx)) * mp + (m ^ dy)))
        return lax.ppermute(x, AXES, perm)

    def send_core(x):
        return lax.ppermute(x, "section", [(s, s ^ 1) for s in range(4)])

    kv = jnp.concatenate([keys, values], axis=1)
    if folded:
        col = jnp.concatenate([kv] + [send_z(kv, k) for k in (1, 2, 3)], axis=0)
        parts = [col] + [send_xy(col, dx, dy) for dx, dy in ((0, 1), (1, 0), (1, 1))]
        own = jnp.concatenate(parts, axis=0)
    else:
        col = lax.all_gather(kv, "mp", axis=0, tiled=True)
        own = jnp.concatenate([col, send_xy(col, 1, 0)], axis=0)
    own = own.reshape(2, IMG_TOK, 2 * width)
    other = send_core(own)

    y, dq, part_own, part_other, gpart = attend(
        folded, seg_image, tile_counts, gate, queries, cotangent, own, other
    )

    got = send_core(part_other)
    gsum = gpart + send_core(gpart)
    both = (part_own.astype(f32) + got.astype(f32)).astype(bf16)
    if folded:
        cut = both.reshape(4, 4 * mine, 2 * width)
        order = ((0, 1), (1, 0), (1, 1))
        recv = [send_xy(cut[2 * dx + dy], dx, dy) for dx, dy in order]
        total = cut[0].astype(f32)
        for r in recv:
            total = total + r.astype(f32)
        gsum = gsum + sum(send_xy(gsum, dx, dy) for dx, dy in order)
        cut = total.astype(bf16).reshape(4, mine, 2 * width)
        recv = [send_z(cut[k], k) for k in (1, 2, 3)]
        owned = cut[0].astype(f32)
        for r in recv:
            owned = owned + r.astype(f32)
        gsum = gsum + sum(send_z(gsum, k) for k in (1, 2, 3))
    else:
        total = both[0].astype(f32) + send_xy(both[1], 1, 0).astype(f32)
        owned = lax.psum_scatter(total, "mp", scatter_dimension=0, tiled=True)
        gsum = lax.psum(gsum + send_xy(gsum, 1, 0), "mp")
    tg = jnp.tanh(gate[0])
    grad_gate = ((1.0 - tg * tg) * jnp.sum(gsum)).reshape(1)
    return (y, dq, owned[:, :width], owned[:, width:], grad_gate)


def solution(mesh):
    rows = P(AXES, None)
    return jax.shard_map(
        functools.partial(local, mesh.shape["mp"]),
        mesh=mesh,
        in_specs=(rows, rows, rows, P(AXES), P(), P(), rows),
        out_specs=(rows, rows, rows, rows, P()),
        check_vma=False,
    )
```

```python
import functools

import jax
import jax.numpy as jnp
from jax import lax
from jax.experimental import pallas as pl
from jax.experimental.pallas import tpu as pltpu
from jax.sharding import Mesh
from jax.sharding import PartitionSpec as P

KV_HEADS = 4
TILE_TOK = 64
IMG_TOK = 256
AXES = ("x", "core", "z", "y")
NEG = -1e30
LOG2E = 1.4426950408889634

NT = (((1,), (1,)), ((), ()))
NN = (((1,), (0,)), ((), ()))
TN = (((0,), (0,)), ((), ()))


def mm(a, b, dims):
    return lax.dot_general(a, b, dims, preferred_element_type=jnp.float32)


def attend_kernel(
    mine,
    cols,
    seg_s,
    cnt_s,
    gate_s,
    seg_v,
    q_ref,
    dy_ref,
    own,
    other,
    y_ref,
    dq_ref,
    part_own,
    part_other,
    g_ref,
    kv,
    acc,
    qc,
    dc,
    p16,
    ds16,
    bias,
    rowsel,
    sems,
):
    step = pl.program_id(0)
    last = pl.num_programs(0) - 1
    tokens = q_ref.shape[0]
    slots, width = kv.shape[1], kv.shape[2] // 2
    hd = width // KV_HEADS
    group = q_ref.shape[1] // hd
    scale = 1.0 / hd**0.5
    core = lax.axis_index("core")
    img_a, img_b = seg_s[0], seg_s[tokens - 1]

    def place(img):
        return (img % 2) ^ core, img // 2

    def fetch(i, img, start):
        par, dx = place(img)

        @pl.when(par == 0)
        def _():
            c = pltpu.make_async_copy(own.at[dx], kv.at[i], sems.at[i])
            c.start() if start else c.wait()

        @pl.when(par != 0)
        def _():
            c = pltpu.make_async_copy(other.at[dx], kv.at[i], sems.at[i])
            c.start() if start else c.wait()

    in_a = seg_v[...] == img_a
    tg = jnp.tanh(jnp.full((1, hd), gate_s[0], jnp.float32))

    @pl.when(step == 0)
    def _():
        fetch(0, img_a, True)
        fetch(1, img_b, True)
        acc[...] = jnp.zeros_like(acc)
        g_ref[...] = jnp.zeros_like(g_ref)
        n = lax.broadcasted_iota(jnp.int32, (slots, tokens), 0)
        outer, inner = n // mine, n % mine
        place_n = (outer % cols) * (2 * mine) + (outer // cols) * mine + inner
        tile = place_n // TILE_TOK
        limit = jnp.where(in_a, cnt_s[img_a], cnt_s[img_b])
        bias[...] = jnp.where(tile < limit, 0.0, NEG)
        rowsel[...] = jnp.broadcast_to(in_a.astype(jnp.float32), (hd, tokens)).T
        fetch(0, img_a, False)
        fetch(1, img_b, False)

    rows_a = rowsel[...] > 0.5
    kcols = pl.ds(pl.multiple_of(step * hd, hd), hd)
    vcols = pl.ds(pl.multiple_of(width + step * hd, hd), hd)
    kcat = jnp.concatenate([kv[0, :, kcols], kv[1, :, kcols]], axis=1)
    vcat = jnp.concatenate([kv[0, :, vcols], kv[1, :, vcols]], axis=1)
    kcat_t = kcat.astype(jnp.float32).T.astype(jnp.bfloat16)
    vcat_t = vcat.astype(jnp.float32).T.astype(jnp.bfloat16)
    zero = jnp.zeros((tokens, hd), jnp.bfloat16)
    for g in range(group):
        feats = slice(g * hd, (g + 1) * hd)
        rows = slice(g * tokens, (g + 1) * tokens)
        q = q_ref[:, feats]
        dy = dy_ref[:, feats].astype(jnp.float32)
        do = (tg * dy).astype(jnp.bfloat16)
        qc[rows, :hd] = jnp.where(rows_a, q, zero)
        qc[rows, hd:] = jnp.where(rows_a, zero, q)
        dc[rows, :hd] = jnp.where(rows_a, do, zero)
        dc[rows, hd:] = jnp.where(rows_a, zero, do)

    pair = 2
    gsum = jnp.zeros((tokens, hd), jnp.float32)
    in_a2 = jnp.concatenate([in_a] * pair, axis=1)
    for h in range(0, group, pair):
        rows = slice(h * tokens, (h + pair) * tokens)
        s = mm(kcat, qc[rows, :], NT)
        s = s + jnp.concatenate([bias[...]] * pair, axis=1)
        top = jnp.max(s, axis=0, keepdims=True)
        e = jnp.exp2((s - top) * (scale * LOG2E))
        p = e * (1.0 / jnp.sum(e, axis=0, keepdims=True))
        ph = p.astype(jnp.bfloat16)
        p16[:, rows] = ph
        dp = mm(vcat, dc[rows, :], NT)
        delta = jnp.sum(ph.astype(jnp.float32) * dp, axis=0, keepdims=True)
        dsh = (scale * p * (dp - delta)).astype(jnp.bfloat16)
        ds16[:, rows] = dsh
        o = mm(vcat_t, ph, NN)
        o = jnp.where(in_a2, o[:hd], o[hd:])
        dq = mm(kcat_t, dsh, NN)
        dq = jnp.where(in_a2, dq[:hd], dq[hd:])
        for j in range(pair):
            feats = slice((h + j) * hd, (h + j + 1) * hd)
            toks = slice(j * tokens, (j + 1) * tokens)
            ot = o[:, toks].T
            y_ref[:, feats] = (tg * ot).astype(jnp.bfloat16)
            gsum = gsum + dy_ref[:, feats].astype(jnp.float32) * ot
            dq_ref[:, feats] = dq[:, toks].T.astype(jnp.bfloat16)
    g_ref[...] += jnp.sum(gsum.reshape(tokens // 8, 8, hd), axis=0)
    dk = mm(ds16[...], qc[...], NN)
    dv = mm(p16[...], dc[...], NN)
    par_a, dx_a = place(img_a)
    par_b, dx_b = place(img_b)
    at_a, at_b = par_a * 2 + dx_a, par_b * 2 + dx_b
    acc[at_b, :, kcols] = dk[:, hd:].astype(jnp.bfloat16)
    acc[at_b, :, vcols] = dv[:, hd:].astype(jnp.bfloat16)
    acc[at_a, :, kcols] = dk[:, :hd].astype(jnp.bfloat16)
    acc[at_a, :, vcols] = dv[:, :hd].astype(jnp.bfloat16)

    @pl.when(step == last)
    def _():
        c1 = pltpu.make_async_copy(acc.at[pl.ds(2, 2)], part_other, sems.at[2])
        c0 = pltpu.make_async_copy(acc.at[pl.ds(0, 2)], part_own, sems.at[3])
        c1.start()
        c0.start()
        c1.wait()
        c0.wait()


def attend(mine, cols, seg, counts, gate, q, dy, own, other):
    tokens, feats = q.shape
    slots, width2 = own.shape[1], own.shape[2]
    hd = width2 // 2 // KV_HEADS
    block = feats // KV_HEADS
    rows = block // hd * tokens
    smem = pl.BlockSpec(memory_space=pltpu.SMEM)
    hbm = pl.BlockSpec(memory_space=pl.ANY)
    cut = pl.BlockSpec((tokens, block), lambda i: (0, i))
    flops = 12 * KV_HEADS * rows * slots * hd * 2
    return pl.pallas_call(
        functools.partial(attend_kernel, mine, cols),
        grid=(KV_HEADS,),
        in_specs=[
            smem,
            smem,
            smem,
            pl.BlockSpec((1, tokens), lambda i: (0, 0)),
            cut,
            cut,
            hbm,
            hbm,
        ],
        out_specs=[cut, cut, hbm, hbm, pl.BlockSpec((8, hd), lambda i: (0, 0))],
        out_shape=[
            jax.ShapeDtypeStruct(q.shape, jnp.bfloat16),
            jax.ShapeDtypeStruct(q.shape, jnp.bfloat16),
            jax.ShapeDtypeStruct(own.shape, jnp.bfloat16),
            jax.ShapeDtypeStruct(own.shape, jnp.bfloat16),
            jax.ShapeDtypeStruct((8, hd), jnp.float32),
        ],
        scratch_shapes=[
            pltpu.VMEM((2, slots, width2), jnp.bfloat16),
            pltpu.VMEM((4, slots, width2), jnp.bfloat16),
            pltpu.VMEM((rows, 2 * hd), jnp.bfloat16),
            pltpu.VMEM((rows, 2 * hd), jnp.bfloat16),
            pltpu.VMEM((slots, rows), jnp.bfloat16),
            pltpu.VMEM((slots, rows), jnp.bfloat16),
            pltpu.VMEM((slots, tokens), jnp.float32),
            pltpu.VMEM((tokens, hd), jnp.float32),
            pltpu.SemaphoreType.DMA((4,)),
        ],
        compiler_params=pltpu.CompilerParams(
            dimension_semantics=("arbitrary",), vmem_limit_bytes=32 * 1024 * 1024
        ),
        cost_estimate=pl.CostEstimate(
            flops=flops,
            bytes_accessed=8 * q.size + 8 * own.size,
            transcendentals=KV_HEADS * rows * slots,
        ),
    )(seg, counts, gate, seg.reshape(1, tokens), q, dy, own, other)


def local(queries, keys, values, seg_image, tile_counts, gate, cotangent):
    f32, bf16 = jnp.float32, jnp.bfloat16
    mine, width = keys.shape
    cols = lax.axis_size("z")

    def send_core(x):
        return lax.ppermute(x, "core", [(0, 1), (1, 0)])

    kv = jnp.concatenate([keys, values], axis=1)
    kv = jnp.broadcast_to(kv[None], (cols,) + kv.shape)
    col = lax.all_to_all(kv, "z", 0, 0, tiled=True)
    col = jnp.broadcast_to(col[None], (4,) + col.shape)
    own = lax.all_to_all(col, ("x", "y"), 0, 0, tiled=True)
    own = own.reshape(2, IMG_TOK, 2 * width)
    other = send_core(own)

    y, dq, part_own, part_other, gpart = attend(
        mine, cols, seg_image, tile_counts, gate, queries, cotangent, own, other
    )

    got = send_core(part_other)
    gates = jnp.broadcast_to(gpart[None], (4 * 2 * cols,) + gpart.shape)
    gates = lax.all_to_all(gates, ("x", "core", "z", "y"), 0, 0, tiled=True)
    both = (part_own.astype(f32) + got.astype(f32)).astype(bf16)
    both = both.reshape(4, cols, mine, 2 * width)
    both = lax.all_to_all(both, ("x", "y"), 0, 0, tiled=True)
    total = jnp.sum(both.astype(f32), axis=0).astype(bf16)
    total = lax.all_to_all(total, "z", 0, 0, tiled=True)
    owned = jnp.sum(total.astype(f32), axis=0)
    tg = jnp.tanh(gate[0])
    grad_gate = ((1.0 - tg * tg) * jnp.sum(gates)).reshape(1)
    return (y, dq, owned[:, :width], owned[:, width:], grad_gate)


def solution(mesh):
    section, mp = mesh.shape["section"], mesh.shape["mp"]
    fine = Mesh(mesh.devices.reshape(section // 2, 2, mp // 2, 2), AXES)
    rows = P(AXES, None)
    return jax.shard_map(
        local,
        mesh=fine,
        in_specs=(rows, rows, rows, P(AXES), P(), P(), rows),
        out_specs=(rows, rows, rows, rows, P()),
        check_vma=False,
    )
```

```python
import functools

import jax
import jax.numpy as jnp
from jax import lax
from jax.experimental import pallas as pl
from jax.experimental.pallas import tpu as pltpu
from jax.sharding import Mesh
from jax.sharding import PartitionSpec as P

KV_HEADS = 4
TILE_TOK = 64
IMG_TOK = 256
AXES = ("x", "core", "z", "y")
NEG = -1e30
LOG2E = 1.4426950408889634
CHUNKS = 2
GROWS = 16
GTOP = 8
PEERS = ((0, 1), (1, 0), (1, 1))

NT = (((1,), (1,)), ((), ()))
NN = (((1,), (0,)), ((), ()))


def mm(a, b, dims):
    return lax.dot_general(a, b, dims, preferred_element_type=jnp.float32)


def attend_kernel(
    mine,
    cols,
    folded,
    first,
    seg_s,
    cnt_s,
    gate_s,
    seg_v,
    q_ref,
    dy_ref,
    own,
    other,
    g_in,
    y_in,
    dq_in,
    y_ref,
    dq_ref,
    part_own,
    part_other,
    g_ref,
    kv,
    acc,
    qc,
    dc,
    p16,
    ds16,
    bias,
    rowsel,
    sems,
):
    step = pl.program_id(0)
    heads = kv.shape[2] // (2 * q_ref.shape[0])
    last = heads - 1
    tokens = q_ref.shape[0]
    slots, width = kv.shape[1], kv.shape[2] // 2
    half = slots // 2
    hd = width // heads
    group = q_ref.shape[1] // hd
    scale = 1.0 / hd**0.5
    core, xpos = lax.axis_index("core"), lax.axis_index("x")
    img_a, img_b = seg_s[0], seg_s[tokens - 1]

    def place(img):
        return (img % 2) ^ core, (img // 2) ^ xpos

    def fetch(i, img, start):
        par, dx = place(img)

        @pl.when(par == 0)
        def _():
            c = pltpu.make_async_copy(own.at[dx], kv.at[i], sems.at[i])
            c.start() if start else c.wait()

        @pl.when(par != 0)
        def _():
            c = pltpu.make_async_copy(other.at[dx], kv.at[i], sems.at[i])
            c.start() if start else c.wait()

    in_a = seg_v[...] == img_a
    tg = jnp.tanh(jnp.full((1, hd), gate_s[0], jnp.float32))

    @pl.when(step == 0)
    def _():
        fetch(0, img_a, True)
        fetch(1, img_b, True)
        acc[...] = jnp.zeros_like(acc)
        g_ref[...] = jnp.zeros_like(g_ref) if first else g_in[...]
        n = lax.broadcasted_iota(jnp.int32, (slots, tokens), 0)
        zi = (n // mine) % cols
        yi = (n // half) ^ lax.axis_index("y")
        if folded:
            zi = zi ^ lax.axis_index("z")
        tile = (zi * (2 * mine) + yi * mine + n % mine) // TILE_TOK
        limit = jnp.where(in_a, cnt_s[img_a], cnt_s[img_b])
        bias[...] = jnp.where(tile < limit, 0.0, NEG)
        rowsel[...] = jnp.broadcast_to(in_a.astype(jnp.float32), (hd, tokens)).T
        fetch(0, img_a, False)
        fetch(1, img_b, False)

    rows_a = rowsel[...] > 0.5
    kcols = pl.ds(pl.multiple_of(step * hd, hd), hd)
    vcols = pl.ds(pl.multiple_of(width + step * hd, hd), hd)
    kcat = jnp.concatenate([kv[0, :, kcols], kv[1, :, kcols]], axis=1)
    vcat = jnp.concatenate([kv[0, :, vcols], kv[1, :, vcols]], axis=1)
    kcat_t = kcat.astype(jnp.float32).T.astype(jnp.bfloat16)
    vcat_t = vcat.astype(jnp.float32).T.astype(jnp.bfloat16)
    zero = jnp.zeros((tokens, hd), jnp.bfloat16)
    for g in range(group):
        feats = slice(g * hd, (g + 1) * hd)
        rows = slice(g * tokens, (g + 1) * tokens)
        q = q_ref[:, feats]
        dy = dy_ref[:, feats].astype(jnp.float32)
        do = (tg * dy).astype(jnp.bfloat16)
        qc[rows, :hd] = jnp.where(rows_a, q, zero)
        qc[rows, hd:] = jnp.where(rows_a, zero, q)
        dc[rows, :hd] = jnp.where(rows_a, do, zero)
        dc[rows, hd:] = jnp.where(rows_a, zero, do)

    pair = 2
    gsum = jnp.zeros((tokens, hd), jnp.float32)
    in_a2 = jnp.concatenate([in_a] * pair, axis=1)
    for h in range(0, group, pair):
        rows = slice(h * tokens, (h + pair) * tokens)
        s = mm(kcat, qc[rows, :], NT)
        s = s + jnp.concatenate([bias[...]] * pair, axis=1)
        top = jnp.max(s, axis=0, keepdims=True)
        e = jnp.exp2((s - top) * (scale * LOG2E))
        p = e * (1.0 / jnp.sum(e, axis=0, keepdims=True))
        ph = p.astype(jnp.bfloat16)
        p16[:, rows] = ph
        dp = mm(vcat, dc[rows, :], NT)
        delta = jnp.sum(ph.astype(jnp.float32) * dp, axis=0, keepdims=True)
        dsh = (scale * p * (dp - delta)).astype(jnp.bfloat16)
        ds16[:, rows] = dsh
        o = mm(vcat_t, ph, NN)
        o = jnp.where(in_a2, o[:hd], o[hd:])
        dq = mm(kcat_t, dsh, NN)
        dq = jnp.where(in_a2, dq[:hd], dq[hd:])
        for j in range(pair):
            feats = slice((h + j) * hd, (h + j + 1) * hd)
            toks = slice(j * tokens, (j + 1) * tokens)
            ot = o[:, toks].T
            y_ref[:, feats] = (tg * ot).astype(jnp.bfloat16)
            gsum = gsum + dy_ref[:, feats].astype(jnp.float32) * ot
            dq_ref[:, feats] = dq[:, toks].T.astype(jnp.bfloat16)
    g_ref[...] += jnp.sum(gsum.reshape(tokens // 8, 8, hd), axis=0)
    dk = mm(ds16[...], qc[...], NN).astype(jnp.bfloat16)
    dv = mm(p16[...], dc[...], NN).astype(jnp.bfloat16)
    par_a, dx_a = place(img_a)
    par_b, dx_b = place(img_b)
    krows = pl.ds(pl.multiple_of(step * half, half), half)
    vrows = pl.ds(pl.multiple_of((heads + step) * half, half), half)
    for at, lanes in ((par_b * 2 + dx_b, slice(hd, 2 * hd)), (par_a * 2 + dx_a, slice(0, hd))):
        for j in range(2):
            part = slice(j * half, (j + 1) * half)
            acc[at, j, krows] = dk[part, lanes]
            acc[at, j, vrows] = dv[part, lanes]

    @pl.when(step == last)
    def _():
        left = jnp.broadcast_to(jnp.sum(g_ref[...], axis=0, keepdims=True), (GROWS, hd))
        line = lax.broadcasted_iota(jnp.int32, (GROWS, hd), 0)
        digits = jnp.zeros((GROWS, hd), jnp.float32)
        for i in range(GROWS):
            unit = 4.0 ** (GTOP - i)
            d = jnp.round(left * (1.0 / unit))
            left = left - d * unit
            digits = jnp.where(line == i, d, digits)
        for i in range(4):
            for j in range(2):
                acc[i, j, 2 * heads * half :] = digits.astype(jnp.bfloat16)
        c1 = pltpu.make_async_copy(acc.at[pl.ds(2, 2)], part_other, sems.at[2])
        c0 = pltpu.make_async_copy(acc.at[pl.ds(0, 2)], part_own, sems.at[3])
        c1.start()
        c0.start()
        c1.wait()
        c0.wait()


def attend(chunk, mine, cols, folded, seg, counts, gate, q, dy, own, other, prev):
    tokens, feats = q.shape
    slots, width2 = own.shape[1], own.shape[2]
    heads = KV_HEADS // CHUNKS
    hd = width2 // 2 // heads
    block = feats // KV_HEADS
    rows = block // hd * tokens
    smem = pl.BlockSpec(memory_space=pltpu.SMEM)
    hbm = pl.BlockSpec(memory_space=pl.ANY)
    cut = pl.BlockSpec((tokens, block), lambda i: (0, i + chunk * heads))
    gspec = pl.BlockSpec((8, hd), lambda i: (0, 0))
    flops = 12 * heads * rows * slots * hd * 2
    first = prev is None
    if first:
        prev = (jnp.zeros((8, hd), jnp.float32), q, q)
    part = (2, 2, heads * slots + GROWS, hd)
    return pl.pallas_call(
        functools.partial(attend_kernel, mine, cols, folded, first),
        grid=(heads,),
        in_specs=[
            smem,
            smem,
            smem,
            pl.BlockSpec((1, tokens), lambda i: (0, 0)),
            cut,
            cut,
            hbm,
            hbm,
            gspec,
            hbm,
            hbm,
        ],
        out_specs=[cut, cut, hbm, hbm, gspec],
        out_shape=[
            jax.ShapeDtypeStruct(q.shape, jnp.bfloat16),
            jax.ShapeDtypeStruct(q.shape, jnp.bfloat16),
            jax.ShapeDtypeStruct(part, jnp.bfloat16),
            jax.ShapeDtypeStruct(part, jnp.bfloat16),
            jax.ShapeDtypeStruct((8, hd), jnp.float32),
        ],
        input_output_aliases={} if first else {9: 0, 10: 1},
        scratch_shapes=[
            pltpu.VMEM((2, slots, width2), jnp.bfloat16),
            pltpu.VMEM((4,) + part[1:], jnp.bfloat16),
            pltpu.VMEM((rows, 2 * hd), jnp.bfloat16),
            pltpu.VMEM((rows, 2 * hd), jnp.bfloat16),
            pltpu.VMEM((slots, rows), jnp.bfloat16),
            pltpu.VMEM((slots, rows), jnp.bfloat16),
            pltpu.VMEM((slots, tokens), jnp.float32),
            pltpu.VMEM((tokens, hd), jnp.float32),
            pltpu.SemaphoreType.DMA((4,)),
        ],
        compiler_params=pltpu.CompilerParams(
            dimension_semantics=("arbitrary",), vmem_limit_bytes=32 * 1024 * 1024
        ),
        cost_estimate=pl.CostEstimate(
            flops=flops,
            bytes_accessed=4 * q.size + 8 * own.size,
            transcendentals=heads * rows * slots,
        ),
    )(seg, counts, gate, seg.reshape(1, tokens), q, dy, own, other, *prev)


def local(queries, keys, values, seg_image, tile_counts, gate, cotangent):
    f32, bf16 = jnp.float32, jnp.bfloat16
    mine, width = keys.shape
    hd = width // KV_HEADS
    heads = KV_HEADS // CHUNKS
    wide = width // CHUNKS
    cols = lax.axis_size("z")
    folded = cols == 4
    half = cols * mine

    def send_z(x, k):
        return lax.ppermute(x, "z", [(i, i ^ k) for i in range(cols)])

    def send_xy(x, dx, dy):
        return lax.ppermute(x, ("x", "y"), [(i, i ^ (2 * dx + dy)) for i in range(4)])

    def send_core(x):
        return lax.ppermute(x, "core", [(0, 1), (1, 0)])

    kv = jnp.stack(
        [
            jnp.concatenate([keys[:, c * wide : (c + 1) * wide], values[:, c * wide : (c + 1) * wide]], axis=1)
            for c in range(CHUNKS)
        ]
    )
    if folded:
        col = [kv] + [send_z(kv, k) for k in (1, 2, 3)]
    else:
        col = [lax.all_gather(kv, "z", axis=1, tiled=True)]

    prev = None
    reduced = []
    for c in range(CHUNKS):
        block = jnp.concatenate([p[c] for p in col], axis=0)
        own = jnp.concatenate([block] + [send_xy(block, *p) for p in PEERS], axis=0)
        own = own.reshape(2, 2 * half, 2 * wide)
        other = send_core(own)
        y, dq, part_own, part_other, g = attend(
            c, mine, cols, folded, seg_image, tile_counts, gate, queries, cotangent, own, other, prev
        )
        prev = (g, y, dq)
        got = send_core(part_other)
        both = (part_own.astype(f32) + got.astype(f32)).astype(bf16)
        total = both[0, 0].astype(f32)
        for dx, dy in PEERS:
            total = total + send_xy(both[dx, dy], dx, dy).astype(f32)
        grads, gates = total[: 2 * heads * half], total[2 * heads * half :]
        grads = grads.reshape(2 * heads, cols, mine, hd)
        if folded:
            grads, gates = grads.astype(bf16), gates.astype(bf16)
            cut = [
                jnp.concatenate([grads[:, k].reshape(2 * heads * mine, hd), gates], axis=0) for k in range(cols)
            ]
            total = cut[0].astype(f32)
            for k in (1, 2, 3):
                total = total + send_z(cut[k], k).astype(f32)
            grads, gates = total[: 2 * heads * mine], total[2 * heads * mine :]
        else:
            grads = lax.psum_scatter(grads, "z", scatter_dimension=1, tiled=True)
            gates = lax.psum(gates, "z")
        reduced.append(grads.reshape(2 * heads, mine, hd))

    def lay(blocks):
        return jnp.concatenate(blocks, axis=1)

    dk = lay([r[i] for r in reduced for i in range(heads)])
    dv = lay([r[heads + i] for r in reduced for i in range(heads)])
    units = 4.0 ** (GTOP - jnp.arange(GROWS, dtype=f32))
    tg = jnp.tanh(gate[0])
    grad_gate = ((1.0 - tg * tg) * jnp.sum(gates * units[:, None])).reshape(1)
    return (y, dq, dk, dv, grad_gate)


def solution(mesh):
    section, mp = mesh.shape["section"], mesh.shape["mp"]
    fine = Mesh(mesh.devices.reshape(section // 2, 2, mp // 2, 2), AXES)
    rows = P(AXES, None)
    return jax.shard_map(
        local,
        mesh=fine,
        in_specs=(rows, rows, rows, P(AXES), P(), P(), rows),
        out_specs=(rows, rows, rows, rows, P()),
        check_vma=False,
    )
```

```python
import functools

import jax
import jax.numpy as jnp
from jax import lax
from jax.experimental import pallas as pl
from jax.experimental.pallas import tpu as pltpu
from jax.sharding import Mesh
from jax.sharding import PartitionSpec as P

KV_HEADS = 4
TILE_TOK = 64
IMG_TOK = 256
AXES = ("x", "core", "z", "y")
NEG = -1e30
LOG2E = 1.4426950408889634
CHUNKS = 2
GROWS = 16
GTOP = 8
PEERS = ((0, 1), (1, 0), (1, 1))

NT = (((1,), (1,)), ((), ()))
NN = (((1,), (0,)), ((), ()))


def mm(a, b, dims):
    return lax.dot_general(a, b, dims, preferred_element_type=jnp.float32)


def attend_kernel(
    mine,
    cols,
    folded,
    first,
    seg_s,
    cnt_s,
    gate_s,
    seg_v,
    q_ref,
    dy_ref,
    own,
    other,
    g_in,
    y_in,
    dq_in,
    y_ref,
    dq_ref,
    part_own,
    part_other,
    g_ref,
    kv,
    acc,
    qc,
    dc,
    p16,
    ds16,
    bias,
    rowsel,
    sems,
):
    step = pl.program_id(0)
    heads = kv.shape[2] // (2 * q_ref.shape[0])
    last = heads - 1
    tokens = q_ref.shape[0]
    slots, width = kv.shape[1], kv.shape[2] // 2
    half = slots // 2
    hd = width // heads
    group = q_ref.shape[1] // hd
    scale = 1.0 / hd**0.5
    core, xpos = lax.axis_index("core"), lax.axis_index("x")
    img_a, img_b = seg_s[0], seg_s[tokens - 1]

    def place(img):
        return (img % 2) ^ core, (img // 2) ^ xpos

    def fetch(i, img, start):
        par, dx = place(img)

        @pl.when(par == 0)
        def _():
            c = pltpu.make_async_copy(own.at[dx], kv.at[i], sems.at[i])
            c.start() if start else c.wait()

        @pl.when(par != 0)
        def _():
            c = pltpu.make_async_copy(other.at[dx], kv.at[i], sems.at[i])
            c.start() if start else c.wait()

    in_a = seg_v[...] == img_a
    tg = jnp.tanh(jnp.full((1, hd), gate_s[0], jnp.float32))

    @pl.when(step == 0)
    def _():
        fetch(0, img_a, True)
        fetch(1, img_b, True)
        acc[...] = jnp.zeros_like(acc)
        g_ref[...] = jnp.zeros_like(g_ref) if first else g_in[...]
        n = lax.broadcasted_iota(jnp.int32, (slots, tokens), 0)
        zi = (n // mine) % cols
        yi = (n // half) ^ lax.axis_index("y")
        if folded:
            zi = zi ^ lax.axis_index("z")
        tile = (zi * (2 * mine) + yi * mine + n % mine) // TILE_TOK
        limit = jnp.where(in_a, cnt_s[img_a], cnt_s[img_b])
        bias[...] = jnp.where(tile < limit, 0.0, NEG)
        side_a = jnp.broadcast_to(in_a.astype(jnp.float32), (hd, tokens)).T
        rowsel[0] = side_a.astype(jnp.bfloat16)
        rowsel[1] = (1.0 - side_a).astype(jnp.bfloat16)
        fetch(0, img_a, False)
        fetch(1, img_b, False)

    kcols = pl.ds(pl.multiple_of(step * hd, hd), hd)
    vcols = pl.ds(pl.multiple_of(width + step * hd, hd), hd)
    kcat = jnp.concatenate([kv[0, :, kcols], kv[1, :, kcols]], axis=1)
    vcat = jnp.concatenate([kv[0, :, vcols], kv[1, :, vcols]], axis=1)
    kcat_t = kcat.T
    vcat_t = vcat.T
    for g in range(group):
        feats = slice(g * hd, (g + 1) * hd)
        rows = slice(g * tokens, (g + 1) * tokens)
        q = q_ref[:, feats]
        dy = dy_ref[:, feats]
        for i in range(2):
            side = slice(i * hd, (i + 1) * hd)
            qc[rows, side] = q * rowsel[i]
            dc[rows, side] = dy * rowsel[i]

    pair = 2
    in_a2 = jnp.concatenate([in_a] * pair, axis=1)
    tg2 = jnp.concatenate([tg] * pair, axis=1)
    for h in range(0, group, pair):
        rows = slice(h * tokens, (h + pair) * tokens)
        s = mm(kcat, qc[rows, :], NT)
        s = s + jnp.concatenate([bias[...]] * pair, axis=1)
        top = jnp.max(s, axis=0, keepdims=True)
        e = jnp.exp2((s - top) * (scale * LOG2E))
        p = e * (1.0 / jnp.sum(e, axis=0, keepdims=True))
        ph = p.astype(jnp.bfloat16)
        p16[:, rows] = ph
        dp = mm(vcat, dc[rows, :], NT)
        delta = jnp.sum(ph.astype(jnp.float32) * dp, axis=0, keepdims=True)
        dsh = ((scale * tg2) * p * (dp - delta)).astype(jnp.bfloat16)
        ds16[:, rows] = dsh
        o = mm(vcat_t, ph, NN)
        o = (tg2 * jnp.where(in_a2, o[:hd], o[hd:])).astype(jnp.bfloat16)
        dq = mm(kcat_t, dsh, NN)
        dq = jnp.where(in_a2, dq[:hd], dq[hd:]).astype(jnp.bfloat16)
        for j in range(pair):
            feats = slice((h + j) * hd, (h + j + 1) * hd)
            toks = slice(j * tokens, (j + 1) * tokens)
            y_ref[:, feats] = o[:, toks].T
            dq_ref[:, feats] = dq[:, toks].T
    dk = mm(ds16[...], qc[...], NN).astype(jnp.bfloat16)
    dv = mm(p16[...], dc[...], NN)
    gsum = dv * vcat.astype(jnp.float32)
    gsum = jnp.sum(gsum.reshape(slots // 8, 8, 2 * hd), axis=0)
    g_ref[...] += gsum[:, :hd] + gsum[:, hd:]
    dv = (jnp.concatenate([tg, tg], axis=1) * dv).astype(jnp.bfloat16)
    par_a, dx_a = place(img_a)
    par_b, dx_b = place(img_b)
    krows = pl.ds(pl.multiple_of(step * half, half), half)
    vrows = pl.ds(pl.multiple_of((heads + step) * half, half), half)
    for at, lanes in ((par_b * 2 + dx_b, slice(hd, 2 * hd)), (par_a * 2 + dx_a, slice(0, hd))):
        for j in range(2):
            part = slice(j * half, (j + 1) * half)
            acc[at, j, krows] = dk[part, lanes]
            acc[at, j, vrows] = dv[part, lanes]

    @pl.when(step == last)
    def _():
        left = jnp.broadcast_to(jnp.sum(g_ref[...], axis=0, keepdims=True), (GROWS, hd))
        line = lax.broadcasted_iota(jnp.int32, (GROWS, hd), 0)
        digits = jnp.zeros((GROWS, hd), jnp.float32)
        for i in range(GROWS):
            unit = 4.0 ** (GTOP - i)
            d = jnp.round(left * (1.0 / unit))
            left = left - d * unit
            digits = jnp.where(line == i, d, digits)
        for i in range(4):
            for j in range(2):
                acc[i, j, 2 * heads * half :] = digits.astype(jnp.bfloat16)
        c1 = pltpu.make_async_copy(acc.at[pl.ds(2, 2)], part_other, sems.at[2])
        c0 = pltpu.make_async_copy(acc.at[pl.ds(0, 2)], part_own, sems.at[3])
        c1.start()
        c0.start()
        c1.wait()
        c0.wait()


def attend(chunk, mine, cols, folded, seg, counts, gate, q, dy, own, other, prev):
    tokens, feats = q.shape
    slots, width2 = own.shape[1], own.shape[2]
    heads = KV_HEADS // CHUNKS
    hd = width2 // 2 // heads
    block = feats // KV_HEADS
    rows = block // hd * tokens
    smem = pl.BlockSpec(memory_space=pltpu.SMEM)
    hbm = pl.BlockSpec(memory_space=pl.ANY)
    cut = pl.BlockSpec((tokens, block), lambda i: (0, i + chunk * heads))
    gspec = pl.BlockSpec((8, hd), lambda i: (0, 0))
    flops = 5 * 12 * heads * rows * slots * hd * 2
    first = prev is None
    if first:
        prev = (jnp.zeros((8, hd), jnp.float32), q, q)
    part = (2, 2, heads * slots + GROWS, hd)
    return pl.pallas_call(
        functools.partial(attend_kernel, mine, cols, folded, first),
        grid=(heads,),
        in_specs=[
            smem,
            smem,
            smem,
            pl.BlockSpec((1, tokens), lambda i: (0, 0)),
            cut,
            cut,
            hbm,
            hbm,
            gspec,
            hbm,
            hbm,
        ],
        out_specs=[cut, cut, hbm, hbm, gspec],
        out_shape=[
            jax.ShapeDtypeStruct(q.shape, jnp.bfloat16),
            jax.ShapeDtypeStruct(q.shape, jnp.bfloat16),
            jax.ShapeDtypeStruct(part, jnp.bfloat16),
            jax.ShapeDtypeStruct(part, jnp.bfloat16),
            jax.ShapeDtypeStruct((8, hd), jnp.float32),
        ],
        input_output_aliases={} if first else {9: 0, 10: 1},
        scratch_shapes=[
            pltpu.VMEM((2, slots, width2), jnp.bfloat16),
            pltpu.VMEM((4,) + part[1:], jnp.bfloat16),
            pltpu.VMEM((rows, 2 * hd), jnp.bfloat16),
            pltpu.VMEM((rows, 2 * hd), jnp.bfloat16),
            pltpu.VMEM((slots, rows), jnp.bfloat16),
            pltpu.VMEM((slots, rows), jnp.bfloat16),
            pltpu.VMEM((slots, tokens), jnp.float32),
            pltpu.VMEM((2, tokens, hd), jnp.bfloat16),
            pltpu.SemaphoreType.DMA((4,)),
        ],
        compiler_params=pltpu.CompilerParams(
            dimension_semantics=("arbitrary",), vmem_limit_bytes=32 * 1024 * 1024
        ),
        cost_estimate=pl.CostEstimate(
            flops=flops,
            bytes_accessed=4 * q.size + 8 * own.size,
            transcendentals=heads * rows * slots,
        ),
    )(seg, counts, gate, seg.reshape(1, tokens), q, dy, own, other, *prev)


def finish_kernel(heads, mine, gate_s, *refs):
    ins, (dk_ref, dv_ref, g_ref) = refs[:-3], refs[-3:]
    hd = ins[0].shape[1]
    each = len(ins) // CHUNKS
    for c in range(CHUNKS):
        total = ins[c * each][...].astype(jnp.float32)
        for r in ins[c * each + 1 : (c + 1) * each]:
            total = total + r[...].astype(jnp.float32)
        for h in range(heads):
            lanes = slice((c * heads + h) * hd, (c * heads + h + 1) * hd)
            dk_ref[:, lanes] = total[h * mine : (h + 1) * mine]
            dv_ref[:, lanes] = total[(heads + h) * mine : (heads + h + 1) * mine]
    digits = total[2 * heads * mine :]
    line = lax.broadcasted_iota(jnp.int32, digits.shape, 0)
    units = jnp.zeros(digits.shape, jnp.float32)
    for i in range(GROWS):
        units = jnp.where(line == i, 4.0 ** (GTOP - i), units)
    tg = jnp.tanh(jnp.full((1, hd), gate_s[0], jnp.float32))
    terms = jnp.sum(digits * units, axis=0, keepdims=True) * (1.0 - tg * tg)
    g_ref[0] = jnp.sum(terms)


def finish(mine, gate, cuts):
    heads = KV_HEADS // CHUNKS
    hd = cuts[0].shape[1]
    smem = pl.BlockSpec(memory_space=pltpu.SMEM)
    vmem = pl.BlockSpec(memory_space=pltpu.VMEM)
    full = jax.ShapeDtypeStruct((mine, KV_HEADS * hd), jnp.float32)
    return pl.pallas_call(
        functools.partial(finish_kernel, heads, mine),
        in_specs=[smem] + [vmem] * len(cuts),
        out_specs=[vmem, vmem, smem],
        out_shape=[full, full, jax.ShapeDtypeStruct((1,), jnp.float32)],
    )(gate, *cuts)


def local(queries, keys, values, seg_image, tile_counts, gate, cotangent):
    f32, bf16 = jnp.float32, jnp.bfloat16
    mine, width = keys.shape
    hd = width // KV_HEADS
    heads = KV_HEADS // CHUNKS
    wide = width // CHUNKS
    cols = lax.axis_size("z")
    folded = cols == 4
    half = cols * mine

    def send_z(x, k):
        return lax.ppermute(x, "z", [(i, i ^ k) for i in range(cols)])

    def send_xy(x, dx, dy):
        return lax.ppermute(x, ("x", "y"), [(i, i ^ (2 * dx + dy)) for i in range(4)])

    def send_core(x):
        return lax.ppermute(x, "core", [(0, 1), (1, 0)])

    kv = jnp.stack([keys, values])
    if folded:
        col = [kv] + [send_z(kv, k) for k in (1, 2, 3)]
    else:
        col = [lax.all_gather(kv, "z", axis=1, tiled=True)]

    def gather(c):
        lanes = slice(c * wide, (c + 1) * wide)
        block = jnp.concatenate([jnp.concatenate([p[0, :, lanes], p[1, :, lanes]], axis=1) for p in col], axis=0)
        own = jnp.concatenate([block] + [send_xy(block, *p) for p in PEERS], axis=0)
        own = own.reshape(2, 2 * half, 2 * wide)
        return own, send_core(own)

    def reduce_core(part_own, part_other):
        got = send_core(part_other)
        return (part_own.astype(f32) + got.astype(f32)).astype(bf16)

    def reduce_xy(both):
        total = both[0, 0].astype(f32)
        for dx, dy in PEERS:
            total = total + send_xy(both[dx, dy], dx, dy).astype(f32)
        return total

    pieces = [gather(c) for c in range(CHUNKS)]
    prev = None
    both = None
    totals = []
    for c in range(CHUNKS):
        own, other = pieces[c]
        if c:
            own, other, both = lax.optimization_barrier((own, other, both))
        y, dq, part_own, part_other, g = attend(
            c, mine, cols, folded, seg_image, tile_counts, gate, queries, cotangent, own, other, prev
        )
        prev = (g, y, dq)
        if c:
            totals.append(reduce_xy(both))
            part_other, totals[-1] = lax.optimization_barrier((part_other, totals[-1]))
        both = reduce_core(part_own, part_other)
    totals.append(reduce_xy(both))

    cuts = []
    for total in totals:
        grads, gates = total[: 2 * heads * half], total[2 * heads * half :]
        grads = grads.reshape(2 * heads, cols, mine, hd)
        if folded:
            grads, gates = grads.astype(bf16), gates.astype(bf16)
            cut = [jnp.concatenate([grads[:, k].reshape(-1, hd), gates], axis=0) for k in range(cols)]
            cuts += [cut[0]] + [send_z(cut[k], k) for k in (1, 2, 3)]
        else:
            grads = lax.psum_scatter(grads, "z", scatter_dimension=1, tiled=True)
            cuts.append(jnp.concatenate([grads.reshape(-1, hd), lax.psum(gates, "z")], axis=0))
    return (y, dq, *finish(mine, gate, cuts))


def solution(mesh):
    section, mp = mesh.shape["section"], mesh.shape["mp"]
    fine = Mesh(mesh.devices.reshape(section // 2, 2, mp // 2, 2), AXES)
    rows = P(AXES, None)
    return jax.shard_map(
        local,
        mesh=fine,
        in_specs=(rows, rows, rows, P(AXES), P(), P(), rows),
        out_specs=(rows, rows, rows, rows, P()),
        check_vma=False,
    )
```

```python
import functools

import jax
import jax.numpy as jnp
from jax import lax
from jax.experimental import pallas as pl
from jax.experimental.pallas import tpu as pltpu
from jax.sharding import Mesh
from jax.sharding import PartitionSpec as P

KV_HEADS = 4
TILE_TOK = 64
IMG_TOK = 256
AXES = ("x", "core", "z", "y")
NEG = -1e30
LOG2E = 1.4426950408889634
CHUNKS = 2
GROWS = 16
GTOP = 8
STRIP = 32
PEERS = ((1, 1), (1, 0), (0, 1))
LINE = (3, 2, 1)

NT = (((1,), (1,)), ((), ()))
NN = (((1,), (0,)), ((), ()))


def mm(a, b, dims):
    return lax.dot_general(a, b, dims, preferred_element_type=jnp.float32)


def attend_kernel(
    mine,
    cols,
    folded,
    first,
    seg_s,
    cnt_s,
    gate_s,
    seg_v,
    q_ref,
    dy_ref,
    own,
    other,
    g_in,
    y_in,
    dq_in,
    y_ref,
    dq_ref,
    part_own,
    part_other,
    g_ref,
    kv,
    acc,
    qc,
    dc,
    p16,
    ds16,
    sbuf,
    dbuf,
    bias,
    rowsel,
    sems,
):
    step = pl.program_id(0)
    heads = kv.shape[2] // (2 * q_ref.shape[0])
    last = heads - 1
    tokens = q_ref.shape[0]
    slots, width = kv.shape[1], kv.shape[2] // 2
    half = slots // 2
    hd = width // heads
    group = q_ref.shape[1] // hd
    scale = 1.0 / hd**0.5
    core, xpos = lax.axis_index("core"), lax.axis_index("x")
    img_a, img_b = seg_s[0], seg_s[tokens - 1]

    def place(img):
        return (img % 2) ^ core, (img // 2) ^ xpos

    def fetch(i, img, start):
        par, dx = place(img)

        @pl.when(par == 0)
        def _():
            c = pltpu.make_async_copy(own.at[dx], kv.at[i], sems.at[i])
            c.start() if start else c.wait()

        @pl.when(par != 0)
        def _():
            c = pltpu.make_async_copy(other.at[dx], kv.at[i], sems.at[i])
            c.start() if start else c.wait()

    in_a = seg_v[...] == img_a
    tg = jnp.tanh(jnp.full((1, hd), gate_s[0], jnp.float32))

    @pl.when(step == 0)
    def _():
        fetch(0, img_a, True)
        fetch(1, img_b, True)
        acc[...] = jnp.zeros_like(acc)
        g_ref[...] = jnp.zeros_like(g_ref) if first else g_in[...]
        n = lax.broadcasted_iota(jnp.int32, (slots, tokens), 0)
        zi = (n // mine) % cols
        yi = (n // half) ^ lax.axis_index("y")
        if folded:
            zi = zi ^ lax.axis_index("z")
        tile = (zi * (2 * mine) + yi * mine + n % mine) // TILE_TOK
        limit = jnp.where(in_a, cnt_s[img_a], cnt_s[img_b])
        bias[...] = jnp.where(tile < limit, 0.0, NEG)
        side_a = jnp.broadcast_to(in_a.astype(jnp.float32), (hd, tokens)).T
        rowsel[0] = side_a.astype(jnp.bfloat16)
        rowsel[1] = (1.0 - side_a).astype(jnp.bfloat16)
        fetch(0, img_a, False)
        fetch(1, img_b, False)

    kcols = pl.ds(pl.multiple_of(step * hd, hd), hd)
    vcols = pl.ds(pl.multiple_of(width + step * hd, hd), hd)
    kcat = jnp.concatenate([kv[0, :, kcols], kv[1, :, kcols]], axis=1)
    vcat = jnp.concatenate([kv[0, :, vcols], kv[1, :, vcols]], axis=1)
    kcat_t = kcat.T
    vcat_t = vcat.T
    for g in range(group):
        feats = slice(g * hd, (g + 1) * hd)
        rows = slice(g * tokens, (g + 1) * tokens)
        q = q_ref[:, feats]
        dy = dy_ref[:, feats]
        for i in range(2):
            side = slice(i * hd, (i + 1) * hd)
            qc[rows, side] = q * rowsel[i]
            dc[rows, side] = dy * rowsel[i]

    span = 2 * tokens
    blocks = group // 2
    strips = [slice(i, i + STRIP) for i in range(0, slots, STRIP)]
    in_a2 = jnp.concatenate([in_a, in_a], axis=1)
    tg2 = jnp.concatenate([tg, tg], axis=1)
    slope = scale * tg2

    def fold8(x):
        return jnp.sum(x.reshape(x.shape[0] // 8, 8, x.shape[1]), axis=0)

    def products(h):
        rows = slice(h * span, (h + 1) * span)
        sbuf[h % 2] = mm(kcat, qc[rows, :], NT)
        dbuf[h % 2] = mm(vcat, dc[rows, :], NT)

    def softmax(h):
        i = h % 2
        rows = slice(h * span, (h + 1) * span)
        top = jnp.full((8, span), NEG, jnp.float32)
        for strip in strips:
            x = sbuf[i, strip] + jnp.concatenate([bias[strip], bias[strip]], axis=1)
            sbuf[i, strip] = x
            top = jnp.maximum(top, jnp.max(x.reshape(STRIP // 8, 8, span), axis=0))
        top = jnp.max(top, axis=0, keepdims=True) * (scale * LOG2E)
        norm = jnp.zeros((8, span), jnp.float32)
        dots = jnp.zeros((8, span), jnp.float32)
        for strip in strips:
            e = jnp.exp2(sbuf[i, strip] * (scale * LOG2E) - top)
            sbuf[i, strip] = e
            norm = norm + fold8(e)
            dots = dots + fold8(e * dbuf[i, strip])
        inv = 1.0 / jnp.sum(norm, axis=0, keepdims=True)
        delta = slope * (inv * jnp.sum(dots, axis=0, keepdims=True))
        for strip in strips:
            p = sbuf[i, strip] * inv
            p16[strip, rows] = p.astype(jnp.bfloat16)
            ds16[strip, rows] = (p * (slope * dbuf[i, strip] - delta)).astype(jnp.bfloat16)

    def outputs(h):
        rows = slice(h * span, (h + 1) * span)
        o = mm(vcat_t, p16[:, rows], NN)
        o = (tg2 * jnp.where(in_a2, o[:hd], o[hd:])).astype(jnp.bfloat16)
        dq = mm(kcat_t, ds16[:, rows], NN)
        dq = jnp.where(in_a2, dq[:hd], dq[hd:]).astype(jnp.bfloat16)
        for j in range(2):
            feats = slice((2 * h + j) * hd, (2 * h + j + 1) * hd)
            toks = slice(j * tokens, (j + 1) * tokens)
            y_ref[:, feats] = o[:, toks].T
            dq_ref[:, feats] = dq[:, toks].T

    def slot_grads(lo, hi):
        rows = slice(lo * span, hi * span)
        return mm(ds16[:, rows], qc[rows, :], NN), mm(p16[:, rows], dc[rows, :], NN)

    products(0)
    dk = dv = 0.0
    for h in range(blocks):
        if h + 1 < blocks:
            products(h + 1)
        softmax(h)
        outputs(h)
        if h % 2:
            more = slot_grads(h - 1, h + 1)
            dk, dv = dk + more[0], dv + more[1]
    dk = dk.astype(jnp.bfloat16)
    g_ref[...] += fold8((dv * vcat.astype(jnp.float32))[:, :hd] + (dv * vcat.astype(jnp.float32))[:, hd:])
    dv = (jnp.concatenate([tg, tg], axis=1) * dv).astype(jnp.bfloat16)
    par_a, dx_a = place(img_a)
    par_b, dx_b = place(img_b)
    krows = pl.ds(pl.multiple_of(step * half, half), half)
    vrows = pl.ds(pl.multiple_of((heads + step) * half, half), half)
    for at, lanes in ((par_b * 2 + dx_b, slice(hd, 2 * hd)), (par_a * 2 + dx_a, slice(0, hd))):
        for j in range(2):
            part = slice(j * half, (j + 1) * half)
            acc[at, j, krows] = dk[part, lanes]
            acc[at, j, vrows] = dv[part, lanes]

    @pl.when(step == last)
    def _():
        left = jnp.broadcast_to(jnp.sum(g_ref[...], axis=0, keepdims=True), (GROWS, hd))
        line = lax.broadcasted_iota(jnp.int32, (GROWS, hd), 0)
        digits = jnp.zeros((GROWS, hd), jnp.float32)
        for i in range(GROWS):
            unit = 4.0 ** (GTOP - i)
            d = jnp.round(left * (1.0 / unit))
            left = left - d * unit
            digits = jnp.where(line == i, d, digits)
        if not first:
            g_ref[...] = jnp.broadcast_to(1.0 - tg * tg, g_ref.shape)
        for i in range(4):
            for j in range(2):
                acc[i, j, 2 * heads * half :] = digits.astype(jnp.bfloat16)
        c1 = pltpu.make_async_copy(acc.at[pl.ds(2, 2)], part_other, sems.at[2])
        c0 = pltpu.make_async_copy(acc.at[pl.ds(0, 2)], part_own, sems.at[3])
        c1.start()
        c0.start()
        c1.wait()
        c0.wait()


def attend(chunk, mine, cols, folded, seg, counts, gate, q, dy, own, other, prev):
    tokens, feats = q.shape
    slots, width2 = own.shape[1], own.shape[2]
    heads = KV_HEADS // CHUNKS
    hd = width2 // 2 // heads
    block = feats // KV_HEADS
    rows = block // hd * tokens
    smem = pl.BlockSpec(memory_space=pltpu.SMEM)
    hbm = pl.BlockSpec(memory_space=pl.ANY)
    cut = pl.BlockSpec((tokens, block), lambda i: (0, i + chunk * heads))
    gspec = pl.BlockSpec((8, hd), lambda i: (0, 0))
    flops = 5 * 12 * heads * rows * slots * hd * 2
    first = prev is None
    if first:
        prev = (jnp.zeros((8, hd), jnp.float32), q, q)
    part = (2, 2, heads * slots + GROWS, hd)
    return pl.pallas_call(
        functools.partial(attend_kernel, mine, cols, folded, first),
        grid=(heads,),
        in_specs=[
            smem,
            smem,
            smem,
            pl.BlockSpec((1, tokens), lambda i: (0, 0)),
            cut,
            cut,
            hbm,
            hbm,
            gspec,
            hbm,
            hbm,
        ],
        out_specs=[cut, cut, hbm, hbm, gspec],
        out_shape=[
            jax.ShapeDtypeStruct(q.shape, jnp.bfloat16),
            jax.ShapeDtypeStruct(q.shape, jnp.bfloat16),
            jax.ShapeDtypeStruct(part, jnp.bfloat16),
            jax.ShapeDtypeStruct(part, jnp.bfloat16),
            jax.ShapeDtypeStruct((8, hd), jnp.float32),
        ],
        input_output_aliases={} if first else {9: 0, 10: 1},
        scratch_shapes=[
            pltpu.VMEM((2, slots, width2), jnp.bfloat16),
            pltpu.VMEM((4,) + part[1:], jnp.bfloat16),
            pltpu.VMEM((rows, 2 * hd), jnp.bfloat16),
            pltpu.VMEM((rows, 2 * hd), jnp.bfloat16),
            pltpu.VMEM((slots, rows), jnp.bfloat16),
            pltpu.VMEM((slots, rows), jnp.bfloat16),
            pltpu.VMEM((2, slots, 2 * tokens), jnp.float32),
            pltpu.VMEM((2, slots, 2 * tokens), jnp.float32),
            pltpu.VMEM((slots, tokens), jnp.float32),
            pltpu.VMEM((2, tokens, hd), jnp.bfloat16),
            pltpu.SemaphoreType.DMA((4,)),
        ],
        compiler_params=pltpu.CompilerParams(
            dimension_semantics=("arbitrary",), vmem_limit_bytes=32 * 1024 * 1024
        ),
        cost_estimate=pl.CostEstimate(
            flops=flops,
            bytes_accessed=4 * q.size + 8 * own.size,
            transcendentals=heads * rows * slots,
        ),
    )(seg, counts, gate, seg.reshape(1, tokens), q, dy, own, other, *prev)


def add_up(refs, at):
    total = refs[0][at].astype(jnp.float32)
    for r in refs[1:]:
        total = total + r[at].astype(jnp.float32)
    return total


def fold_kernel(cols, mine, both, *refs):
    outs = refs[len(PEERS) :]
    parts = (both.at[0, 0],) + refs[: len(PEERS)]
    groups = (outs[0].shape[0] - GROWS) // mine
    gates = add_up(parts, slice(groups * cols * mine, None)).astype(jnp.bfloat16)
    for k in range(cols):
        for b in range(groups):
            at = (b * cols + k) * mine
            outs[k][b * mine : (b + 1) * mine] = add_up(parts, slice(at, at + mine)).astype(jnp.bfloat16)
        outs[k][groups * mine :] = gates


def fold(cols, mine, both, recv):
    rows = (both.shape[2] - GROWS) // cols + GROWS
    vmem = pl.BlockSpec(memory_space=pltpu.VMEM)
    return pl.pallas_call(
        functools.partial(fold_kernel, cols, mine),
        in_specs=[vmem] * (1 + len(recv)),
        out_specs=[vmem] * cols,
        out_shape=[jax.ShapeDtypeStruct((rows, both.shape[3]), jnp.bfloat16)] * cols,
    )(both, *recv)


def finish_kernel(heads, mine, gate, *refs):
    ins, (dk_ref, dv_ref, g_ref) = refs[:-3], refs[-3:]
    hd = ins[0].shape[1]
    each = len(ins) // CHUNKS
    for c in range(CHUNKS):
        parts = ins[c * each : (c + 1) * each]
        for h in range(2 * heads):
            out = (dk_ref, dv_ref)[h // heads]
            lanes = slice((c * heads + h % heads) * hd, (c * heads + h % heads + 1) * hd)
            out[:, lanes] = add_up(parts, slice(h * mine, (h + 1) * mine))
    digits = add_up(parts, slice(2 * heads * mine, None))
    line = lax.broadcasted_iota(jnp.int32, digits.shape, 0)
    units = jnp.zeros(digits.shape, jnp.float32)
    for i in range(GROWS):
        units = jnp.where(line == i, 4.0 ** (GTOP - i), units)
    g_ref[0] = jnp.sum(jnp.sum(digits * units, axis=0, keepdims=True) * gate[0:1, :])


def finish(mine, gate, cuts):
    heads = KV_HEADS // CHUNKS
    hd = cuts[0].shape[1]
    smem = pl.BlockSpec(memory_space=pltpu.SMEM)
    vmem = pl.BlockSpec(memory_space=pltpu.VMEM)
    full = jax.ShapeDtypeStruct((mine, KV_HEADS * hd), jnp.float32)
    return pl.pallas_call(
        functools.partial(finish_kernel, heads, mine),
        in_specs=[vmem] + [vmem] * len(cuts),
        out_specs=[vmem, vmem, smem],
        out_shape=[full, full, jax.ShapeDtypeStruct((1,), jnp.float32)],
    )(gate, *cuts)


def local(queries, keys, values, seg_image, tile_counts, gate, cotangent):
    f32, bf16 = jnp.float32, jnp.bfloat16
    mine, width = keys.shape
    hd = width // KV_HEADS
    heads = KV_HEADS // CHUNKS
    wide = width // CHUNKS
    cols = lax.axis_size("z")
    folded = cols == 4
    half = cols * mine

    def send_z(x, k):
        return lax.ppermute(x, "z", [(i, i ^ k) for i in range(cols)])

    def send_xy(x, dx, dy):
        return lax.ppermute(x, ("x", "y"), [(i, i ^ (2 * dx + dy)) for i in range(4)])

    def send_core(x):
        return lax.ppermute(x, "core", [(0, 1), (1, 0)])

    kv = lax.optimization_barrier(jnp.stack([keys, values]))
    if folded:
        col = {k: send_z(kv, k) for k in LINE}
        col = [kv] + [col[k] for k in sorted(col)]
    else:
        col = [lax.all_gather(kv, "z", axis=1, tiled=True)]

    def gather(c):
        lanes = slice(c * wide, (c + 1) * wide)
        block = jnp.concatenate([jnp.concatenate([p[0, :, lanes], p[1, :, lanes]], axis=1) for p in col], axis=0)
        recv = {p: send_xy(block, *p) for p in PEERS}
        own = jnp.concatenate([block] + [recv[p] for p in sorted(recv)], axis=0)
        own = own.reshape(2, 2 * half, 2 * wide)
        return own, send_core(own)

    def reduce_core(part_own, part_other):
        got = send_core(part_other)
        return (part_own.astype(f32) + got.astype(f32)).astype(bf16)

    def reduce_xy(both):
        recv = [send_xy(both[p], *p) for p in PEERS]
        if folded:
            return fold(cols, mine, both, recv)
        return [sum(r.astype(f32) for r in [both[0, 0]] + recv)]

    pieces = [gather(c) for c in range(CHUNKS)]
    prev = None
    both = None
    sums = []
    for c in range(CHUNKS):
        own, other = pieces[c]
        if c:
            own, other, both = lax.optimization_barrier((own, other, both))
        y, dq, part_own, part_other, g = attend(
            c, mine, cols, folded, seg_image, tile_counts, gate, queries, cotangent, own, other, prev
        )
        prev = (g, y, dq)
        if c:
            sums.append(reduce_xy(both))
            part_other, sums[-1] = lax.optimization_barrier((part_other, sums[-1]))
        both = reduce_core(part_own, part_other)
    sums.append(reduce_xy(both))

    cuts = []
    for cut in sums:
        if folded:
            cuts += [cut[0]] + [send_z(cut[k], k) for k in LINE]
        else:
            grads, gates = cut[0][: 2 * heads * half], cut[0][2 * heads * half :]
            grads = grads.reshape(2 * heads, cols, mine, hd)
            grads = lax.psum_scatter(grads, "z", scatter_dimension=1, tiled=True)
            cuts.append(jnp.concatenate([grads.reshape(-1, hd), lax.psum(gates, "z")], axis=0))
    return (y, dq, *finish(mine, g, cuts))


def solution(mesh):
    section, mp = mesh.shape["section"], mesh.shape["mp"]
    fine = Mesh(mesh.devices.reshape(section // 2, 2, mp // 2, 2), AXES)
    rows = P(AXES, None)
    return jax.shard_map(
        local,
        mesh=fine,
        in_specs=(rows, rows, rows, P(AXES), P(), P(), rows),
        out_specs=(rows, rows, rows, rows, P()),
        check_vma=False,
    )
```

```python
import functools

import jax
import jax.numpy as jnp
from jax import lax
from jax.experimental import pallas as pl
from jax.experimental.pallas import tpu as pltpu
from jax.sharding import Mesh
from jax.sharding import PartitionSpec as P

KV_HEADS = 4
TILE_TOK = 64
IMG_TOK = 256
AXES = ("x", "core", "z", "y")
NEG = -1e30
LOG2E = 1.4426950408889634
GROWS = 16
GTOP = 8
STRIP = 32

NT = (((1,), (1,)), ((), ()))
NN = (((1,), (0,)), ((), ()))


def mm(a, b, dims):
    return lax.dot_general(a, b, dims, preferred_element_type=jnp.float32)


def attend_kernel(
    mine,
    cols,
    folded,
    seg_s,
    cnt_s,
    gate_s,
    seg_v,
    q_ref,
    dy_ref,
    own,
    other,
    y_ref,
    dq_ref,
    part_own,
    part_other,
    g_ref,
    kv,
    acc,
    qc,
    dc,
    p16,
    ds16,
    sbuf,
    dbuf,
    bias,
    rowsel,
    sems,
):
    step = pl.program_id(0)
    heads = pl.num_programs(0)
    tokens = q_ref.shape[0]
    slots, width = kv.shape[1], kv.shape[2] // 2
    half = slots // 2
    hd = width // heads
    group = q_ref.shape[1] // hd
    scale = 1.0 / hd**0.5
    core, xpos = lax.axis_index("core"), lax.axis_index("x")
    ypos, zpos = lax.axis_index("y"), lax.axis_index("z")
    img_a, img_b = seg_s[0], seg_s[tokens - 1]

    def place(img, h):
        par, dx = img % 2, (img // 2) ^ xpos
        return par, jnp.where(par == 0, h, dx), jnp.where(par == 0, dx, h)

    def fetch(i, img, start):
        for h in range(2):
            par, j0, j1 = place(img, h)
            for src, mask in ((own, par == core), (other, par != core)):

                @pl.when(mask)
                def _():
                    c = pltpu.make_async_copy(src.at[j0, j1], kv.at[i, pl.ds(h * half, half)], sems.at[i])
                    c.start() if start else c.wait()

    def tile_of(n, img):
        side, rest = n // half, n % half
        outer, inner = rest // mine, rest % mine
        if folded:
            z0 = (2 * (outer % 2) + outer // 2) ^ zpos
            y0 = side ^ ypos
            z1 = ((outer // 2) * 2 + side) ^ zpos
            y1 = (outer % 2) ^ ypos
        else:
            z0 = z1 = outer
            y0 = y1 = side ^ ypos
        even = img % 2 == 0
        z, y = jnp.where(even, z0, z1), jnp.where(even, y0, y1)
        return (z * (2 * mine) + y * mine + inner) // TILE_TOK

    in_a = seg_v[...] == img_a
    tg = jnp.tanh(jnp.full((1, hd), gate_s[0], jnp.float32))

    @pl.when(step == 0)
    def _():
        fetch(0, img_a, True)
        fetch(1, img_b, True)
        acc[...] = jnp.zeros_like(acc)
        g_ref[...] = jnp.zeros_like(g_ref)
        n = lax.broadcasted_iota(jnp.int32, (slots, tokens), 0)
        seen_a = tile_of(n, img_a) < cnt_s[img_a]
        seen_b = tile_of(n, img_b) < cnt_s[img_b]
        seen = jnp.where(in_a, seen_a.astype(jnp.float32), seen_b.astype(jnp.float32))
        bias[...] = jnp.where(seen > 0.5, 0.0, NEG)
        side_a = jnp.broadcast_to(in_a.astype(jnp.float32), (hd, tokens)).T
        rowsel[0] = side_a.astype(jnp.bfloat16)
        rowsel[1] = (1.0 - side_a).astype(jnp.bfloat16)
        fetch(0, img_a, False)
        fetch(1, img_b, False)

    kcols = pl.ds(pl.multiple_of(step * hd, hd), hd)
    vcols = pl.ds(pl.multiple_of(width + step * hd, hd), hd)
    kcat = jnp.concatenate([kv[0, :, kcols], kv[1, :, kcols]], axis=1)
    vcat = jnp.concatenate([kv[0, :, vcols], kv[1, :, vcols]], axis=1)
    kcat_t = kcat.T
    vcat_t = vcat.T
    for g in range(group):
        feats = slice(g * hd, (g + 1) * hd)
        rows = slice(g * tokens, (g + 1) * tokens)
        q = q_ref[:, feats]
        dy = dy_ref[:, feats]
        for i in range(2):
            side = slice(i * hd, (i + 1) * hd)
            qc[rows, side] = q * rowsel[i]
            dc[rows, side] = dy * rowsel[i]

    span = 2 * tokens
    blocks = group // 2
    strips = [slice(i, i + STRIP) for i in range(0, slots, STRIP)]
    in_a2 = jnp.concatenate([in_a, in_a], axis=1)
    tg2 = jnp.concatenate([tg, tg], axis=1)
    slope = scale * tg2

    def fold8(x):
        return jnp.sum(x.reshape(x.shape[0] // 8, 8, x.shape[1]), axis=0)

    def products(h):
        rows = slice(h * span, (h + 1) * span)
        sbuf[h % 2] = mm(kcat, qc[rows, :], NT)
        dbuf[h % 2] = mm(vcat, dc[rows, :], NT)

    def softmax(h):
        i = h % 2
        rows = slice(h * span, (h + 1) * span)
        top = jnp.full((8, span), NEG, jnp.float32)
        for strip in strips:
            x = sbuf[i, strip] + jnp.concatenate([bias[strip], bias[strip]], axis=1)
            sbuf[i, strip] = x
            top = jnp.maximum(top, jnp.max(x.reshape(STRIP // 8, 8, span), axis=0))
        top = jnp.max(top, axis=0, keepdims=True) * (scale * LOG2E)
        norm = jnp.zeros((8, span), jnp.float32)
        dots = jnp.zeros((8, span), jnp.float32)
        for strip in strips:
            e = jnp.exp2(sbuf[i, strip] * (scale * LOG2E) - top)
            sbuf[i, strip] = e
            norm = norm + fold8(e)
            dots = dots + fold8(e * dbuf[i, strip])
        inv = 1.0 / jnp.sum(norm, axis=0, keepdims=True)
        delta = slope * (inv * jnp.sum(dots, axis=0, keepdims=True))
        for strip in strips:
            p = sbuf[i, strip] * inv
            p16[strip, rows] = p.astype(jnp.bfloat16)
            ds16[strip, rows] = (p * (slope * dbuf[i, strip] - delta)).astype(jnp.bfloat16)

    def outputs(h):
        rows = slice(h * span, (h + 1) * span)
        o = mm(vcat_t, p16[:, rows], NN)
        o = (tg2 * jnp.where(in_a2, o[:hd], o[hd:])).astype(jnp.bfloat16)
        dq = mm(kcat_t, ds16[:, rows], NN)
        dq = jnp.where(in_a2, dq[:hd], dq[hd:]).astype(jnp.bfloat16)
        for j in range(2):
            feats = slice((2 * h + j) * hd, (2 * h + j + 1) * hd)
            toks = slice(j * tokens, (j + 1) * tokens)
            y_ref[:, feats] = o[:, toks].T
            dq_ref[:, feats] = dq[:, toks].T

    def slot_grads(lo, hi):
        rows = slice(lo * span, hi * span)
        return mm(ds16[:, rows], qc[rows, :], NN), mm(p16[:, rows], dc[rows, :], NN)

    products(0)
    dk = dv = 0.0
    for h in range(blocks):
        if h + 1 < blocks:
            products(h + 1)
        softmax(h)
        outputs(h)
        if h % 2:
            more = slot_grads(h - 1, h + 1)
            dk, dv = dk + more[0], dv + more[1]
    dk = dk.astype(jnp.bfloat16)
    g_ref[...] += fold8((dv * vcat.astype(jnp.float32))[:, :hd] + (dv * vcat.astype(jnp.float32))[:, hd:])
    dv = (jnp.concatenate([tg, tg], axis=1) * dv).astype(jnp.bfloat16)
    pieces = 2 * acc.shape[3]
    per = slots // pieces
    krows = pl.ds(pl.multiple_of(step * per, per), per)
    vrows = pl.ds(pl.multiple_of((heads + step) * per, per), per)
    for img, lanes in ((img_b, slice(hd, 2 * hd)), (img_a, slice(0, hd))):
        for h in range(2):
            par, j0, j1 = place(img, h)
            for j in range(pieces // 2):
                at = slice(h * half + j * per, h * half + (j + 1) * per)
                acc[par, j0, j1, j, krows] = dk[at, lanes]
                acc[par, j0, j1, j, vrows] = dv[at, lanes]

    @pl.when(step == heads - 1)
    def _():
        left = jnp.broadcast_to(jnp.sum(g_ref[...], axis=0, keepdims=True), (GROWS, hd))
        line = lax.broadcasted_iota(jnp.int32, (GROWS, hd), 0)
        digits = jnp.zeros((GROWS, hd), jnp.float32)
        for i in range(GROWS):
            unit = 4.0 ** (GTOP - i)
            d = jnp.round(left * (1.0 / unit))
            left = left - d * unit
            digits = jnp.where(line == i, d, digits)
        digits = digits.astype(jnp.bfloat16)
        g_ref[...] = jnp.broadcast_to(1.0 - tg * tg, g_ref.shape)
        for i in range(8):
            for j in range(pieces // 2):
                acc[i // 4, i // 2 % 2, i % 2, j, 2 * heads * per :] = digits
        c1 = pltpu.make_async_copy(acc.at[1 - core], part_other, sems.at[2])
        c0 = pltpu.make_async_copy(acc.at[core], part_own, sems.at[3])
        c1.start()
        c0.start()
        c1.wait()
        c0.wait()


def attend(mine, cols, folded, seg, counts, gate, q, dy, own, other):
    tokens, feats = q.shape
    slots, width2 = 2 * own.shape[2], own.shape[3]
    hd = width2 // 2 // KV_HEADS
    block = feats // KV_HEADS
    rows = block // hd * tokens
    smem = pl.BlockSpec(memory_space=pltpu.SMEM)
    hbm = pl.BlockSpec(memory_space=pl.ANY)
    cut = pl.BlockSpec((tokens, block), lambda i: (0, i))
    gspec = pl.BlockSpec((8, hd), lambda i: (0, 0))
    flops = 12 * KV_HEADS * rows * slots * hd * 2
    pieces = 8 if folded else 2
    part = (2, 2, pieces // 2, 2 * KV_HEADS * (slots // pieces) + GROWS, hd)
    return pl.pallas_call(
        functools.partial(attend_kernel, mine, cols, folded),
        grid=(KV_HEADS,),
        in_specs=[
            smem,
            smem,
            smem,
            pl.BlockSpec((1, tokens), lambda i: (0, 0)),
            cut,
            cut,
            hbm,
            hbm,
        ],
        out_specs=[cut, cut, hbm, hbm, gspec],
        out_shape=[
            jax.ShapeDtypeStruct(q.shape, jnp.bfloat16),
            jax.ShapeDtypeStruct(q.shape, jnp.bfloat16),
            jax.ShapeDtypeStruct(part, jnp.bfloat16),
            jax.ShapeDtypeStruct(part, jnp.bfloat16),
            jax.ShapeDtypeStruct((8, hd), jnp.float32),
        ],
        scratch_shapes=[
            pltpu.VMEM((2, slots, width2), jnp.bfloat16),
            pltpu.VMEM((2,) + part, jnp.bfloat16),
            pltpu.VMEM((rows, 2 * hd), jnp.bfloat16),
            pltpu.VMEM((rows, 2 * hd), jnp.bfloat16),
            pltpu.VMEM((slots, rows), jnp.bfloat16),
            pltpu.VMEM((slots, rows), jnp.bfloat16),
            pltpu.VMEM((2, slots, 2 * tokens), jnp.float32),
            pltpu.VMEM((2, slots, 2 * tokens), jnp.float32),
            pltpu.VMEM((slots, tokens), jnp.float32),
            pltpu.VMEM((2, tokens, hd), jnp.bfloat16),
            pltpu.SemaphoreType.DMA((4,)),
        ],
        compiler_params=pltpu.CompilerParams(
            dimension_semantics=("arbitrary",), vmem_limit_bytes=32 * 1024 * 1024
        ),
        cost_estimate=pl.CostEstimate(
            flops=flops,
            bytes_accessed=8 * q.size + 8 * own.size,
            transcendentals=KV_HEADS * rows * slots,
        ),
    )(seg, counts, gate, seg.reshape(1, tokens), q, dy, own, other)


def add_up(refs, at):
    total = refs[0][at].astype(jnp.float32)
    for r in refs[1:]:
        total = total + r[at].astype(jnp.float32)
    return total


def finish_kernel(mine, gate, *refs):
    ins, (dk_ref, dv_ref, g_ref) = refs[:-3], refs[-3:]
    hd = ins[0].shape[1]
    for h in range(2 * KV_HEADS):
        out = (dk_ref, dv_ref)[h // KV_HEADS]
        lanes = slice(h % KV_HEADS * hd, (h % KV_HEADS + 1) * hd)
        out[:, lanes] = add_up(ins, slice(h * mine, (h + 1) * mine))
    digits = add_up(ins, slice(2 * KV_HEADS * mine, None))
    line = lax.broadcasted_iota(jnp.int32, digits.shape, 0)
    units = jnp.zeros(digits.shape, jnp.float32)
    for i in range(GROWS):
        units = jnp.where(line == i, 4.0 ** (GTOP - i), units)
    g_ref[0] = jnp.sum(jnp.sum(digits * units, axis=0, keepdims=True) * gate[0:1, :])


def finish(mine, gate, parts):
    hd = parts[0].shape[1]
    smem = pl.BlockSpec(memory_space=pltpu.SMEM)
    vmem = pl.BlockSpec(memory_space=pltpu.VMEM)
    full = jax.ShapeDtypeStruct((mine, KV_HEADS * hd), jnp.float32)
    return pl.pallas_call(
        functools.partial(finish_kernel, mine),
        in_specs=[vmem] + [vmem] * len(parts),
        out_specs=[vmem, vmem, smem],
        out_shape=[full, full, jax.ShapeDtypeStruct((1,), jnp.float32)],
        compiler_params=pltpu.CompilerParams(vmem_limit_bytes=4 * 1024 * 1024),
    )(gate, *parts)


def local(queries, keys, values, seg_image, tile_counts, gate, cotangent):
    f32, bf16 = jnp.float32, jnp.bfloat16
    mine, width = keys.shape
    hd = width // KV_HEADS
    cols = lax.axis_size("z")
    folded = cols == 4
    half = cols * mine

    def swap(x, even, odd):
        perm = []
        for i in range(8 * cols):
            place = [i // (4 * cols), i // (2 * cols) % 2, i // 2 % cols, i % 2]
            dim, bit = odd if place[1] else even
            place[dim] ^= bit
            perm.append((i, ((place[0] * 2 + place[1]) * cols + place[2]) * 2 + place[3]))
        return lax.ppermute(x, AXES, perm)

    x1, y1, z1, z2 = (0, 1), (3, 1), (2, 1), (2, 2)
    near = ((z2, y1), (z1, z2))
    far = ((x1, z1), (y1, x1)) if folded else ((x1, y1), (y1, x1))
    steps = near + far if folded else far

    buf = jnp.concatenate([keys, values], axis=1)
    if not folded:
        buf = lax.all_gather(buf, "z", axis=0, tiled=True)
    for even, odd in steps:
        buf = jnp.concatenate([buf, swap(buf, even, odd)], axis=0)
    own = buf.reshape(2, 2, half, 2 * width)
    core = ((1, 1), (1, 1))
    other = swap(own, *core)

    y, dq, part_own, part_other, g = attend(
        mine, cols, folded, seg_image, tile_counts, gate, queries, cotangent, own, other
    )

    part = (part_own.astype(f32) + swap(part_other, *core).astype(f32)).astype(bf16)
    part = part.reshape((-1,) + part.shape[3:])
    for even, odd in steps[::-1]:
        keep, away = jnp.split(part, 2)
        parts = [keep, swap(away, even, odd)]
        part = (parts[0].astype(f32) + parts[1].astype(f32)).astype(bf16)
    if folded:
        parts = [p[0] for p in parts]
    else:
        part = parts[0][0].astype(f32) + parts[1][0].astype(f32)
        grads, gates = part[:-GROWS].reshape(2 * KV_HEADS, cols, mine, hd), part[-GROWS:]
        grads = lax.psum_scatter(grads, "z", scatter_dimension=1, tiled=True)
        parts = [jnp.concatenate([grads.reshape(-1, hd), lax.psum(gates, "z")], axis=0)]
    return (y, dq, *finish(mine, g, parts))


def solution(mesh):
    section, mp = mesh.shape["section"], mesh.shape["mp"]
    fine = Mesh(mesh.devices.reshape(section // 2, 2, mp // 2, 2), AXES)
    rows = P(AXES, None)
    return jax.shard_map(
        local,
        mesh=fine,
        in_specs=(rows, rows, rows, P(AXES), P(), P(), rows),
        out_specs=(rows, rows, rows, rows, P()),
        check_vma=False,
    )
```

```python
import functools

import jax
import jax.numpy as jnp
from jax import lax
from jax.experimental import pallas as pl
from jax.experimental.pallas import tpu as pltpu
from jax.sharding import Mesh
from jax.sharding import PartitionSpec as P

KV_HEADS = 4
TILE_TOK = 64
IMG_TOK = 256
AXES = ("x", "core", "z", "y")
NEG = -1e30
LOG2E = 1.4426950408889634
GROWS = 16
GTOP = 8
STRIP = 32
LINE = PEERS = (1, 2, 3)

NT = (((1,), (1,)), ((), ()))
NN = (((1,), (0,)), ((), ()))


def mm(a, b, dims):
    return lax.dot_general(a, b, dims, preferred_element_type=jnp.float32)


def attend_kernel(
    mine,
    cols,
    folded,
    seg_s,
    cnt_s,
    gate_s,
    seg_v,
    q_ref,
    dy_ref,
    own,
    other,
    y_ref,
    dq_ref,
    part_own,
    part_other,
    g_ref,
    kv,
    acc,
    qc,
    dc,
    p16,
    ds16,
    sbuf,
    dbuf,
    bias,
    rowsel,
    sems,
):
    step = pl.program_id(0)
    heads = pl.num_programs(0)
    tokens = q_ref.shape[0]
    slots, width = kv.shape[1], kv.shape[2] // 2
    half = slots // 2
    hd = width // heads
    group = q_ref.shape[1] // hd
    scale = 1.0 / hd**0.5
    core, xpos = lax.axis_index("core"), lax.axis_index("x")
    ypos, zpos = lax.axis_index("y"), lax.axis_index("z")
    img_a, img_b = seg_s[0], seg_s[tokens - 1]

    def place(img):
        return img % 2, (img // 2) ^ xpos

    def fetch(i, img, start):
        par, dx = place(img)
        for src, mask in ((own, par == core), (other, par != core)):

            @pl.when(mask)
            def _():
                for h in range(2):
                    c = pltpu.make_async_copy(src.at[dx, h], kv.at[i, pl.ds(h * half, half)], sems.at[i])
                    c.start() if start else c.wait()

    in_a = seg_v[...] == img_a
    tg = jnp.tanh(jnp.full((1, hd), gate_s[0], jnp.float32))

    @pl.when(step == 0)
    def _():
        fetch(0, img_a, True)
        fetch(1, img_b, True)
        acc[...] = jnp.zeros_like(acc)
        g_ref[...] = jnp.zeros_like(g_ref)
        n = lax.broadcasted_iota(jnp.int32, (slots, tokens), 0)
        z, y = n // mine % cols, (n // half) ^ ypos
        if folded:
            z = z ^ zpos
        tile = (z * (2 * mine) + y * mine + n % mine) // TILE_TOK
        bias[...] = jnp.where(tile < jnp.where(in_a, cnt_s[img_a], cnt_s[img_b]), 0.0, NEG)
        side_a = jnp.broadcast_to(in_a.astype(jnp.float32), (hd, tokens)).T
        rowsel[0] = side_a.astype(jnp.bfloat16)
        rowsel[1] = (1.0 - side_a).astype(jnp.bfloat16)
        fetch(0, img_a, False)
        fetch(1, img_b, False)

    kcols = pl.ds(pl.multiple_of(step * hd, hd), hd)
    vcols = pl.ds(pl.multiple_of(width + step * hd, hd), hd)
    kcat = jnp.concatenate([kv[0, :, kcols], kv[1, :, kcols]], axis=1)
    vcat = jnp.concatenate([kv[0, :, vcols], kv[1, :, vcols]], axis=1)
    kcat_t = kcat.T
    vcat_t = vcat.T
    for g in range(group):
        feats = slice(g * hd, (g + 1) * hd)
        rows = slice(g * tokens, (g + 1) * tokens)
        q = q_ref[:, feats]
        dy = dy_ref[:, feats]
        for i in range(2):
            side = slice(i * hd, (i + 1) * hd)
            qc[rows, side] = q * rowsel[i]
            dc[rows, side] = dy * rowsel[i]

    span = 2 * tokens
    blocks = group // 2
    strips = [slice(i, i + STRIP) for i in range(0, slots, STRIP)]
    in_a2 = jnp.concatenate([in_a, in_a], axis=1)
    tg2 = jnp.concatenate([tg, tg], axis=1)
    slope = scale * tg2

    def fold8(x):
        return jnp.sum(x.reshape(x.shape[0] // 8, 8, x.shape[1]), axis=0)

    def products(h):
        i = h % 2
        rows = slice(h * span, (h + 1) * span)
        s = mm(kcat, qc[rows, :], NT)
        top = jnp.full((8, span), NEG, jnp.float32)
        for strip in strips:
            x = s[strip] + jnp.concatenate([bias[strip], bias[strip]], axis=1)
            sbuf[i, strip] = x
            top = jnp.maximum(top, jnp.max(x.reshape(STRIP // 8, 8, span), axis=0))
        dbuf[i] = mm(vcat, dc[rows, :], NT)
        return top

    def softmax(h, top):
        i = h % 2
        rows = slice(h * span, (h + 1) * span)
        top = jnp.max(top, axis=0, keepdims=True) * (scale * LOG2E)
        norm = jnp.zeros((8, span), jnp.float32)
        dots = jnp.zeros((8, span), jnp.float32)
        for strip in strips:
            e = jnp.exp2(sbuf[i, strip] * (scale * LOG2E) - top)
            sbuf[i, strip] = e
            norm = norm + fold8(e)
            dots = dots + fold8(e * dbuf[i, strip])
        inv = 1.0 / jnp.sum(norm, axis=0, keepdims=True)
        delta = slope * (inv * jnp.sum(dots, axis=0, keepdims=True))
        for strip in strips:
            p = sbuf[i, strip] * inv
            p16[strip, rows] = p.astype(jnp.bfloat16)
            ds16[strip, rows] = (p * (slope * dbuf[i, strip] - delta)).astype(jnp.bfloat16)

    def outputs(h):
        rows = slice(h * span, (h + 1) * span)
        o = mm(vcat_t, p16[:, rows], NN)
        o = (tg2 * jnp.where(in_a2, o[:hd], o[hd:])).astype(jnp.bfloat16)
        dq = mm(kcat_t, ds16[:, rows], NN)
        dq = jnp.where(in_a2, dq[:hd], dq[hd:]).astype(jnp.bfloat16)
        for j in range(2):
            feats = slice((2 * h + j) * hd, (2 * h + j + 1) * hd)
            toks = slice(j * tokens, (j + 1) * tokens)
            y_ref[:, feats] = o[:, toks].T
            dq_ref[:, feats] = dq[:, toks].T

    def slot_grads(lo, hi):
        rows = slice(lo * span, hi * span)
        return mm(ds16[:, rows], qc[rows, :], NN), mm(p16[:, rows], dc[rows, :], NN)

    top = products(0)
    dk = dv = 0.0
    for h in range(blocks):
        ahead = products(h + 1) if h + 1 < blocks else None
        softmax(h, top)
        top = ahead
        outputs(h)
        if h % 2:
            more = slot_grads(h - 1, h + 1)
            dk, dv = dk + more[0], dv + more[1]
    dk = dk.astype(jnp.bfloat16)
    g_ref[...] += fold8((dv * vcat.astype(jnp.float32))[:, :hd] + (dv * vcat.astype(jnp.float32))[:, hd:])
    dv = (jnp.concatenate([tg, tg], axis=1) * dv).astype(jnp.bfloat16)
    pieces = 2 * acc.shape[3]
    per = slots // pieces
    krows = pl.ds(pl.multiple_of(step * per, per), per)
    vrows = pl.ds(pl.multiple_of((heads + step) * per, per), per)
    for img, lanes in ((img_b, slice(hd, 2 * hd)), (img_a, slice(0, hd))):
        par, dx = place(img)
        for j in range(pieces):
            at = slice(j * per, (j + 1) * per)
            acc[par, dx, j // (pieces // 2), j % (pieces // 2), krows] = dk[at, lanes]
            acc[par, dx, j // (pieces // 2), j % (pieces // 2), vrows] = dv[at, lanes]

    def leave(rows, i):
        lay = slice(None), slice(None), slice(None), rows
        return (
            pltpu.make_async_copy(acc.at[(1 - core,) + lay], part_other.at[lay], sems.at[2 + 2 * i]),
            pltpu.make_async_copy(acc.at[(core,) + lay], part_own.at[lay], sems.at[3 + 2 * i]),
        )

    def head_rows(h):
        return pl.ds(h * per, per), pl.ds((heads + h) * per, per)

    for h in range(KV_HEADS):

        @pl.when(step == h)
        def _():
            for i, rows in enumerate(head_rows(h)):
                for c in leave(rows, 2 * h + i):
                    c.start()

    @pl.when(step == heads - 1)
    def _():
        left = jnp.broadcast_to(jnp.sum(g_ref[...], axis=0, keepdims=True), (GROWS, hd))
        line = lax.broadcasted_iota(jnp.int32, (GROWS, hd), 0)
        digits = jnp.zeros((GROWS, hd), jnp.float32)
        for i in range(GROWS):
            unit = 4.0 ** (GTOP - i)
            d = jnp.round(left * (1.0 / unit))
            left = left - d * unit
            digits = jnp.where(line == i, d, digits)
        digits = digits.astype(jnp.bfloat16)
        g_ref[...] = jnp.broadcast_to(1.0 - tg * tg, g_ref.shape)
        for i in range(8):
            for j in range(pieces // 2):
                acc[i // 4, i // 2 % 2, i % 2, j, 2 * heads * per :] = digits
        tail = leave(pl.ds(2 * KV_HEADS * per, GROWS), 2 * KV_HEADS)
        for c in tail:
            c.start()
        for h in range(KV_HEADS):
            for i, rows in enumerate(head_rows(h)):
                for c in leave(rows, 2 * h + i):
                    c.wait()
        for c in tail:
            c.wait()


def attend(mine, cols, folded, seg, counts, gate, q, dy, own, other):
    tokens, feats = q.shape
    slots, width2 = 2 * own.shape[2], own.shape[3]
    hd = width2 // 2 // KV_HEADS
    block = feats // KV_HEADS
    rows = block // hd * tokens
    smem = pl.BlockSpec(memory_space=pltpu.SMEM)
    hbm = pl.BlockSpec(memory_space=pl.ANY)
    cut = pl.BlockSpec((tokens, block), lambda i: (0, i))
    gspec = pl.BlockSpec((8, hd), lambda i: (0, 0))
    flops = 12 * KV_HEADS * rows * slots * hd * 2
    pieces = 8 if folded else 2
    part = (2, 2, pieces // 2, 2 * KV_HEADS * (slots // pieces) + GROWS, hd)
    return pl.pallas_call(
        functools.partial(attend_kernel, mine, cols, folded),
        grid=(KV_HEADS,),
        in_specs=[
            smem,
            smem,
            smem,
            pl.BlockSpec((1, tokens), lambda i: (0, 0)),
            cut,
            cut,
            hbm,
            hbm,
        ],
        out_specs=[cut, cut, hbm, hbm, gspec],
        out_shape=[
            jax.ShapeDtypeStruct(q.shape, jnp.bfloat16),
            jax.ShapeDtypeStruct(q.shape, jnp.bfloat16),
            jax.ShapeDtypeStruct(part, jnp.bfloat16),
            jax.ShapeDtypeStruct(part, jnp.bfloat16),
            jax.ShapeDtypeStruct((8, hd), jnp.float32),
        ],
        scratch_shapes=[
            pltpu.VMEM((2, slots, width2), jnp.bfloat16),
            pltpu.VMEM((2,) + part, jnp.bfloat16),
            pltpu.VMEM((rows, 2 * hd), jnp.bfloat16),
            pltpu.VMEM((rows, 2 * hd), jnp.bfloat16),
            pltpu.VMEM((slots, rows), jnp.bfloat16),
            pltpu.VMEM((slots, rows), jnp.bfloat16),
            pltpu.VMEM((2, slots, 2 * tokens), jnp.float32),
            pltpu.VMEM((2, slots, 2 * tokens), jnp.float32),
            pltpu.VMEM((slots, tokens), jnp.float32),
            pltpu.VMEM((2, tokens, hd), jnp.bfloat16),
            pltpu.SemaphoreType.DMA((4 + 4 * KV_HEADS,)),
        ],
        compiler_params=pltpu.CompilerParams(
            dimension_semantics=("arbitrary",), vmem_limit_bytes=32 * 1024 * 1024
        ),
        cost_estimate=pl.CostEstimate(
            flops=flops,
            bytes_accessed=8 * q.size + 8 * own.size,
            transcendentals=KV_HEADS * rows * slots,
        ),
    )(seg, counts, gate, seg.reshape(1, tokens), q, dy, own, other)


def add_up(refs, at):
    total = refs[0][at].astype(jnp.float32)
    for r in refs[1:]:
        total = total + r[at].astype(jnp.float32)
    return total


def finish_kernel(mine, gate, *refs):
    ins, (dk_ref, dv_ref, g_ref) = refs[:-3], refs[-3:]
    hd = ins[0].shape[1]
    for h in range(2 * KV_HEADS):
        out = (dk_ref, dv_ref)[h // KV_HEADS]
        lanes = slice(h % KV_HEADS * hd, (h % KV_HEADS + 1) * hd)
        out[:, lanes] = add_up(ins, slice(h * mine, (h + 1) * mine))
    digits = add_up(ins, slice(2 * KV_HEADS * mine, None))
    line = lax.broadcasted_iota(jnp.int32, digits.shape, 0)
    units = jnp.zeros(digits.shape, jnp.float32)
    for i in range(GROWS):
        units = jnp.where(line == i, 4.0 ** (GTOP - i), units)
    g_ref[0] = jnp.sum(jnp.sum(digits * units, axis=0, keepdims=True) * gate[0:1, :])


def finish(mine, gate, parts):
    hd = parts[0].shape[1]
    smem = pl.BlockSpec(memory_space=pltpu.SMEM)
    vmem = pl.BlockSpec(memory_space=pltpu.VMEM)
    full = jax.ShapeDtypeStruct((mine, KV_HEADS * hd), jnp.float32)
    return pl.pallas_call(
        functools.partial(finish_kernel, mine),
        in_specs=[vmem] + [vmem] * len(parts),
        out_specs=[vmem, vmem, smem],
        out_shape=[full, full, jax.ShapeDtypeStruct((1,), jnp.float32)],
        compiler_params=pltpu.CompilerParams(vmem_limit_bytes=4 * 1024 * 1024),
    )(gate, *parts)


def local(queries, keys, values, seg_image, tile_counts, gate, cotangent):
    f32, bf16 = jnp.float32, jnp.bfloat16
    mine, width = keys.shape
    hd = width // KV_HEADS
    cols = lax.axis_size("z")
    folded = cols == 4
    half = cols * mine

    def send_z(x, k):
        return lax.ppermute(x, "z", [(i, i ^ k) for i in range(cols)])

    def send_xy(x, p):
        return lax.ppermute(x, ("x", "y"), [(i, i ^ p) for i in range(4)])

    def send_core(x):
        return lax.ppermute(x, "core", [(0, 1), (1, 0)])

    kv = jnp.concatenate([keys, values], axis=1)
    if folded:
        line = [send_z(kv, k) for k in LINE]
        near = [send_xy(kv, p) for p in (1, 2)]
        line, near = lax.optimization_barrier((jnp.concatenate(line, axis=0), near))
        block = jnp.concatenate([kv, line], axis=0)
        diag = send_xy(block, 3)
        own = [block, near[0], send_xy(line, 1), near[1], send_xy(line, 2), diag]
    else:
        line = lax.all_gather(kv, "z", axis=0, tiled=True)
        own = [line] + [send_xy(line, p) for p in PEERS]
    own = jnp.concatenate(own, axis=0).reshape(2, 2, half, 2 * width)
    other = send_core(own)

    y, dq, part_own, part_other, g = attend(
        mine, cols, folded, seg_image, tile_counts, gate, queries, cotangent, own, other
    )

    part = (part_own.astype(f32) + send_core(part_other).astype(f32)).astype(bf16)
    part = part.reshape((4,) + part.shape[2:])
    if folded:
        line = part[0, 1:].astype(f32)
        for p in PEERS:
            line = line + send_xy(part[p, 1:], p).astype(f32)
        line = line.astype(bf16)
        parts = [part[0, 0]] + [send_xy(part[p, 0], p) for p in PEERS]
        parts += [send_z(line[k - 1], k) for k in LINE]
    else:
        line = part[0, 0].astype(f32)
        for p in PEERS:
            line = line + send_xy(part[p, 0], p).astype(f32)
        grads, gates = line[:-GROWS].reshape(2 * KV_HEADS, cols, mine, hd), line[-GROWS:]
        grads = lax.psum_scatter(grads, "z", scatter_dimension=1, tiled=True)
        parts = [jnp.concatenate([grads.reshape(-1, hd), lax.psum(gates, "z")], axis=0)]
    return (y, dq, *finish(mine, g, parts))


def solution(mesh):
    section, mp = mesh.shape["section"], mesh.shape["mp"]
    fine = Mesh(mesh.devices.reshape(section // 2, 2, mp // 2, 2), AXES)
    rows = P(AXES, None)
    return jax.shard_map(
        local,
        mesh=fine,
        in_specs=(rows, rows, rows, P(AXES), P(), P(), rows),
        out_specs=(rows, rows, rows, rows, P()),
        check_vma=False,
    )
```

```python
import functools

import jax
import jax.numpy as jnp
from jax import lax
from jax.experimental import pallas as pl
from jax.experimental.pallas import tpu as pltpu
from jax.sharding import Mesh
from jax.sharding import PartitionSpec as P

KV_HEADS = 4
TILE_TOK = 64
IMG_TOK = 256
AXES = ("x", "core", "z", "y")
NEG = -1e30
LOG2E = 1.4426950408889634
GROWS = 16
GTOP = 8
STRIP = 32
LINE = PEERS = (1, 2, 3)

NT = (((1,), (1,)), ((), ()))
NN = (((1,), (0,)), ((), ()))


def mm(a, b, dims):
    return lax.dot_general(a, b, dims, preferred_element_type=jnp.float32)


def prepare_kernel(seg_s, seg_v, q_ref, dy_ref, qc, dc, qt, dt, rowsel):
    tokens = q_ref.shape[0]
    hd = rowsel.shape[2]
    in_a = (seg_v[...] == seg_s[0]).astype(jnp.float32)

    @pl.when(pl.program_id(0) == 0)
    def _():
        side_a = jnp.broadcast_to(in_a, (hd, tokens)).T
        rowsel[0] = side_a.astype(jnp.bfloat16)
        rowsel[1] = (1.0 - side_a).astype(jnp.bfloat16)

    lanesel = [jnp.broadcast_to(m, (hd, tokens)).astype(jnp.bfloat16) for m in (in_a, 1.0 - in_a)]
    for g in range(q_ref.shape[1] // hd):
        feats = slice(g * hd, (g + 1) * hd)
        rows = slice(g * tokens, (g + 1) * tokens)
        for src, plain, turned in ((q_ref, qc, qt), (dy_ref, dc, dt)):
            x = src[:, feats]
            xt = x.T
            for i in range(2):
                side = slice(i * hd, (i + 1) * hd)
                plain[0, rows, side] = x * rowsel[i]
                turned[0, side, rows] = xt * lanesel[i]


def prepare(hd, seg, q, dy):
    tokens, feats = q.shape
    block = feats // KV_HEADS
    rows = block // hd * tokens
    cut = pl.BlockSpec((tokens, block), lambda i: (0, i))
    shapes = [(rows, 2 * hd)] * 2 + [(2 * hd, rows)] * 2
    return pl.pallas_call(
        prepare_kernel,
        grid=(KV_HEADS,),
        in_specs=[
            pl.BlockSpec(memory_space=pltpu.SMEM),
            pl.BlockSpec((1, tokens), lambda i: (0, 0)),
            cut,
            cut,
        ],
        out_specs=[pl.BlockSpec((1,) + s, lambda i: (i, 0, 0)) for s in shapes],
        out_shape=[jax.ShapeDtypeStruct((KV_HEADS,) + s, jnp.bfloat16) for s in shapes],
        scratch_shapes=[pltpu.VMEM((2, tokens, hd), jnp.bfloat16)],
        compiler_params=pltpu.CompilerParams(vmem_limit_bytes=16 * 1024 * 1024),
        cost_estimate=pl.CostEstimate(flops=4 * 10**9, bytes_accessed=20 * q.size, transcendentals=0),
    )(seg, seg.reshape(1, tokens), q, dy)


def outputs_kernel(seg_s, gate_s, seg_v, p16, ds16, k_ref, v_ref, y_ref, dq_ref):
    tokens = y_ref.shape[0]
    hd = k_ref.shape[2]
    span = 2 * tokens
    in_a = seg_v[...] == seg_s[0]
    in_a2 = jnp.concatenate([in_a, in_a], axis=1)
    tg2 = jnp.tanh(jnp.full((1, span), gate_s[0], jnp.float32))
    kcat_t = jnp.concatenate([k_ref[0], k_ref[1]], axis=1).T
    vcat_t = jnp.concatenate([v_ref[0], v_ref[1]], axis=1).T
    for h in range(y_ref.shape[1] // hd // 2):
        rows = slice(h * span, (h + 1) * span)
        o = mm(vcat_t, p16[0, :, rows], NN)
        o = (tg2 * jnp.where(in_a2, o[:hd], o[hd:])).astype(jnp.bfloat16)
        dq = mm(kcat_t, ds16[0, :, rows], NN)
        dq = jnp.where(in_a2, dq[:hd], dq[hd:]).astype(jnp.bfloat16)
        for j in range(2):
            feats = slice((2 * h + j) * hd, (2 * h + j + 1) * hd)
            toks = slice(j * tokens, (j + 1) * tokens)
            y_ref[:, feats] = o[:, toks].T
            dq_ref[:, feats] = dq[:, toks].T


def outputs(seg, gate, p16, ds16, kv):
    tokens = seg.shape[0]
    slots, rows = p16.shape[1:]
    hd = kv.shape[2] // 2 // KV_HEADS
    block = rows // tokens * hd
    smem = pl.BlockSpec(memory_space=pltpu.SMEM)
    full = pl.BlockSpec((1, slots, rows), lambda i: (i, 0, 0))
    cut = pl.BlockSpec((tokens, block), lambda i: (0, i))
    shape = jax.ShapeDtypeStruct((tokens, KV_HEADS * block), jnp.bfloat16)
    return pl.pallas_call(
        outputs_kernel,
        grid=(KV_HEADS,),
        in_specs=[
            smem,
            smem,
            pl.BlockSpec((1, tokens), lambda i: (0, 0)),
            full,
            full,
            pl.BlockSpec((2, slots, hd), lambda i: (0, 0, i)),
            pl.BlockSpec((2, slots, hd), lambda i: (0, 0, KV_HEADS + i)),
        ],
        out_specs=[cut, cut],
        out_shape=[shape, shape],
        compiler_params=pltpu.CompilerParams(vmem_limit_bytes=16 * 1024 * 1024),
        cost_estimate=pl.CostEstimate(flops=5 * 10**9, bytes_accessed=12 * p16.size, transcendentals=0),
    )(seg, gate, seg.reshape(1, tokens), p16, ds16, kv, kv)


def scores_kernel(
    mine,
    cols,
    folded,
    seg_s,
    cnt_s,
    gate_s,
    seg_v,
    qc,
    dc,
    qt,
    dt,
    own,
    other,
    p16,
    ds16,
    kv_out,
    part_own,
    part_other,
    g_ref,
    kv,
    acc,
    sbuf,
    dbuf,
    bias,
    sems,
):
    step = pl.program_id(0)
    heads = pl.num_programs(0)
    tokens = seg_v.shape[1]
    slots, width = kv.shape[1], kv.shape[2] // 2
    half = slots // 2
    hd = width // heads
    group = qc.shape[1] // tokens
    scale = 1.0 / hd**0.5
    core, xpos = lax.axis_index("core"), lax.axis_index("x")
    ypos, zpos = lax.axis_index("y"), lax.axis_index("z")
    img_a, img_b = seg_s[0], seg_s[tokens - 1]

    def place(img):
        return img % 2, (img // 2) ^ xpos

    def fetch(i, img, start):
        par, dx = place(img)
        for src, mask in ((own, par == core), (other, par != core)):

            @pl.when(mask)
            def _():
                for h in range(2):
                    c = pltpu.make_async_copy(src.at[dx, h], kv.at[i, pl.ds(h * half, half)], sems.at[i])
                    c.start() if start else c.wait()

    in_a = seg_v[...] == img_a
    tg = jnp.tanh(jnp.full((1, hd), gate_s[0], jnp.float32))

    @pl.when(step == 0)
    def _():
        fetch(0, img_a, True)
        fetch(1, img_b, True)
        acc[...] = jnp.zeros_like(acc)
        g_ref[...] = jnp.zeros_like(g_ref)
        n = lax.broadcasted_iota(jnp.int32, (slots, tokens), 0)
        z, y = n // mine % cols, (n // half) ^ ypos
        if folded:
            z = z ^ zpos
        tile = (z * (2 * mine) + y * mine + n % mine) // TILE_TOK
        bias[...] = jnp.where(tile < jnp.where(in_a, cnt_s[img_a], cnt_s[img_b]), 0.0, NEG)
        fetch(0, img_a, False)
        fetch(1, img_b, False)
        pltpu.make_async_copy(kv, kv_out, sems.at[2]).start()

    kcols = pl.ds(pl.multiple_of(step * hd, hd), hd)
    vcols = pl.ds(pl.multiple_of(width + step * hd, hd), hd)
    kcat = jnp.concatenate([kv[0, :, kcols], kv[1, :, kcols]], axis=1)
    vcat = jnp.concatenate([kv[0, :, vcols], kv[1, :, vcols]], axis=1)
    span = 2 * tokens
    blocks = group // 2
    strips = [slice(i, i + STRIP) for i in range(0, slots, STRIP)]
    slope = scale * jnp.concatenate([tg, tg], axis=1)

    def fold8(x):
        return jnp.sum(x.reshape(x.shape[0] // 8, 8, x.shape[1]), axis=0)

    def products(h):
        i = h % 2
        rows = slice(h * span, (h + 1) * span)
        s = mm(kcat, qt[0, :, rows], NN)
        top = jnp.full((8, span), NEG, jnp.float32)
        for strip in strips:
            x = s[strip] + jnp.concatenate([bias[strip], bias[strip]], axis=1)
            sbuf[i, strip] = x
            top = jnp.maximum(top, jnp.max(x.reshape(STRIP // 8, 8, span), axis=0))
        dbuf[i] = mm(vcat, dt[0, :, rows], NN)
        return top

    def softmax(h, top):
        i = h % 2
        rows = slice(h * span, (h + 1) * span)
        top = jnp.max(top, axis=0, keepdims=True) * (scale * LOG2E)
        norm = jnp.zeros((8, span), jnp.float32)
        dots = jnp.zeros((8, span), jnp.float32)
        for strip in strips:
            e = jnp.exp2(sbuf[i, strip] * (scale * LOG2E) - top)
            sbuf[i, strip] = e
            norm = norm + fold8(e)
            dots = dots + fold8(e * dbuf[i, strip])
        inv = 1.0 / jnp.sum(norm, axis=0, keepdims=True)
        delta = slope * (inv * jnp.sum(dots, axis=0, keepdims=True))
        for strip in strips:
            p = sbuf[i, strip] * inv
            p16[0, strip, rows] = p.astype(jnp.bfloat16)
            ds16[0, strip, rows] = (p * (slope * dbuf[i, strip] - delta)).astype(jnp.bfloat16)

    def slot_grads(lo, hi):
        rows = slice(lo * span, hi * span)
        return mm(ds16[0, :, rows], qc[0, rows, :], NN), mm(p16[0, :, rows], dc[0, rows, :], NN)

    top = products(0)
    dk = dv = 0.0
    for h in range(blocks):
        ahead = products(h + 1) if h + 1 < blocks else None
        softmax(h, top)
        top = ahead
        if h % 2:
            more = slot_grads(h - 1, h + 1)
            dk, dv = dk + more[0], dv + more[1]
    dk = dk.astype(jnp.bfloat16)
    g_ref[...] += fold8((dv * vcat.astype(jnp.float32))[:, :hd] + (dv * vcat.astype(jnp.float32))[:, hd:])
    dv = (jnp.concatenate([tg, tg], axis=1) * dv).astype(jnp.bfloat16)
    pieces = 2 * acc.shape[3]
    per = slots // pieces
    krows = pl.ds(pl.multiple_of(step * per, per), per)
    vrows = pl.ds(pl.multiple_of((heads + step) * per, per), per)
    for img, lanes in ((img_b, slice(hd, 2 * hd)), (img_a, slice(0, hd))):
        par, dx = place(img)
        for j in range(pieces):
            at = slice(j * per, (j + 1) * per)
            acc[par, dx, j // (pieces // 2), j % (pieces // 2), krows] = dk[at, lanes]
            acc[par, dx, j // (pieces // 2), j % (pieces // 2), vrows] = dv[at, lanes]

    def leave(rows, i):
        lay = slice(None), slice(None), slice(None), rows
        return (
            pltpu.make_async_copy(acc.at[(1 - core,) + lay], part_other.at[lay], sems.at[3 + 2 * i]),
            pltpu.make_async_copy(acc.at[(core,) + lay], part_own.at[lay], sems.at[4 + 2 * i]),
        )

    def head_rows(h):
        return pl.ds(h * per, per), pl.ds((heads + h) * per, per)

    for h in range(KV_HEADS):

        @pl.when(step == h)
        def _():
            for i, rows in enumerate(head_rows(h)):
                for c in leave(rows, 2 * h + i):
                    c.start()

    @pl.when(step == heads - 1)
    def _():
        left = jnp.broadcast_to(jnp.sum(g_ref[...], axis=0, keepdims=True), (GROWS, hd))
        line = lax.broadcasted_iota(jnp.int32, (GROWS, hd), 0)
        digits = jnp.zeros((GROWS, hd), jnp.float32)
        for i in range(GROWS):
            unit = 4.0 ** (GTOP - i)
            d = jnp.round(left * (1.0 / unit))
            left = left - d * unit
            digits = jnp.where(line == i, d, digits)
        digits = digits.astype(jnp.bfloat16)
        g_ref[...] = jnp.broadcast_to(1.0 - tg * tg, g_ref.shape)
        for i in range(8):
            for j in range(pieces // 2):
                acc[i // 4, i // 2 % 2, i % 2, j, 2 * heads * per :] = digits
        tail = leave(pl.ds(2 * KV_HEADS * per, GROWS), 2 * KV_HEADS)
        for c in tail:
            c.start()
        for h in range(KV_HEADS):
            for i, rows in enumerate(head_rows(h)):
                for c in leave(rows, 2 * h + i):
                    c.wait()
        for c in tail:
            c.wait()
        pltpu.make_async_copy(kv, kv_out, sems.at[2]).wait()


def scores(mine, cols, folded, seg, counts, gate, prepared, own, other):
    tokens = seg.shape[0]
    slots, width2 = 2 * own.shape[2], own.shape[3]
    hd = width2 // 2 // KV_HEADS
    rows = prepared[0].shape[1]
    smem = pl.BlockSpec(memory_space=pltpu.SMEM)
    hbm = pl.BlockSpec(memory_space=pl.ANY)
    gspec = pl.BlockSpec((8, hd), lambda i: (0, 0))
    full = pl.BlockSpec((1, slots, rows), lambda i: (i, 0, 0))
    pieces = 8 if folded else 2
    part = (2, 2, pieces // 2, 2 * KV_HEADS * (slots // pieces) + GROWS, hd)
    return pl.pallas_call(
        functools.partial(scores_kernel, mine, cols, folded),
        grid=(KV_HEADS,),
        in_specs=[
            smem,
            smem,
            smem,
            pl.BlockSpec((1, tokens), lambda i: (0, 0)),
        ]
        + [pl.BlockSpec((1,) + x.shape[1:], lambda i: (i, 0, 0)) for x in prepared]
        + [hbm, hbm],
        out_specs=[full, full, hbm, hbm, hbm, gspec],
        out_shape=[
            jax.ShapeDtypeStruct((KV_HEADS, slots, rows), jnp.bfloat16),
            jax.ShapeDtypeStruct((KV_HEADS, slots, rows), jnp.bfloat16),
            jax.ShapeDtypeStruct((2, slots, width2), jnp.bfloat16),
            jax.ShapeDtypeStruct(part, jnp.bfloat16),
            jax.ShapeDtypeStruct(part, jnp.bfloat16),
            jax.ShapeDtypeStruct((8, hd), jnp.float32),
        ],
        scratch_shapes=[
            pltpu.VMEM((2, slots, width2), jnp.bfloat16),
            pltpu.VMEM((2,) + part, jnp.bfloat16),
            pltpu.VMEM((2, slots, 2 * tokens), jnp.float32),
            pltpu.VMEM((2, slots, 2 * tokens), jnp.float32),
            pltpu.VMEM((slots, tokens), jnp.float32),
            pltpu.SemaphoreType.DMA((5 + 4 * KV_HEADS,)),
        ],
        compiler_params=pltpu.CompilerParams(vmem_limit_bytes=28 * 1024 * 1024),
        cost_estimate=pl.CostEstimate(
            flops=8 * KV_HEADS * rows * slots * hd * 2,
            bytes_accessed=12 * KV_HEADS * rows * slots,
            transcendentals=KV_HEADS * rows * slots,
        ),
    )(seg, counts, gate, seg.reshape(1, tokens), *prepared, own, other)


def add_up(refs, at):
    total = refs[0][at].astype(jnp.float32)
    for r in refs[1:]:
        total = total + r[at].astype(jnp.float32)
    return total


def finish_kernel(mine, gate, *refs):
    ins, (dk_ref, dv_ref, g_ref) = refs[:-3], refs[-3:]
    hd = ins[0].shape[1]
    for h in range(2 * KV_HEADS):
        out = (dk_ref, dv_ref)[h // KV_HEADS]
        lanes = slice(h % KV_HEADS * hd, (h % KV_HEADS + 1) * hd)
        out[:, lanes] = add_up(ins, slice(h * mine, (h + 1) * mine))
    digits = add_up(ins, slice(2 * KV_HEADS * mine, None))
    line = lax.broadcasted_iota(jnp.int32, digits.shape, 0)
    units = jnp.zeros(digits.shape, jnp.float32)
    for i in range(GROWS):
        units = jnp.where(line == i, 4.0 ** (GTOP - i), units)
    g_ref[0] = jnp.sum(jnp.sum(digits * units, axis=0, keepdims=True) * gate[0:1, :])


def finish(mine, gate, parts):
    hd = parts[0].shape[1]
    smem = pl.BlockSpec(memory_space=pltpu.SMEM)
    vmem = pl.BlockSpec(memory_space=pltpu.VMEM)
    full = jax.ShapeDtypeStruct((mine, KV_HEADS * hd), jnp.float32)
    return pl.pallas_call(
        functools.partial(finish_kernel, mine),
        in_specs=[vmem] + [vmem] * len(parts),
        out_specs=[vmem, vmem, smem],
        out_shape=[full, full, jax.ShapeDtypeStruct((1,), jnp.float32)],
        compiler_params=pltpu.CompilerParams(vmem_limit_bytes=4 * 1024 * 1024),
    )(gate, *parts)


def local(queries, keys, values, seg_image, tile_counts, gate, cotangent):
    f32, bf16 = jnp.float32, jnp.bfloat16
    mine, width = keys.shape
    hd = width // KV_HEADS
    cols = lax.axis_size("z")
    folded = cols == 4
    half = cols * mine

    def send_z(x, k):
        return lax.ppermute(x, "z", [(i, i ^ k) for i in range(cols)])

    def send_xy(x, p):
        return lax.ppermute(x, ("x", "y"), [(i, i ^ p) for i in range(4)])

    def send_core(x):
        return lax.ppermute(x, "core", [(0, 1), (1, 0)])

    kv = lax.optimization_barrier(jnp.concatenate([keys, values], axis=1))
    if folded:
        line = [send_z(kv, k) for k in LINE]
        near = [send_xy(kv, p) for p in (1, 2)]
        line, near, seg_late = lax.optimization_barrier((jnp.concatenate(line, axis=0), near, seg_image))
        block = jnp.concatenate([kv, line], axis=0)
        diag = send_xy(block, 3)
        own = [block, near[0], send_xy(line, 1), near[1], send_xy(line, 2), diag]
    else:
        line = lax.all_gather(kv, "z", axis=0, tiled=True)
        own = [line] + [send_xy(line, p) for p in PEERS]
        seg_late = seg_image
    own = jnp.concatenate(own, axis=0).reshape(2, 2, half, 2 * width)
    prepared = list(prepare(hd, seg_late, queries, cotangent))
    own, prepared[0] = lax.optimization_barrier((own, prepared[0]))
    other = send_core(own)
    p16, ds16, kv_used, part_own, part_other, g = scores(
        mine, cols, folded, seg_image, tile_counts, gate, prepared, own, other
    )

    part = (part_own.astype(f32) + send_core(part_other).astype(f32)).astype(bf16)
    part, p16 = lax.optimization_barrier((part, p16))
    y, dq = outputs(seg_image, gate, p16, ds16, kv_used)
    part = part.reshape((4,) + part.shape[2:])
    if folded:
        line = part[0, 1:].astype(f32)
        for p in PEERS:
            line = line + send_xy(part[p, 1:], p).astype(f32)
        late, y = lax.optimization_barrier((part, y))
        line, y = lax.optimization_barrier((line.astype(bf16), y))
        parts = [late[0, 0]] + [send_xy(late[p, 0], p) for p in PEERS]
        parts += [send_z(line[k - 1], k) for k in LINE]
    else:
        line = part[0, 0].astype(f32)
        for p in PEERS:
            line = line + send_xy(part[p, 0], p).astype(f32)
        grads, gates = line[:-GROWS].reshape(2 * KV_HEADS, cols, mine, hd), line[-GROWS:]
        grads = lax.psum_scatter(grads, "z", scatter_dimension=1, tiled=True)
        parts = [jnp.concatenate([grads.reshape(-1, hd), lax.psum(gates, "z")], axis=0)]
    return (y, dq, *finish(mine, g, parts))


def solution(mesh):
    section, mp = mesh.shape["section"], mesh.shape["mp"]
    fine = Mesh(mesh.devices.reshape(section // 2, 2, mp // 2, 2), AXES)
    rows = P(AXES, None)
    return jax.shard_map(
        local,
        mesh=fine,
        in_specs=(rows, rows, rows, P(AXES), P(), P(), rows),
        out_specs=(rows, rows, rows, rows, P()),
        check_vma=False,
    )
```

```python
import functools

import jax
import jax.numpy as jnp
from jax import lax
from jax.experimental import pallas as pl
from jax.experimental.pallas import tpu as pltpu
from jax.sharding import Mesh
from jax.sharding import PartitionSpec as P

KV_HEADS = 4
TILE_TOK = 64
IMG_TOK = 256
AXES = ("x", "core", "z", "y")
NEG = -1e30
LOG2E = 1.4426950408889634
GROWS = 16
GTOP = 8
STRIP = 32
LINE = PEERS = (1, 2, 3)

NT = (((1,), (1,)), ((), ()))
NN = (((1,), (0,)), ((), ()))


def mm(a, b, dims):
    return lax.dot_general(a, b, dims, preferred_element_type=jnp.float32)


def outputs_kernel(seg_s, gate_s, seg_v, p16, ds16, k_ref, v_ref, y_ref, dq_ref):
    tokens = y_ref.shape[0]
    hd = k_ref.shape[2]
    span = 2 * tokens
    in_a = seg_v[...] == seg_s[0]
    in_a2 = jnp.concatenate([in_a, in_a], axis=1)
    tg2 = jnp.tanh(jnp.full((1, span), gate_s[0], jnp.float32))
    kcat_t = jnp.concatenate([k_ref[0], k_ref[1]], axis=1).T
    vcat_t = jnp.concatenate([v_ref[0], v_ref[1]], axis=1).T
    for h in range(y_ref.shape[1] // hd // 2):
        rows = slice(h * span, (h + 1) * span)
        o = mm(vcat_t, p16[0, :, rows], NN)
        o = (tg2 * jnp.where(in_a2, o[:hd], o[hd:])).astype(jnp.bfloat16)
        dq = mm(kcat_t, ds16[0, :, rows], NN)
        dq = jnp.where(in_a2, dq[:hd], dq[hd:]).astype(jnp.bfloat16)
        for j in range(2):
            feats = slice((2 * h + j) * hd, (2 * h + j + 1) * hd)
            toks = slice(j * tokens, (j + 1) * tokens)
            y_ref[:, feats] = o[:, toks].T
            dq_ref[:, feats] = dq[:, toks].T


def outputs(seg, gate, p16, ds16, kv):
    tokens = seg.shape[0]
    slots, rows = p16.shape[1:]
    hd = kv.shape[2] // 2 // KV_HEADS
    block = rows // tokens * hd
    smem = pl.BlockSpec(memory_space=pltpu.SMEM)
    full = pl.BlockSpec((1, slots, rows), lambda i: (i, 0, 0))
    cut = pl.BlockSpec((tokens, block), lambda i: (0, i))
    shape = jax.ShapeDtypeStruct((tokens, KV_HEADS * block), jnp.bfloat16)
    return pl.pallas_call(
        outputs_kernel,
        grid=(KV_HEADS,),
        in_specs=[
            smem,
            smem,
            pl.BlockSpec((1, tokens), lambda i: (0, 0)),
            full,
            full,
            pl.BlockSpec((2, slots, hd), lambda i: (0, 0, i)),
            pl.BlockSpec((2, slots, hd), lambda i: (0, 0, KV_HEADS + i)),
        ],
        out_specs=[cut, cut],
        out_shape=[shape, shape],
        compiler_params=pltpu.CompilerParams(vmem_limit_bytes=16 * 1024 * 1024),
        cost_estimate=pl.CostEstimate(flops=5 * 10**9, bytes_accessed=12 * p16.size, transcendentals=0),
    )(seg, gate, seg.reshape(1, tokens), p16, ds16, kv, kv)


def scores_kernel(
    mine,
    cols,
    folded,
    seg_s,
    cnt_s,
    gate_s,
    seg_v,
    q_ref,
    dy_ref,
    own,
    other,
    p16,
    ds16,
    kv_out,
    part_own,
    part_other,
    g_ref,
    kv,
    acc,
    qc,
    dc,
    rowsel,
    sbuf,
    dbuf,
    bias,
    sems,
):
    step = pl.program_id(0)
    heads = pl.num_programs(0)
    tokens = seg_v.shape[1]
    slots, width = kv.shape[1], kv.shape[2] // 2
    half = slots // 2
    hd = width // heads
    group = qc.shape[0] // tokens
    scale = 1.0 / hd**0.5
    core, xpos = lax.axis_index("core"), lax.axis_index("x")
    ypos, zpos = lax.axis_index("y"), lax.axis_index("z")
    img_a, img_b = seg_s[0], seg_s[tokens - 1]

    def place(img):
        return img % 2, (img // 2) ^ xpos

    def fetch(i, img, start):
        par, dx = place(img)
        for src, mask in ((own, par == core), (other, par != core)):

            @pl.when(mask)
            def _():
                for h in range(2):
                    c = pltpu.make_async_copy(src.at[dx, h], kv.at[i, pl.ds(h * half, half)], sems.at[i])
                    c.start() if start else c.wait()

    in_a = seg_v[...] == img_a
    tg = jnp.tanh(jnp.full((1, hd), gate_s[0], jnp.float32))

    @pl.when(step == 0)
    def _():
        fetch(0, img_a, True)
        fetch(1, img_b, True)
        acc[...] = jnp.zeros_like(acc)
        g_ref[...] = jnp.zeros_like(g_ref)
        n = lax.broadcasted_iota(jnp.int32, (slots, tokens), 0)
        z, y = n // mine % cols, (n // half) ^ ypos
        if folded:
            z = z ^ zpos
        tile = (z * (2 * mine) + y * mine + n % mine) // TILE_TOK
        bias[...] = jnp.where(tile < jnp.where(in_a, cnt_s[img_a], cnt_s[img_b]), 0.0, NEG)
        side_a = jnp.broadcast_to(in_a.astype(jnp.float32), (hd, tokens)).T
        rowsel[0] = side_a.astype(jnp.bfloat16)
        rowsel[1] = (1.0 - side_a).astype(jnp.bfloat16)
        fetch(0, img_a, False)
        fetch(1, img_b, False)
        pltpu.make_async_copy(kv, kv_out, sems.at[2]).start()

    kcols = pl.ds(pl.multiple_of(step * hd, hd), hd)
    vcols = pl.ds(pl.multiple_of(width + step * hd, hd), hd)
    kcat = jnp.concatenate([kv[0, :, kcols], kv[1, :, kcols]], axis=1)
    vcat = jnp.concatenate([kv[0, :, vcols], kv[1, :, vcols]], axis=1)
    for g in range(group):
        feats = slice(g * hd, (g + 1) * hd)
        rows = slice(g * tokens, (g + 1) * tokens)
        q, dy = q_ref[:, feats], dy_ref[:, feats]
        for i in range(2):
            side = slice(i * hd, (i + 1) * hd)
            qc[rows, side] = q * rowsel[i]
            dc[rows, side] = dy * rowsel[i]

    span = 2 * tokens
    blocks = group // 2
    strips = [slice(i, i + STRIP) for i in range(0, slots, STRIP)]
    slope = scale * jnp.concatenate([tg, tg], axis=1)

    def fold8(x):
        return jnp.sum(x.reshape(x.shape[0] // 8, 8, x.shape[1]), axis=0)

    def products(h):
        i = h % 2
        rows = slice(h * span, (h + 1) * span)
        s = mm(kcat, qc[rows, :], NT)
        top = jnp.full((8, span), NEG, jnp.float32)
        for strip in strips:
            x = s[strip] + jnp.concatenate([bias[strip], bias[strip]], axis=1)
            sbuf[i, strip] = x
            top = jnp.maximum(top, jnp.max(x.reshape(STRIP // 8, 8, span), axis=0))
        dbuf[i] = mm(vcat, dc[rows, :], NT)
        return top

    def softmax(h, top):
        i = h % 2
        rows = slice(h * span, (h + 1) * span)
        top = jnp.max(top, axis=0, keepdims=True) * (scale * LOG2E)
        norm = jnp.zeros((8, span), jnp.float32)
        dots = jnp.zeros((8, span), jnp.float32)
        for strip in strips:
            e = jnp.exp2(sbuf[i, strip] * (scale * LOG2E) - top)
            sbuf[i, strip] = e
            norm = norm + fold8(e)
            dots = dots + fold8(e * dbuf[i, strip])
        inv = 1.0 / jnp.sum(norm, axis=0, keepdims=True)
        delta = slope * (inv * jnp.sum(dots, axis=0, keepdims=True))
        for strip in strips:
            p = sbuf[i, strip] * inv
            p16[0, strip, rows] = p.astype(jnp.bfloat16)
            ds16[0, strip, rows] = (p * (slope * dbuf[i, strip] - delta)).astype(jnp.bfloat16)

    def slot_grads(lo, hi):
        rows = slice(lo * span, hi * span)
        return mm(ds16[0, :, rows], qc[rows, :], NN), mm(p16[0, :, rows], dc[rows, :], NN)

    top = products(0)
    dk = dv = 0.0
    for h in range(blocks):
        ahead = products(h + 1) if h + 1 < blocks else None
        softmax(h, top)
        top = ahead
        if h % 2:
            more = slot_grads(h - 1, h + 1)
            dk, dv = dk + more[0], dv + more[1]
    dk = dk.astype(jnp.bfloat16)
    g_ref[...] += fold8((dv * vcat.astype(jnp.float32))[:, :hd] + (dv * vcat.astype(jnp.float32))[:, hd:])
    dv = (jnp.concatenate([tg, tg], axis=1) * dv).astype(jnp.bfloat16)
    pieces = 2 * acc.shape[3]
    per = slots // pieces
    krows = pl.ds(pl.multiple_of(step * per, per), per)
    vrows = pl.ds(pl.multiple_of((heads + step) * per, per), per)
    for img, lanes in ((img_b, slice(hd, 2 * hd)), (img_a, slice(0, hd))):
        par, dx = place(img)
        for j in range(pieces):
            at = slice(j * per, (j + 1) * per)
            acc[par, dx, j // (pieces // 2), j % (pieces // 2), krows] = dk[at, lanes]
            acc[par, dx, j // (pieces // 2), j % (pieces // 2), vrows] = dv[at, lanes]

    def leave(rows, i):
        lay = slice(None), slice(None), slice(None), rows
        return (
            pltpu.make_async_copy(acc.at[(1 - core,) + lay], part_other.at[lay], sems.at[3 + 2 * i]),
            pltpu.make_async_copy(acc.at[(core,) + lay], part_own.at[lay], sems.at[4 + 2 * i]),
        )

    def head_rows(h):
        return pl.ds(h * per, per), pl.ds((heads + h) * per, per)

    for h in range(KV_HEADS):

        @pl.when(step == h)
        def _():
            for i, rows in enumerate(head_rows(h)):
                for c in leave(rows, 2 * h + i):
                    c.start()

    @pl.when(step == heads - 1)
    def _():
        left = jnp.broadcast_to(jnp.sum(g_ref[...], axis=0, keepdims=True), (GROWS, hd))
        line = lax.broadcasted_iota(jnp.int32, (GROWS, hd), 0)
        digits = jnp.zeros((GROWS, hd), jnp.float32)
        for i in range(GROWS):
            unit = 4.0 ** (GTOP - i)
            d = jnp.round(left * (1.0 / unit))
            left = left - d * unit
            digits = jnp.where(line == i, d, digits)
        digits = digits.astype(jnp.bfloat16)
        g_ref[...] = jnp.broadcast_to(1.0 - tg * tg, g_ref.shape)
        for i in range(8):
            for j in range(pieces // 2):
                acc[i // 4, i // 2 % 2, i % 2, j, 2 * heads * per :] = digits
        tail = leave(pl.ds(2 * KV_HEADS * per, GROWS), 2 * KV_HEADS)
        for c in tail:
            c.start()
        for h in range(KV_HEADS):
            for i, rows in enumerate(head_rows(h)):
                for c in leave(rows, 2 * h + i):
                    c.wait()
        for c in tail:
            c.wait()
        pltpu.make_async_copy(kv, kv_out, sems.at[2]).wait()


def scores(mine, cols, folded, seg, counts, gate, q, dy, own, other):
    tokens = seg.shape[0]
    slots, width2 = 2 * own.shape[2], own.shape[3]
    hd = width2 // 2 // KV_HEADS
    block = q.shape[1] // KV_HEADS
    rows = block // hd * tokens
    smem = pl.BlockSpec(memory_space=pltpu.SMEM)
    hbm = pl.BlockSpec(memory_space=pl.ANY)
    gspec = pl.BlockSpec((8, hd), lambda i: (0, 0))
    full = pl.BlockSpec((1, slots, rows), lambda i: (i, 0, 0))
    pieces = 8 if folded else 2
    part = (2, 2, pieces // 2, 2 * KV_HEADS * (slots // pieces) + GROWS, hd)
    return pl.pallas_call(
        functools.partial(scores_kernel, mine, cols, folded),
        grid=(KV_HEADS,),
        in_specs=[
            smem,
            smem,
            smem,
            pl.BlockSpec((1, tokens), lambda i: (0, 0)),
        ]
        + [pl.BlockSpec((tokens, block), lambda i: (0, i))] * 2
        + [hbm, hbm],
        out_specs=[full, full, hbm, hbm, hbm, gspec],
        out_shape=[
            jax.ShapeDtypeStruct((KV_HEADS, slots, rows), jnp.bfloat16),
            jax.ShapeDtypeStruct((KV_HEADS, slots, rows), jnp.bfloat16),
            jax.ShapeDtypeStruct((2, slots, width2), jnp.bfloat16),
            jax.ShapeDtypeStruct(part, jnp.bfloat16),
            jax.ShapeDtypeStruct(part, jnp.bfloat16),
            jax.ShapeDtypeStruct((8, hd), jnp.float32),
        ],
        scratch_shapes=[
            pltpu.VMEM((2, slots, width2), jnp.bfloat16),
            pltpu.VMEM((2,) + part, jnp.bfloat16),
            pltpu.VMEM((rows, 2 * hd), jnp.bfloat16),
            pltpu.VMEM((rows, 2 * hd), jnp.bfloat16),
            pltpu.VMEM((2, tokens, hd), jnp.bfloat16),
            pltpu.VMEM((2, slots, 2 * tokens), jnp.float32),
            pltpu.VMEM((2, slots, 2 * tokens), jnp.float32),
            pltpu.VMEM((slots, tokens), jnp.float32),
            pltpu.SemaphoreType.DMA((5 + 4 * KV_HEADS,)),
        ],
        compiler_params=pltpu.CompilerParams(vmem_limit_bytes=28 * 1024 * 1024),
        cost_estimate=pl.CostEstimate(
            flops=8 * KV_HEADS * rows * slots * hd * 2,
            bytes_accessed=12 * KV_HEADS * rows * slots,
            transcendentals=KV_HEADS * rows * slots,
        ),
    )(seg, counts, gate, seg.reshape(1, tokens), q, dy, own, other)


def add_up(refs, at):
    total = refs[0][at].astype(jnp.float32)
    for r in refs[1:]:
        total = total + r[at].astype(jnp.float32)
    return total


def finish_kernel(mine, gate, *refs):
    ins, (dk_ref, dv_ref, g_ref) = refs[:-3], refs[-3:]
    hd = ins[0].shape[1]
    for h in range(2 * KV_HEADS):
        out = (dk_ref, dv_ref)[h // KV_HEADS]
        lanes = slice(h % KV_HEADS * hd, (h % KV_HEADS + 1) * hd)
        out[:, lanes] = add_up(ins, slice(h * mine, (h + 1) * mine))
    digits = add_up(ins, slice(2 * KV_HEADS * mine, None))
    line = lax.broadcasted_iota(jnp.int32, digits.shape, 0)
    units = jnp.zeros(digits.shape, jnp.float32)
    for i in range(GROWS):
        units = jnp.where(line == i, 4.0 ** (GTOP - i), units)
    g_ref[0] = jnp.sum(jnp.sum(digits * units, axis=0, keepdims=True) * gate[0:1, :])


def finish(mine, gate, parts):
    hd = parts[0].shape[1]
    smem = pl.BlockSpec(memory_space=pltpu.SMEM)
    vmem = pl.BlockSpec(memory_space=pltpu.VMEM)
    full = jax.ShapeDtypeStruct((mine, KV_HEADS * hd), jnp.float32)
    return pl.pallas_call(
        functools.partial(finish_kernel, mine),
        in_specs=[vmem] + [vmem] * len(parts),
        out_specs=[vmem, vmem, smem],
        out_shape=[full, full, jax.ShapeDtypeStruct((1,), jnp.float32)],
        compiler_params=pltpu.CompilerParams(vmem_limit_bytes=4 * 1024 * 1024),
    )(gate, *parts)


def local(queries, keys, values, seg_image, tile_counts, gate, cotangent):
    f32, bf16 = jnp.float32, jnp.bfloat16
    mine, width = keys.shape
    hd = width // KV_HEADS
    cols = lax.axis_size("z")
    folded = cols == 4
    half = cols * mine

    def send_z(x, k):
        return lax.ppermute(x, "z", [(i, i ^ k) for i in range(cols)])

    def send_xy(x, p):
        return lax.ppermute(x, ("x", "y"), [(i, i ^ p) for i in range(4)])

    def send_core(x):
        return lax.ppermute(x, "core", [(0, 1), (1, 0)])

    kv = lax.optimization_barrier(jnp.concatenate([keys, values], axis=1))
    if folded:
        line = [send_z(kv, k) for k in LINE]
        near = [send_xy(kv, p) for p in (1, 2)]
        line, near = lax.optimization_barrier((jnp.concatenate(line, axis=0), near))
        block = jnp.concatenate([kv, line], axis=0)
        diag = send_xy(block, 3)
        own = [block, near[0], send_xy(line, 1), near[1], send_xy(line, 2), diag]
    else:
        line = lax.all_gather(kv, "z", axis=0, tiled=True)
        own = [line] + [send_xy(line, p) for p in PEERS]
    own = jnp.concatenate(own, axis=0).reshape(2, 2, half, 2 * width)
    other = send_core(own)
    p16, ds16, kv_used, part_own, part_other, g = scores(
        mine, cols, folded, seg_image, tile_counts, gate, queries, cotangent, own, other
    )

    part = (part_own.astype(f32) + send_core(part_other).astype(f32)).astype(bf16)
    part, p16 = lax.optimization_barrier((part, p16))
    y, dq = outputs(seg_image, gate, p16, ds16, kv_used)
    part = part.reshape((4,) + part.shape[2:])
    if folded:
        line = part[0].astype(f32)
        for p in PEERS:
            line = line + send_xy(part[p], p).astype(f32)
        line, y = lax.optimization_barrier((line.astype(bf16), y))
        parts = [line[0]] + [send_z(line[k], k) for k in LINE]
    else:
        line = part[0, 0].astype(f32)
        for p in PEERS:
            line = line + send_xy(part[p, 0], p).astype(f32)
        grads, gates = line[:-GROWS].reshape(2 * KV_HEADS, cols, mine, hd), line[-GROWS:]
        grads = lax.psum_scatter(grads, "z", scatter_dimension=1, tiled=True)
        parts = [jnp.concatenate([grads.reshape(-1, hd), lax.psum(gates, "z")], axis=0)]
    return (y, dq, *finish(mine, g, parts))


def solution(mesh):
    section, mp = mesh.shape["section"], mesh.shape["mp"]
    fine = Mesh(mesh.devices.reshape(section // 2, 2, mp // 2, 2), AXES)
    rows = P(AXES, None)
    return jax.shard_map(
        local,
        mesh=fine,
        in_specs=(rows, rows, rows, P(AXES), P(), P(), rows),
        out_specs=(rows, rows, rows, rows, P()),
        check_vma=False,
    )
```

```python
import functools

import jax
import jax.numpy as jnp
from jax import lax
from jax.experimental import pallas as pl
from jax.experimental.pallas import tpu as pltpu
from jax.sharding import Mesh
from jax.sharding import PartitionSpec as P

KV_HEADS = 4
TILE_TOK = 64
IMG_TOK = 256
AXES = ("x", "core", "z", "y")
NEG = -1e30
LOG2E = 1.4426950408889634
GROWS = 16
GTOP = 8
STRIP = 32
LINE = PEERS = (1, 2, 3)

NT = (((1,), (1,)), ((), ()))
NN = (((1,), (0,)), ((), ()))


def mm(a, b, dims):
    return lax.dot_general(a, b, dims, preferred_element_type=jnp.float32)


def outputs_kernel(seg_s, gate_s, seg_v, p16, ds16, k_ref, v_ref, y_ref, dq_ref):
    tokens = y_ref.shape[0]
    hd = k_ref.shape[2]
    span = 2 * tokens
    in_a = seg_v[...] == seg_s[0]
    in_a2 = jnp.concatenate([in_a, in_a], axis=1)
    tg2 = jnp.tanh(jnp.full((1, span), gate_s[0], jnp.float32))
    kcat_t = jnp.concatenate([k_ref[0], k_ref[1]], axis=1).T
    vcat_t = jnp.concatenate([v_ref[0], v_ref[1]], axis=1).T
    for h in range(y_ref.shape[1] // hd // 2):
        rows = slice(h * span, (h + 1) * span)
        o = mm(vcat_t, p16[0, :, rows], NN)
        o = (tg2 * jnp.where(in_a2, o[:hd], o[hd:])).astype(jnp.bfloat16)
        dq = mm(kcat_t, ds16[0, :, rows], NN)
        dq = (tg2 * (1.0 / hd**0.5) * jnp.where(in_a2, dq[:hd], dq[hd:])).astype(jnp.bfloat16)
        for j in range(2):
            feats = slice((2 * h + j) * hd, (2 * h + j + 1) * hd)
            toks = slice(j * tokens, (j + 1) * tokens)
            y_ref[:, feats] = o[:, toks].T
            dq_ref[:, feats] = dq[:, toks].T


def outputs(seg, gate, p16, ds16, kv):
    tokens = seg.shape[0]
    slots, rows = p16.shape[1:]
    hd = kv.shape[2] // 2 // KV_HEADS
    block = rows // tokens * hd
    smem = pl.BlockSpec(memory_space=pltpu.SMEM)
    full = pl.BlockSpec((1, slots, rows), lambda i: (i, 0, 0))
    cut = pl.BlockSpec((tokens, block), lambda i: (0, i))
    shape = jax.ShapeDtypeStruct((tokens, KV_HEADS * block), jnp.bfloat16)
    return pl.pallas_call(
        outputs_kernel,
        grid=(KV_HEADS,),
        in_specs=[
            smem,
            smem,
            pl.BlockSpec((1, tokens), lambda i: (0, 0)),
            full,
            full,
            pl.BlockSpec((2, slots, hd), lambda i: (0, 0, i)),
            pl.BlockSpec((2, slots, hd), lambda i: (0, 0, KV_HEADS + i)),
        ],
        out_specs=[cut, cut],
        out_shape=[shape, shape],
        compiler_params=pltpu.CompilerParams(vmem_limit_bytes=16 * 1024 * 1024),
        cost_estimate=pl.CostEstimate(flops=5 * 10**9, bytes_accessed=12 * p16.size, transcendentals=0),
    )(seg, gate, seg.reshape(1, tokens), p16, ds16, kv, kv)


def scores_kernel(
    mine,
    cols,
    folded,
    seg_s,
    cnt_s,
    gate_s,
    seg_v,
    q_ref,
    dy_ref,
    own,
    other,
    p16,
    ds16,
    kv_out,
    part_own,
    part_other,
    g_ref,
    kv,
    acc,
    qc,
    dc,
    rowsel,
    sbuf,
    dbuf,
    bias,
    sems,
    fetched,
):
    step = pl.program_id(0)
    heads = pl.num_programs(0)
    tokens = seg_v.shape[1]
    slots, width = kv.shape[1], kv.shape[2] // 2
    half = slots // 2
    hd = width // heads
    group = qc.shape[0] // tokens
    scale = 1.0 / hd**0.5
    core, xpos = lax.axis_index("core"), lax.axis_index("x")
    ypos, zpos = lax.axis_index("y"), lax.axis_index("z")
    img_a, img_b = seg_s[0], seg_s[tokens - 1]

    def place(img):
        return img % 2, (img // 2) ^ xpos

    def fetch(head, start):
        for i, img in enumerate((img_a, img_b)):
            par, dx = place(img)
            for src, mask in ((own, par == core), (other, par != core)):

                @pl.when(mask)
                def _():
                    for h in range(2):
                        for lane in (head * hd, width + head * hd):
                            lanes = pl.ds(lane, hd)
                            c = pltpu.make_async_copy(
                                src.at[dx, h, :, lanes],
                                kv.at[i, pl.ds(h * half, half), lanes],
                                fetched.at[head],
                            )
                            c.start() if start else c.wait()

    in_a = seg_v[...] == img_a
    tg = jnp.tanh(jnp.full((1, hd), gate_s[0], jnp.float32))

    @pl.when(step == 0)
    def _():
        for h in range(KV_HEADS):
            fetch(h, True)
        acc[...] = jnp.zeros_like(acc)
        g_ref[...] = jnp.zeros_like(g_ref)
        n = lax.broadcasted_iota(jnp.int32, (slots, tokens), 0)
        z, y = n // mine % cols, (n // half) ^ ypos
        if folded:
            z = z ^ zpos
        tile = (z * (2 * mine) + y * mine + n % mine) // TILE_TOK
        bias[...] = jnp.where(tile < jnp.where(in_a, cnt_s[img_a], cnt_s[img_b]), 0.0, NEG)
        side_a = jnp.broadcast_to(in_a.astype(jnp.float32), (hd, tokens)).T
        rowsel[0] = side_a.astype(jnp.bfloat16)
        rowsel[1] = (1.0 - side_a).astype(jnp.bfloat16)
    for h in range(KV_HEADS):

        @pl.when(step == h)
        def _():
            fetch(h, False)

    @pl.when(step == heads - 1)
    def _():
        pltpu.make_async_copy(kv, kv_out, sems.at[2]).start()

    kcols = pl.ds(pl.multiple_of(step * hd, hd), hd)
    vcols = pl.ds(pl.multiple_of(width + step * hd, hd), hd)
    kcat = jnp.concatenate([kv[0, :, kcols], kv[1, :, kcols]], axis=1)
    vcat = jnp.concatenate([kv[0, :, vcols], kv[1, :, vcols]], axis=1)
    for g in range(group):
        feats = slice(g * hd, (g + 1) * hd)
        rows = slice(g * tokens, (g + 1) * tokens)
        q, dy = q_ref[:, feats], dy_ref[:, feats]
        for i in range(2):
            side = slice(i * hd, (i + 1) * hd)
            qc[rows, side] = q * rowsel[i]
            dc[rows, side] = dy * rowsel[i]

    span = 2 * tokens
    blocks = group // 2
    strips = [slice(i, i + STRIP) for i in range(0, slots, STRIP)]
    tg2 = jnp.concatenate([tg, tg], axis=1)

    def fold8(x):
        return jnp.sum(x.reshape(x.shape[0] // 8, 8, x.shape[1]), axis=0)

    def products(h):
        i = h % 2
        rows = slice(h * span, (h + 1) * span)
        s = mm(kcat, qc[rows, :], NT)
        top = jnp.full((8, span), NEG, jnp.float32)
        for strip in strips:
            x = s[strip] + jnp.concatenate([bias[strip], bias[strip]], axis=1)
            sbuf[i, strip] = x
            top = jnp.maximum(top, jnp.max(x.reshape(STRIP // 8, 8, span), axis=0))
        dbuf[i] = mm(vcat, dc[rows, :], NT)
        return top

    def softmax(h, top):
        i = h % 2
        rows = slice(h * span, (h + 1) * span)
        top = jnp.max(top, axis=0, keepdims=True) * (scale * LOG2E)
        norm = jnp.zeros((8, span), jnp.float32)
        dots = jnp.zeros((8, span), jnp.float32)
        for strip in strips:
            e = jnp.exp2(sbuf[i, strip] * (scale * LOG2E) - top)
            sbuf[i, strip] = e
            norm = norm + fold8(e)
            dots = dots + fold8(e * dbuf[i, strip])
        inv = 1.0 / jnp.sum(norm, axis=0, keepdims=True)
        delta = inv * jnp.sum(dots, axis=0, keepdims=True)
        for strip in strips:
            p = sbuf[i, strip] * inv
            p16[0, strip, rows] = p.astype(jnp.bfloat16)
            ds16[0, strip, rows] = (p * (dbuf[i, strip] - delta)).astype(jnp.bfloat16)

    def slot_grads(lo, hi):
        rows = slice(lo * span, hi * span)
        return mm(ds16[0, :, rows], qc[rows, :], NN), mm(p16[0, :, rows], dc[rows, :], NN)

    top = products(0)
    dk = dv = 0.0
    for h in range(blocks):
        ahead = products(h + 1) if h + 1 < blocks else None
        softmax(h, top)
        top = ahead
        if h % 2:
            more = slot_grads(h - 1, h + 1)
            dk, dv = dk + more[0], dv + more[1]
    dk = (scale * tg2 * dk).astype(jnp.bfloat16)
    g_ref[...] += fold8((dv * vcat.astype(jnp.float32))[:, :hd] + (dv * vcat.astype(jnp.float32))[:, hd:])
    dv = (tg2 * dv).astype(jnp.bfloat16)
    pieces = 2 * acc.shape[3]
    per = slots // pieces
    krows = pl.ds(pl.multiple_of(step * per, per), per)
    vrows = pl.ds(pl.multiple_of((heads + step) * per, per), per)
    for img, lanes in ((img_b, slice(hd, 2 * hd)), (img_a, slice(0, hd))):
        par, dx = place(img)
        for j in range(pieces):
            at = slice(j * per, (j + 1) * per)
            acc[par, dx, j // (pieces // 2), j % (pieces // 2), krows] = dk[at, lanes]
            acc[par, dx, j // (pieces // 2), j % (pieces // 2), vrows] = dv[at, lanes]

    def leave(rows, i):
        lay = slice(None), slice(None), slice(None), rows
        return (
            pltpu.make_async_copy(acc.at[(1 - core,) + lay], part_other.at[lay], sems.at[3 + 2 * i]),
            pltpu.make_async_copy(acc.at[(core,) + lay], part_own.at[lay], sems.at[4 + 2 * i]),
        )

    def head_rows(h):
        return pl.ds(h * per, per), pl.ds((heads + h) * per, per)

    for h in range(KV_HEADS):

        @pl.when(step == h)
        def _():
            for i, rows in enumerate(head_rows(h)):
                for c in leave(rows, 2 * h + i):
                    c.start()

    @pl.when(step == heads - 1)
    def _():
        left = jnp.broadcast_to(jnp.sum(g_ref[...], axis=0, keepdims=True), (GROWS, hd))
        line = lax.broadcasted_iota(jnp.int32, (GROWS, hd), 0)
        digits = jnp.zeros((GROWS, hd), jnp.float32)
        for i in range(GROWS):
            unit = 4.0 ** (GTOP - i)
            d = jnp.round(left * (1.0 / unit))
            left = left - d * unit
            digits = jnp.where(line == i, d, digits)
        digits = digits.astype(jnp.bfloat16)
        g_ref[...] = jnp.broadcast_to(1.0 - tg * tg, g_ref.shape)
        for i in range(8):
            for j in range(pieces // 2):
                acc[i // 4, i // 2 % 2, i % 2, j, 2 * heads * per :] = digits
        tail = leave(pl.ds(2 * KV_HEADS * per, GROWS), 2 * KV_HEADS)
        for c in tail:
            c.start()
        for h in range(KV_HEADS):
            for i, rows in enumerate(head_rows(h)):
                for c in leave(rows, 2 * h + i):
                    c.wait()
        for c in tail:
            c.wait()
        pltpu.make_async_copy(kv, kv_out, sems.at[2]).wait()


def scores(mine, cols, folded, seg, counts, gate, q, dy, own, other):
    tokens = seg.shape[0]
    slots, width2 = 2 * own.shape[2], own.shape[3]
    hd = width2 // 2 // KV_HEADS
    block = q.shape[1] // KV_HEADS
    rows = block // hd * tokens
    smem = pl.BlockSpec(memory_space=pltpu.SMEM)
    hbm = pl.BlockSpec(memory_space=pl.ANY)
    gspec = pl.BlockSpec((8, hd), lambda i: (0, 0))
    full = pl.BlockSpec((1, slots, rows), lambda i: (i, 0, 0))
    pieces = 8 if folded else 2
    part = (2, 2, pieces // 2, 2 * KV_HEADS * (slots // pieces) + GROWS, hd)
    return pl.pallas_call(
        functools.partial(scores_kernel, mine, cols, folded),
        grid=(KV_HEADS,),
        in_specs=[
            smem,
            smem,
            smem,
            pl.BlockSpec((1, tokens), lambda i: (0, 0)),
        ]
        + [pl.BlockSpec((tokens, block), lambda i: (0, i))] * 2
        + [hbm, hbm],
        out_specs=[full, full, hbm, hbm, hbm, gspec],
        out_shape=[
            jax.ShapeDtypeStruct((KV_HEADS, slots, rows), jnp.bfloat16),
            jax.ShapeDtypeStruct((KV_HEADS, slots, rows), jnp.bfloat16),
            jax.ShapeDtypeStruct((2, slots, width2), jnp.bfloat16),
            jax.ShapeDtypeStruct(part, jnp.bfloat16),
            jax.ShapeDtypeStruct(part, jnp.bfloat16),
            jax.ShapeDtypeStruct((8, hd), jnp.float32),
        ],
        scratch_shapes=[
            pltpu.VMEM((2, slots, width2), jnp.bfloat16),
            pltpu.VMEM((2,) + part, jnp.bfloat16),
            pltpu.VMEM((rows, 2 * hd), jnp.bfloat16),
            pltpu.VMEM((rows, 2 * hd), jnp.bfloat16),
            pltpu.VMEM((2, tokens, hd), jnp.bfloat16),
            pltpu.VMEM((2, slots, 2 * tokens), jnp.float32),
            pltpu.VMEM((2, slots, 2 * tokens), jnp.float32),
            pltpu.VMEM((slots, tokens), jnp.float32),
            pltpu.SemaphoreType.DMA((5 + 4 * KV_HEADS,)),
            pltpu.SemaphoreType.DMA((KV_HEADS,)),
        ],
        compiler_params=pltpu.CompilerParams(vmem_limit_bytes=28 * 1024 * 1024),
        cost_estimate=pl.CostEstimate(
            flops=8 * KV_HEADS * rows * slots * hd * 2,
            bytes_accessed=12 * KV_HEADS * rows * slots,
            transcendentals=KV_HEADS * rows * slots,
        ),
    )(seg, counts, gate, seg.reshape(1, tokens), q, dy, own, other)


def add_up(refs, at):
    total = refs[0][at].astype(jnp.float32)
    for r in refs[1:]:
        total = total + r[at].astype(jnp.float32)
    return total


def finish_kernel(mine, gate, *refs):
    ins, (dk_ref, dv_ref, g_ref) = refs[:-3], refs[-3:]
    hd = ins[0].shape[1]
    for h in range(2 * KV_HEADS):
        out = (dk_ref, dv_ref)[h // KV_HEADS]
        lanes = slice(h % KV_HEADS * hd, (h % KV_HEADS + 1) * hd)
        out[:, lanes] = add_up(ins, slice(h * mine, (h + 1) * mine))
    digits = add_up(ins, slice(2 * KV_HEADS * mine, None))
    line = lax.broadcasted_iota(jnp.int32, digits.shape, 0)
    units = jnp.zeros(digits.shape, jnp.float32)
    for i in range(GROWS):
        units = jnp.where(line == i, 4.0 ** (GTOP - i), units)
    g_ref[0] = jnp.sum(jnp.sum(digits * units, axis=0, keepdims=True) * gate[0:1, :])


def finish(mine, gate, parts):
    hd = parts[0].shape[1]
    smem = pl.BlockSpec(memory_space=pltpu.SMEM)
    vmem = pl.BlockSpec(memory_space=pltpu.VMEM)
    full = jax.ShapeDtypeStruct((mine, KV_HEADS * hd), jnp.float32)
    return pl.pallas_call(
        functools.partial(finish_kernel, mine),
        in_specs=[vmem] + [vmem] * len(parts),
        out_specs=[vmem, vmem, smem],
        out_shape=[full, full, jax.ShapeDtypeStruct((1,), jnp.float32)],
        compiler_params=pltpu.CompilerParams(vmem_limit_bytes=4 * 1024 * 1024),
    )(gate, *parts)


def local(queries, keys, values, seg_image, tile_counts, gate, cotangent):
    f32, bf16 = jnp.float32, jnp.bfloat16
    mine, width = keys.shape
    hd = width // KV_HEADS
    cols = lax.axis_size("z")
    folded = cols == 4
    half = cols * mine

    def send_z(x, k):
        return lax.ppermute(x, "z", [(i, i ^ k) for i in range(cols)])

    def send_xy(x, p):
        return lax.ppermute(x, ("x", "y"), [(i, i ^ p) for i in range(4)])

    def send_core(x):
        return lax.ppermute(x, "core", [(0, 1), (1, 0)])

    kv = jnp.concatenate([keys, values], axis=1)
    if folded:
        near = [send_xy(kv, p) for p in (1, 2)]
        line = [send_z(kv, k) for k in LINE]
        line, near = lax.optimization_barrier((jnp.concatenate(line, axis=0), near))
        kv, line = lax.optimization_barrier((kv, line))
        block = jnp.concatenate([kv, line], axis=0)
        diag = send_xy(block, 3)
        own = [block, near[0], send_xy(line, 1), near[1], send_xy(line, 2), diag]
    else:
        line = lax.all_gather(kv, "z", axis=0, tiled=True)
        own = [line] + [send_xy(line, p) for p in PEERS]
    own = jnp.concatenate(own, axis=0).reshape(2, 2, half, 2 * width)
    other = send_core(own)
    p16, ds16, kv_used, part_own, part_other, g = scores(
        mine, cols, folded, seg_image, tile_counts, gate, queries, cotangent, own, other
    )

    got, p16 = lax.optimization_barrier((send_core(part_other), p16))
    part = (part_own.astype(f32) + got.astype(f32)).astype(bf16)
    y, dq = outputs(seg_image, gate, p16, ds16, kv_used)
    part = part.reshape((4,) + part.shape[2:])
    if folded:
        parts = [part[0, 0]] + [send_xy(part[p, 0], p) for p in PEERS]
        line = part[0, 1:].astype(f32)
        for p in PEERS:
            line = line + send_xy(part[p, 1:], p).astype(f32)
        line, y = lax.optimization_barrier((line.astype(bf16), y))
        parts += [send_z(line[k - 1], k) for k in LINE]
    else:
        line = part[0, 0].astype(f32)
        for p in PEERS:
            line = line + send_xy(part[p, 0], p).astype(f32)
        grads, gates = line[:-GROWS].reshape(2 * KV_HEADS, cols, mine, hd), line[-GROWS:]
        grads = lax.psum_scatter(grads, "z", scatter_dimension=1, tiled=True)
        parts = [jnp.concatenate([grads.reshape(-1, hd), lax.psum(gates, "z")], axis=0)]
    return (y, dq, *finish(mine, g, parts))


def solution(mesh):
    section, mp = mesh.shape["section"], mesh.shape["mp"]
    fine = Mesh(mesh.devices.reshape(section // 2, 2, mp // 2, 2), AXES)
    rows = P(AXES, None)
    return jax.shard_map(
        local,
        mesh=fine,
        in_specs=(rows, rows, rows, P(AXES), P(), P(), rows),
        out_specs=(rows, rows, rows, rows, P()),
        check_vma=False,
    )
```

```python
import functools

import jax
import jax.numpy as jnp
from jax import lax
from jax.experimental import pallas as pl
from jax.experimental.pallas import tpu as pltpu
from jax.sharding import Mesh
from jax.sharding import PartitionSpec as P

KV_HEADS = 4
TILE_TOK = 64
IMG_TOK = 256
AXES = ("x", "core", "z", "y")
NEG = -1e30
LOG2E = 1.4426950408889634
GROWS = 16
GTOP = 8
STRIP = 64
LINE = PEERS = (1, 2, 3)

NT = (((1,), (1,)), ((), ()))
NN = (((1,), (0,)), ((), ()))


def mm(a, b, dims):
    return lax.dot_general(a, b, dims, preferred_element_type=jnp.float32)


def outputs_kernel(seg_s, gate_s, seg_v, p16, ds16, k_ref, v_ref, y_ref, dq_ref):
    tokens = y_ref.shape[0]
    hd = k_ref.shape[2]
    span = 2 * tokens
    in_a = seg_v[...] == seg_s[0]
    in_a2 = jnp.concatenate([in_a, in_a], axis=1)
    tg2 = jnp.tanh(jnp.full((1, span), gate_s[0], jnp.float32))
    kcat_t = jnp.concatenate([k_ref[0], k_ref[1]], axis=1).T
    vcat_t = jnp.concatenate([v_ref[0], v_ref[1]], axis=1).T
    for h in range(y_ref.shape[1] // hd // 2):
        rows = slice(h * span, (h + 1) * span)
        o = mm(vcat_t, p16[0, :, rows], NN)
        o = (tg2 * jnp.where(in_a2, o[:hd], o[hd:])).astype(jnp.bfloat16)
        dq = mm(kcat_t, ds16[0, :, rows], NN)
        dq = (tg2 * (1.0 / hd**0.5) * jnp.where(in_a2, dq[:hd], dq[hd:])).astype(jnp.bfloat16)
        for j in range(2):
            feats = slice((2 * h + j) * hd, (2 * h + j + 1) * hd)
            toks = slice(j * tokens, (j + 1) * tokens)
            y_ref[:, feats] = o[:, toks].T
            dq_ref[:, feats] = dq[:, toks].T


def outputs(seg, gate, p16, ds16, kv):
    tokens = seg.shape[0]
    slots, rows = p16.shape[1:]
    hd = kv.shape[2] // 2 // KV_HEADS
    block = rows // tokens * hd
    smem = pl.BlockSpec(memory_space=pltpu.SMEM)
    full = pl.BlockSpec((1, slots, rows), lambda i: (i, 0, 0))
    cut = pl.BlockSpec((tokens, block), lambda i: (0, i))
    shape = jax.ShapeDtypeStruct((tokens, KV_HEADS * block), jnp.bfloat16)
    return pl.pallas_call(
        outputs_kernel,
        grid=(KV_HEADS,),
        in_specs=[
            smem,
            smem,
            pl.BlockSpec((1, tokens), lambda i: (0, 0)),
            full,
            full,
            pl.BlockSpec((2, slots, hd), lambda i: (0, 0, i)),
            pl.BlockSpec((2, slots, hd), lambda i: (0, 0, KV_HEADS + i)),
        ],
        out_specs=[cut, cut],
        out_shape=[shape, shape],
        compiler_params=pltpu.CompilerParams(vmem_limit_bytes=16 * 1024 * 1024),
        cost_estimate=pl.CostEstimate(flops=5 * 10**9, bytes_accessed=12 * p16.size, transcendentals=0),
    )(seg, gate, seg.reshape(1, tokens), p16, ds16, kv, kv)


def scores_kernel(
    mine,
    cols,
    folded,
    seg_s,
    cnt_s,
    gate_s,
    seg_v,
    q_ref,
    dy_ref,
    own,
    other,
    p16,
    ds16,
    kv_out,
    part_own,
    part_other,
    g_ref,
    kv,
    acc,
    qc,
    dc,
    rowsel,
    sbuf,
    dbuf,
    bias,
    sems,
    fetched,
):
    step = pl.program_id(0)
    heads = pl.num_programs(0)
    tokens = seg_v.shape[1]
    slots, width = kv.shape[1], kv.shape[2] // 2
    half = slots // 2
    hd = width // heads
    group = qc.shape[0] // tokens
    scale = 1.0 / hd**0.5
    core, xpos = lax.axis_index("core"), lax.axis_index("x")
    ypos, zpos = lax.axis_index("y"), lax.axis_index("z")
    img_a, img_b = seg_s[0], seg_s[tokens - 1]

    def place(img):
        return img % 2, (img // 2) ^ xpos

    def fetch(head, start):
        for i, img in enumerate((img_a, img_b)):
            par, dx = place(img)
            for src, mask in ((own, par == core), (other, par != core)):

                @pl.when(mask)
                def _():
                    for h in range(2):
                        for lane in (head * hd, width + head * hd):
                            lanes = pl.ds(lane, hd)
                            c = pltpu.make_async_copy(
                                src.at[dx, h, :, lanes],
                                kv.at[i, pl.ds(h * half, half), lanes],
                                fetched.at[head],
                            )
                            c.start() if start else c.wait()

    in_a = seg_v[...] == img_a
    tg = jnp.tanh(jnp.full((1, hd), gate_s[0], jnp.float32))

    @pl.when(step == 0)
    def _():
        for h in range(KV_HEADS):
            fetch(h, True)
        acc[...] = jnp.zeros_like(acc)
        g_ref[...] = jnp.zeros_like(g_ref)
        n = lax.broadcasted_iota(jnp.int32, (slots, tokens), 0)
        z, y = n // mine % cols, (n // half) ^ ypos
        if folded:
            z = z ^ zpos
        tile = (z * (2 * mine) + y * mine + n % mine) // TILE_TOK
        bias[...] = jnp.where(tile < jnp.where(in_a, cnt_s[img_a], cnt_s[img_b]), 0.0, NEG)
        side_a = jnp.broadcast_to(in_a.astype(jnp.float32), (hd, tokens)).T
        rowsel[0] = side_a.astype(jnp.bfloat16)
        rowsel[1] = (1.0 - side_a).astype(jnp.bfloat16)
    for h in range(KV_HEADS):

        @pl.when(step == h)
        def _():
            fetch(h, False)

    @pl.when(step == heads - 1)
    def _():
        pltpu.make_async_copy(kv, kv_out, sems.at[2]).start()

    kcols = pl.ds(pl.multiple_of(step * hd, hd), hd)
    vcols = pl.ds(pl.multiple_of(width + step * hd, hd), hd)
    kcat = jnp.concatenate([kv[0, :, kcols], kv[1, :, kcols]], axis=1)
    vcat = jnp.concatenate([kv[0, :, vcols], kv[1, :, vcols]], axis=1)
    for g in range(group):
        feats = slice(g * hd, (g + 1) * hd)
        rows = slice(g * tokens, (g + 1) * tokens)
        q, dy = q_ref[:, feats], dy_ref[:, feats]
        for i in range(2):
            side = slice(i * hd, (i + 1) * hd)
            qc[rows, side] = q * rowsel[i]
            dc[rows, side] = dy * rowsel[i]

    span = tokens
    blocks = group
    strips = [slice(i, i + STRIP) for i in range(0, slots, STRIP)]
    tg2 = jnp.concatenate([tg, tg], axis=1)

    def fold8(x):
        return jnp.sum(x.reshape(x.shape[0] // 8, 8, x.shape[1]), axis=0)

    def products(h):
        i = h % 2
        rows = slice(h * span, (h + 1) * span)
        s = mm(kcat, qc[rows, :], NT)
        top = jnp.full((8, span), NEG, jnp.float32)
        for strip in strips:
            x = s[strip] + bias[strip]
            sbuf[i, strip] = x
            top = jnp.maximum(top, jnp.max(x.reshape(STRIP // 8, 8, span), axis=0))
        dbuf[i] = mm(vcat, dc[rows, :], NT)
        return top

    def softmax(h, top):
        i = h % 2
        rows = slice(h * span, (h + 1) * span)
        top = jnp.max(top, axis=0, keepdims=True) * (scale * LOG2E)
        norm = jnp.zeros((8, span), jnp.float32)
        dots = jnp.zeros((8, span), jnp.float32)
        for strip in strips:
            e = jnp.exp2(sbuf[i, strip] * (scale * LOG2E) - top)
            sbuf[i, strip] = e
            norm = norm + fold8(e)
            dots = dots + fold8(e * dbuf[i, strip])
        inv = 1.0 / jnp.sum(norm, axis=0, keepdims=True)
        delta = inv * jnp.sum(dots, axis=0, keepdims=True)
        for strip in strips:
            p = sbuf[i, strip] * inv
            p16[0, strip, rows] = p.astype(jnp.bfloat16)
            ds16[0, strip, rows] = (p * (dbuf[i, strip] - delta)).astype(jnp.bfloat16)

    def slot_grads(lo, hi):
        rows = slice(lo * span, hi * span)
        return mm(ds16[0, :, rows], qc[rows, :], NN), mm(p16[0, :, rows], dc[rows, :], NN)

    top = products(0)
    dk = dv = 0.0
    for h in range(blocks):
        ahead = products(h + 1) if h + 1 < blocks else None
        softmax(h, top)
        top = ahead
        if h % 4 == 3:
            more = slot_grads(h - 3, h + 1)
            dk, dv = dk + more[0], dv + more[1]
    dk = (scale * tg2 * dk).astype(jnp.bfloat16)
    g_ref[...] += fold8((dv * vcat.astype(jnp.float32))[:, :hd] + (dv * vcat.astype(jnp.float32))[:, hd:])
    dv = (tg2 * dv).astype(jnp.bfloat16)
    pieces = 2 * acc.shape[3]
    per = slots // pieces
    krows = pl.ds(pl.multiple_of(step * per, per), per)
    vrows = pl.ds(pl.multiple_of((heads + step) * per, per), per)
    for img, lanes in ((img_b, slice(hd, 2 * hd)), (img_a, slice(0, hd))):
        par, dx = place(img)
        for j in range(pieces):
            at = slice(j * per, (j + 1) * per)
            acc[par, dx, j // (pieces // 2), j % (pieces // 2), krows] = dk[at, lanes]
            acc[par, dx, j // (pieces // 2), j % (pieces // 2), vrows] = dv[at, lanes]

    def leave(rows, i):
        lay = slice(None), slice(None), slice(None), rows
        return (
            pltpu.make_async_copy(acc.at[(1 - core,) + lay], part_other.at[lay], sems.at[3 + 2 * i]),
            pltpu.make_async_copy(acc.at[(core,) + lay], part_own.at[lay], sems.at[4 + 2 * i]),
        )

    def head_rows(h):
        return pl.ds(h * per, per), pl.ds((heads + h) * per, per)

    for h in range(KV_HEADS):

        @pl.when(step == h)
        def _():
            for i, rows in enumerate(head_rows(h)):
                for c in leave(rows, 2 * h + i):
                    c.start()

    @pl.when(step == heads - 1)
    def _():
        left = jnp.broadcast_to(jnp.sum(g_ref[...], axis=0, keepdims=True), (GROWS, hd))
        line = lax.broadcasted_iota(jnp.int32, (GROWS, hd), 0)
        digits = jnp.zeros((GROWS, hd), jnp.float32)
        for i in range(GROWS):
            unit = 4.0 ** (GTOP - i)
            d = jnp.round(left * (1.0 / unit))
            left = left - d * unit
            digits = jnp.where(line == i, d, digits)
        digits = digits.astype(jnp.bfloat16)
        g_ref[...] = jnp.broadcast_to(1.0 - tg * tg, g_ref.shape)
        for i in range(8):
            for j in range(pieces // 2):
                acc[i // 4, i // 2 % 2, i % 2, j, 2 * heads * per :] = digits
        tail = leave(pl.ds(2 * KV_HEADS * per, GROWS), 2 * KV_HEADS)
        for c in tail:
            c.start()
        for h in range(KV_HEADS):
            for i, rows in enumerate(head_rows(h)):
                for c in leave(rows, 2 * h + i):
                    c.wait()
        for c in tail:
            c.wait()
        pltpu.make_async_copy(kv, kv_out, sems.at[2]).wait()


def scores(mine, cols, folded, seg, counts, gate, q, dy, own, other):
    tokens = seg.shape[0]
    slots, width2 = 2 * own.shape[2], own.shape[3]
    hd = width2 // 2 // KV_HEADS
    block = q.shape[1] // KV_HEADS
    rows = block // hd * tokens
    smem = pl.BlockSpec(memory_space=pltpu.SMEM)
    hbm = pl.BlockSpec(memory_space=pl.ANY)
    gspec = pl.BlockSpec((8, hd), lambda i: (0, 0))
    full = pl.BlockSpec((1, slots, rows), lambda i: (i, 0, 0))
    pieces = 8 if folded else 2
    part = (2, 2, pieces // 2, 2 * KV_HEADS * (slots // pieces) + GROWS, hd)
    return pl.pallas_call(
        functools.partial(scores_kernel, mine, cols, folded),
        grid=(KV_HEADS,),
        in_specs=[
            smem,
            smem,
            smem,
            pl.BlockSpec((1, tokens), lambda i: (0, 0)),
        ]
        + [pl.BlockSpec((tokens, block), lambda i: (0, i))] * 2
        + [hbm, hbm],
        out_specs=[full, full, hbm, hbm, hbm, gspec],
        out_shape=[
            jax.ShapeDtypeStruct((KV_HEADS, slots, rows), jnp.bfloat16),
            jax.ShapeDtypeStruct((KV_HEADS, slots, rows), jnp.bfloat16),
            jax.ShapeDtypeStruct((2, slots, width2), jnp.bfloat16),
            jax.ShapeDtypeStruct(part, jnp.bfloat16),
            jax.ShapeDtypeStruct(part, jnp.bfloat16),
            jax.ShapeDtypeStruct((8, hd), jnp.float32),
        ],
        scratch_shapes=[
            pltpu.VMEM((2, slots, width2), jnp.bfloat16),
            pltpu.VMEM((2,) + part, jnp.bfloat16),
            pltpu.VMEM((rows, 2 * hd), jnp.bfloat16),
            pltpu.VMEM((rows, 2 * hd), jnp.bfloat16),
            pltpu.VMEM((2, tokens, hd), jnp.bfloat16),
            pltpu.VMEM((2, slots, tokens), jnp.float32),
            pltpu.VMEM((2, slots, tokens), jnp.float32),
            pltpu.VMEM((slots, tokens), jnp.float32),
            pltpu.SemaphoreType.DMA((5 + 4 * KV_HEADS,)),
            pltpu.SemaphoreType.DMA((KV_HEADS,)),
        ],
        compiler_params=pltpu.CompilerParams(vmem_limit_bytes=28 * 1024 * 1024),
        cost_estimate=pl.CostEstimate(
            flops=8 * KV_HEADS * rows * slots * hd * 2,
            bytes_accessed=12 * KV_HEADS * rows * slots,
            transcendentals=KV_HEADS * rows * slots,
        ),
    )(seg, counts, gate, seg.reshape(1, tokens), q, dy, own, other)


def add_up(refs, at):
    total = refs[0][at].astype(jnp.float32)
    for r in refs[1:]:
        total = total + r[at].astype(jnp.float32)
    return total


def finish_kernel(mine, gate, *refs):
    ins, (dk_ref, dv_ref, g_ref) = refs[:-3], refs[-3:]
    hd = ins[0].shape[1]
    for h in range(2 * KV_HEADS):
        out = (dk_ref, dv_ref)[h // KV_HEADS]
        lanes = slice(h % KV_HEADS * hd, (h % KV_HEADS + 1) * hd)
        out[:, lanes] = add_up(ins, slice(h * mine, (h + 1) * mine))
    digits = add_up(ins, slice(2 * KV_HEADS * mine, None))
    line = lax.broadcasted_iota(jnp.int32, digits.shape, 0)
    units = jnp.zeros(digits.shape, jnp.float32)
    for i in range(GROWS):
        units = jnp.where(line == i, 4.0 ** (GTOP - i), units)
    g_ref[0] = jnp.sum(jnp.sum(digits * units, axis=0, keepdims=True) * gate[0:1, :])


def finish(mine, gate, parts):
    hd = parts[0].shape[1]
    smem = pl.BlockSpec(memory_space=pltpu.SMEM)
    vmem = pl.BlockSpec(memory_space=pltpu.VMEM)
    full = jax.ShapeDtypeStruct((mine, KV_HEADS * hd), jnp.float32)
    return pl.pallas_call(
        functools.partial(finish_kernel, mine),
        in_specs=[vmem] + [vmem] * len(parts),
        out_specs=[vmem, vmem, smem],
        out_shape=[full, full, jax.ShapeDtypeStruct((1,), jnp.float32)],
        compiler_params=pltpu.CompilerParams(vmem_limit_bytes=4 * 1024 * 1024),
    )(gate, *parts)


def local(queries, keys, values, seg_image, tile_counts, gate, cotangent):
    f32, bf16 = jnp.float32, jnp.bfloat16
    mine, width = keys.shape
    hd = width // KV_HEADS
    cols = lax.axis_size("z")
    folded = cols == 4
    half = cols * mine

    def send_z(x, k):
        return lax.ppermute(x, "z", [(i, i ^ k) for i in range(cols)])

    def send_xy(x, p):
        return lax.ppermute(x, ("x", "y"), [(i, i ^ p) for i in range(4)])

    def send_core(x):
        return lax.ppermute(x, "core", [(0, 1), (1, 0)])

    kv = jnp.concatenate([keys, values], axis=1)
    if folded:
        near = [send_xy(kv, p) for p in (1, 2)]
        line = [send_z(kv, k) for k in LINE]
        line, near = lax.optimization_barrier((jnp.concatenate(line, axis=0), near))
        kv, line = lax.optimization_barrier((kv, line))
        block = jnp.concatenate([kv, line], axis=0)
        diag = send_xy(block, 3)
        own = [block, near[0], send_xy(line, 1), near[1], send_xy(line, 2), diag]
    else:
        line = lax.all_gather(kv, "z", axis=0, tiled=True)
        own = [line] + [send_xy(line, p) for p in PEERS]
    own = jnp.concatenate(own, axis=0).reshape(2, 2, half, 2 * width)
    other = send_core(own)
    p16, ds16, kv_used, part_own, part_other, g = scores(
        mine, cols, folded, seg_image, tile_counts, gate, queries, cotangent, own, other
    )

    got, p16 = lax.optimization_barrier((send_core(part_other), p16))
    part = (part_own.astype(f32) + got.astype(f32)).astype(bf16)
    y, dq = outputs(seg_image, gate, p16, ds16, kv_used)
    part = part.reshape((4,) + part.shape[2:])
    if folded:
        parts = [part[0, 0]] + [send_xy(part[p, 0], p) for p in PEERS]
        line = part[0, 1:].astype(f32)
        for p in PEERS:
            line = line + send_xy(part[p, 1:], p).astype(f32)
        line, y = lax.optimization_barrier((line.astype(bf16), y))
        parts += [send_z(line[k - 1], k) for k in LINE]
    else:
        line = part[0, 0].astype(f32)
        for p in PEERS:
            line = line + send_xy(part[p, 0], p).astype(f32)
        grads, gates = line[:-GROWS].reshape(2 * KV_HEADS, cols, mine, hd), line[-GROWS:]
        grads = lax.psum_scatter(grads, "z", scatter_dimension=1, tiled=True)
        parts = [jnp.concatenate([grads.reshape(-1, hd), lax.psum(gates, "z")], axis=0)]
    return (y, dq, *finish(mine, g, parts))


def solution(mesh):
    section, mp = mesh.shape["section"], mesh.shape["mp"]
    fine = Mesh(mesh.devices.reshape(section // 2, 2, mp // 2, 2), AXES)
    rows = P(AXES, None)
    return jax.shard_map(
        local,
        mesh=fine,
        in_specs=(rows, rows, rows, P(AXES), P(), P(), rows),
        out_specs=(rows, rows, rows, rows, P()),
        check_vma=False,
    )
```

```python
import functools

import jax
import jax.numpy as jnp
from jax import lax
from jax.experimental import pallas as pl
from jax.experimental.pallas import tpu as pltpu
from jax.sharding import Mesh
from jax.sharding import PartitionSpec as P

KV_HEADS = 4
TILE_TOK = 64
IMG_TOK = 256
AXES = ("x", "core", "z", "y")
NEG = -1e30
LOG2E = 1.4426950408889634
GROWS = 16
GTOP = 8
STRIP = 32
LINE = PEERS = (1, 2, 3)

NT = (((1,), (1,)), ((), ()))
NN = (((1,), (0,)), ((), ()))


def mm(a, b, dims):
    return lax.dot_general(a, b, dims, preferred_element_type=jnp.float32)


def outputs_kernel(seg_s, gate_s, seg_v, p16, ds16, k_ref, v_ref, y_ref, dq_ref):
    tokens = y_ref.shape[0]
    hd = k_ref.shape[2]
    span = 2 * tokens
    in_a = seg_v[...] == seg_s[0]
    in_a2 = jnp.concatenate([in_a, in_a], axis=1)
    tg2 = jnp.tanh(jnp.full((1, span), gate_s[0], jnp.float32))
    kcat_t = jnp.concatenate([k_ref[0], k_ref[1]], axis=1).T
    vcat_t = jnp.concatenate([v_ref[0], v_ref[1]], axis=1).T
    for h in range(y_ref.shape[1] // hd // 2):
        rows = slice(h * span, (h + 1) * span)
        o = mm(vcat_t, p16[0, :, rows], NN)
        o = (tg2 * jnp.where(in_a2, o[:hd], o[hd:])).astype(jnp.bfloat16)
        dq = mm(kcat_t, ds16[0, :, rows], NN)
        dq = (tg2 * (1.0 / hd**0.5) * jnp.where(in_a2, dq[:hd], dq[hd:])).astype(jnp.bfloat16)
        for j in range(2):
            feats = slice((2 * h + j) * hd, (2 * h + j + 1) * hd)
            toks = slice(j * tokens, (j + 1) * tokens)
            y_ref[:, feats] = o[:, toks].T
            dq_ref[:, feats] = dq[:, toks].T


def outputs(seg, gate, p16, ds16, kv):
    tokens = seg.shape[0]
    slots, rows = p16.shape[1:]
    hd = kv.shape[2] // 2 // KV_HEADS
    block = rows // tokens * hd
    smem = pl.BlockSpec(memory_space=pltpu.SMEM)
    full = pl.BlockSpec((1, slots, rows), lambda i: (i, 0, 0))
    cut = pl.BlockSpec((tokens, block), lambda i: (0, i))
    shape = jax.ShapeDtypeStruct((tokens, KV_HEADS * block), jnp.bfloat16)
    return pl.pallas_call(
        outputs_kernel,
        grid=(KV_HEADS,),
        in_specs=[
            smem,
            smem,
            pl.BlockSpec((1, tokens), lambda i: (0, 0)),
            full,
            full,
            pl.BlockSpec((2, slots, hd), lambda i: (0, 0, i)),
            pl.BlockSpec((2, slots, hd), lambda i: (0, 0, KV_HEADS + i)),
        ],
        out_specs=[cut, cut],
        out_shape=[shape, shape],
        compiler_params=pltpu.CompilerParams(vmem_limit_bytes=16 * 1024 * 1024),
        cost_estimate=pl.CostEstimate(flops=5 * 10**9, bytes_accessed=12 * p16.size, transcendentals=0),
    )(seg, gate, seg.reshape(1, tokens), p16, ds16, kv, kv)


def scores_kernel(
    mine,
    cols,
    folded,
    seg_s,
    cnt_s,
    gate_s,
    seg_v,
    q_ref,
    dy_ref,
    own,
    other,
    p16,
    ds16,
    kv_out,
    part_own,
    part_other,
    g_ref,
    kv,
    acc,
    qc,
    dc,
    rowsel,
    sbuf,
    dbuf,
    bias,
    sems,
    fetched,
):
    step = pl.program_id(0)
    heads = pl.num_programs(0)
    tokens = seg_v.shape[1]
    slots, width = kv.shape[1], kv.shape[2] // 2
    half = slots // 2
    hd = width // heads
    group = qc.shape[0] // tokens
    scale = 1.0 / hd**0.5
    core, xpos = lax.axis_index("core"), lax.axis_index("x")
    ypos, zpos = lax.axis_index("y"), lax.axis_index("z")
    img_a, img_b = seg_s[0], seg_s[tokens - 1]

    def place(img):
        return img % 2, (img // 2) ^ xpos

    def fetch(head, start):
        for i, img in enumerate((img_a, img_b)):
            par, dx = place(img)
            for src, mask in ((own, par == core), (other, par != core)):

                @pl.when(mask)
                def _():
                    for h in range(2):
                        for lane in (head * hd, width + head * hd):
                            lanes = pl.ds(lane, hd)
                            c = pltpu.make_async_copy(
                                src.at[dx, h, :, lanes],
                                kv.at[i, pl.ds(h * half, half), lanes],
                                fetched.at[head],
                            )
                            c.start() if start else c.wait()

    in_a = seg_v[...] == img_a
    tg = jnp.tanh(jnp.full((1, hd), gate_s[0], jnp.float32))

    @pl.when(step == 0)
    def _():
        for h in range(KV_HEADS):
            fetch(h, True)
        acc[...] = jnp.zeros_like(acc)
        g_ref[...] = jnp.zeros_like(g_ref)
        n = lax.broadcasted_iota(jnp.int32, (slots, tokens), 0)
        z, y = n // mine % cols, (n // half) ^ ypos
        if folded:
            z = z ^ zpos
        tile = (z * (2 * mine) + y * mine + n % mine) // TILE_TOK
        bias[...] = jnp.where(tile < jnp.where(in_a, cnt_s[img_a], cnt_s[img_b]), 0.0, NEG)
        side_a = jnp.broadcast_to(in_a.astype(jnp.float32), (hd, tokens)).T
        rowsel[0] = side_a.astype(jnp.bfloat16)
        rowsel[1] = (1.0 - side_a).astype(jnp.bfloat16)
    for h in range(KV_HEADS):

        @pl.when(step == h)
        def _():
            fetch(h, False)

    @pl.when(step == heads - 1)
    def _():
        pltpu.make_async_copy(kv, kv_out, sems.at[2]).start()

    kcols = pl.ds(pl.multiple_of(step * hd, hd), hd)
    vcols = pl.ds(pl.multiple_of(width + step * hd, hd), hd)
    kcat = jnp.concatenate([kv[0, :, kcols], kv[1, :, kcols]], axis=1)
    vcat = jnp.concatenate([kv[0, :, vcols], kv[1, :, vcols]], axis=1)
    for g in range(group):
        feats = slice(g * hd, (g + 1) * hd)
        rows = slice(g * tokens, (g + 1) * tokens)
        q, dy = q_ref[:, feats], dy_ref[:, feats]
        for i in range(2):
            side = slice(i * hd, (i + 1) * hd)
            qc[rows, side] = q * rowsel[i]
            dc[rows, side] = dy * rowsel[i]

    span = 2 * tokens
    blocks = group // 2
    strips = [slice(i, i + STRIP) for i in range(0, slots, STRIP)]
    tg2 = jnp.concatenate([tg, tg], axis=1)

    def fold8(x):
        return jnp.sum(x.reshape(x.shape[0] // 8, 8, x.shape[1]), axis=0)

    def slot_grads(lo, hi):
        rows = slice(lo * span, hi * span)
        return mm(ds16[0, :, rows], qc[rows, :], NN), mm(p16[0, :, rows], dc[rows, :], NN)

    dk = dv = 0.0
    tops, invs, deltas = {}, {}, {}
    for t in range(blocks + 2):
        new, mid, old = t, t - 1, t - 2
        if new < blocks:
            rows = slice(new * span, (new + 1) * span)
            s = mm(kcat, qc[rows, :], NT)
            dbuf[new % 3] = mm(vcat, dc[rows, :], NT)
            top = jnp.full((8, span), NEG, jnp.float32)
        norm = dots = jnp.zeros((8, span), jnp.float32)
        for strip in strips:
            if old >= 0:
                rows = slice(old * span, (old + 1) * span)
                p = sbuf[old % 3, strip] * invs[old]
                p16[0, strip, rows] = p.astype(jnp.bfloat16)
                ds16[0, strip, rows] = (p * (dbuf[old % 3, strip] - deltas[old])).astype(jnp.bfloat16)
            if 0 <= mid < blocks:
                e = jnp.exp2(sbuf[mid % 3, strip] * (scale * LOG2E) - tops[mid])
                sbuf[mid % 3, strip] = e
                norm = norm + fold8(e)
                dots = dots + fold8(e * dbuf[mid % 3, strip])
            if new < blocks:
                x = s[strip] + jnp.concatenate([bias[strip], bias[strip]], axis=1)
                sbuf[new % 3, strip] = x
                top = jnp.maximum(top, jnp.max(x.reshape(STRIP // 8, 8, span), axis=0))
        if new < blocks:
            tops[new] = jnp.max(top, axis=0, keepdims=True) * (scale * LOG2E)
        if 0 <= mid < blocks:
            invs[mid] = 1.0 / jnp.sum(norm, axis=0, keepdims=True)
            deltas[mid] = invs[mid] * jnp.sum(dots, axis=0, keepdims=True)
        if old >= 0 and old % 2:
            more = slot_grads(old - 1, old + 1)
            dk, dv = dk + more[0], dv + more[1]
    dk = (scale * tg2 * dk).astype(jnp.bfloat16)
    g_ref[...] += fold8((dv * vcat.astype(jnp.float32))[:, :hd] + (dv * vcat.astype(jnp.float32))[:, hd:])
    dv = (tg2 * dv).astype(jnp.bfloat16)
    pieces = 2 * acc.shape[3]
    per = slots // pieces
    krows = pl.ds(pl.multiple_of(step * per, per), per)
    vrows = pl.ds(pl.multiple_of((heads + step) * per, per), per)
    for img, lanes in ((img_b, slice(hd, 2 * hd)), (img_a, slice(0, hd))):
        par, dx = place(img)
        for j in range(pieces):
            at = slice(j * per, (j + 1) * per)
            acc[par, dx, j // (pieces // 2), j % (pieces // 2), krows] = dk[at, lanes]
            acc[par, dx, j // (pieces // 2), j % (pieces // 2), vrows] = dv[at, lanes]

    def leave(rows, i):
        lay = slice(None), slice(None), slice(None), rows
        return (
            pltpu.make_async_copy(acc.at[(1 - core,) + lay], part_other.at[lay], sems.at[3 + 2 * i]),
            pltpu.make_async_copy(acc.at[(core,) + lay], part_own.at[lay], sems.at[4 + 2 * i]),
        )

    def head_rows(h):
        return pl.ds(h * per, per), pl.ds((heads + h) * per, per)

    for h in range(KV_HEADS):

        @pl.when(step == h)
        def _():
            for i, rows in enumerate(head_rows(h)):
                for c in leave(rows, 2 * h + i):
                    c.start()

    @pl.when(step == heads - 1)
    def _():
        left = jnp.broadcast_to(jnp.sum(g_ref[...], axis=0, keepdims=True), (GROWS, hd))
        line = lax.broadcasted_iota(jnp.int32, (GROWS, hd), 0)
        digits = jnp.zeros((GROWS, hd), jnp.float32)
        for i in range(GROWS):
            unit = 4.0 ** (GTOP - i)
            d = jnp.round(left * (1.0 / unit))
            left = left - d * unit
            digits = jnp.where(line == i, d, digits)
        digits = digits.astype(jnp.bfloat16)
        g_ref[...] = jnp.broadcast_to(1.0 - tg * tg, g_ref.shape)
        for i in range(8):
            for j in range(pieces // 2):
                acc[i // 4, i // 2 % 2, i % 2, j, 2 * heads * per :] = digits
        tail = leave(pl.ds(2 * KV_HEADS * per, GROWS), 2 * KV_HEADS)
        for c in tail:
            c.start()
        for h in range(KV_HEADS):
            for i, rows in enumerate(head_rows(h)):
                for c in leave(rows, 2 * h + i):
                    c.wait()
        for c in tail:
            c.wait()
        pltpu.make_async_copy(kv, kv_out, sems.at[2]).wait()


def scores(mine, cols, folded, seg, counts, gate, q, dy, own, other):
    tokens = seg.shape[0]
    slots, width2 = 2 * own.shape[2], own.shape[3]
    hd = width2 // 2 // KV_HEADS
    block = q.shape[1] // KV_HEADS
    rows = block // hd * tokens
    smem = pl.BlockSpec(memory_space=pltpu.SMEM)
    hbm = pl.BlockSpec(memory_space=pl.ANY)
    gspec = pl.BlockSpec((8, hd), lambda i: (0, 0))
    full = pl.BlockSpec((1, slots, rows), lambda i: (i, 0, 0))
    pieces = 8 if folded else 2
    part = (2, 2, pieces // 2, 2 * KV_HEADS * (slots // pieces) + GROWS, hd)
    return pl.pallas_call(
        functools.partial(scores_kernel, mine, cols, folded),
        grid=(KV_HEADS,),
        in_specs=[
            smem,
            smem,
            smem,
            pl.BlockSpec((1, tokens), lambda i: (0, 0)),
        ]
        + [pl.BlockSpec((tokens, block), lambda i: (0, i))] * 2
        + [hbm, hbm],
        out_specs=[full, full, hbm, hbm, hbm, gspec],
        out_shape=[
            jax.ShapeDtypeStruct((KV_HEADS, slots, rows), jnp.bfloat16),
            jax.ShapeDtypeStruct((KV_HEADS, slots, rows), jnp.bfloat16),
            jax.ShapeDtypeStruct((2, slots, width2), jnp.bfloat16),
            jax.ShapeDtypeStruct(part, jnp.bfloat16),
            jax.ShapeDtypeStruct(part, jnp.bfloat16),
            jax.ShapeDtypeStruct((8, hd), jnp.float32),
        ],
        scratch_shapes=[
            pltpu.VMEM((2, slots, width2), jnp.bfloat16),
            pltpu.VMEM((2,) + part, jnp.bfloat16),
            pltpu.VMEM((rows, 2 * hd), jnp.bfloat16),
            pltpu.VMEM((rows, 2 * hd), jnp.bfloat16),
            pltpu.VMEM((2, tokens, hd), jnp.bfloat16),
            pltpu.VMEM((3, slots, 2 * tokens), jnp.float32),
            pltpu.VMEM((3, slots, 2 * tokens), jnp.float32),
            pltpu.VMEM((slots, tokens), jnp.float32),
            pltpu.SemaphoreType.DMA((5 + 4 * KV_HEADS,)),
            pltpu.SemaphoreType.DMA((KV_HEADS,)),
        ],
        compiler_params=pltpu.CompilerParams(vmem_limit_bytes=28 * 1024 * 1024),
        cost_estimate=pl.CostEstimate(
            flops=8 * KV_HEADS * rows * slots * hd * 2,
            bytes_accessed=12 * KV_HEADS * rows * slots,
            transcendentals=KV_HEADS * rows * slots,
        ),
    )(seg, counts, gate, seg.reshape(1, tokens), q, dy, own, other)


def add_up(refs, at):
    total = refs[0][at].astype(jnp.float32)
    for r in refs[1:]:
        total = total + r[at].astype(jnp.float32)
    return total


def finish_kernel(mine, gate, *refs):
    ins, (dk_ref, dv_ref, g_ref) = refs[:-3], refs[-3:]
    hd = ins[0].shape[1]
    for h in range(2 * KV_HEADS):
        out = (dk_ref, dv_ref)[h // KV_HEADS]
        lanes = slice(h % KV_HEADS * hd, (h % KV_HEADS + 1) * hd)
        out[:, lanes] = add_up(ins, slice(h * mine, (h + 1) * mine))
    digits = add_up(ins, slice(2 * KV_HEADS * mine, None))
    line = lax.broadcasted_iota(jnp.int32, digits.shape, 0)
    units = jnp.zeros(digits.shape, jnp.float32)
    for i in range(GROWS):
        units = jnp.where(line == i, 4.0 ** (GTOP - i), units)
    g_ref[0] = jnp.sum(jnp.sum(digits * units, axis=0, keepdims=True) * gate[0:1, :])


def finish(mine, gate, parts):
    hd = parts[0].shape[1]
    smem = pl.BlockSpec(memory_space=pltpu.SMEM)
    vmem = pl.BlockSpec(memory_space=pltpu.VMEM)
    full = jax.ShapeDtypeStruct((mine, KV_HEADS * hd), jnp.float32)
    return pl.pallas_call(
        functools.partial(finish_kernel, mine),
        in_specs=[vmem] + [vmem] * len(parts),
        out_specs=[vmem, vmem, smem],
        out_shape=[full, full, jax.ShapeDtypeStruct((1,), jnp.float32)],
        compiler_params=pltpu.CompilerParams(vmem_limit_bytes=4 * 1024 * 1024),
    )(gate, *parts)


def local(queries, keys, values, seg_image, tile_counts, gate, cotangent):
    f32, bf16 = jnp.float32, jnp.bfloat16
    mine, width = keys.shape
    hd = width // KV_HEADS
    cols = lax.axis_size("z")
    folded = cols == 4
    half = cols * mine

    def send_z(x, k):
        return lax.ppermute(x, "z", [(i, i ^ k) for i in range(cols)])

    def send_xy(x, p):
        return lax.ppermute(x, ("x", "y"), [(i, i ^ p) for i in range(4)])

    def send_core(x):
        return lax.ppermute(x, "core", [(0, 1), (1, 0)])

    kv = jnp.concatenate([keys, values], axis=1)
    if folded:
        near = [send_xy(kv, p) for p in (1, 2)]
        line = [send_z(kv, k) for k in LINE]
        line, near = lax.optimization_barrier((jnp.concatenate(line, axis=0), near))
        kv, line = lax.optimization_barrier((kv, line))
        block = jnp.concatenate([kv, line], axis=0)
        diag = send_xy(block, 3)
        own = [block, near[0], send_xy(line, 1), near[1], send_xy(line, 2), diag]
    else:
        line = lax.all_gather(kv, "z", axis=0, tiled=True)
        own = [line] + [send_xy(line, p) for p in PEERS]
    own = jnp.concatenate(own, axis=0).reshape(2, 2, half, 2 * width)
    other = send_core(own)
    p16, ds16, kv_used, part_own, part_other, g = scores(
        mine, cols, folded, seg_image, tile_counts, gate, queries, cotangent, own, other
    )

    got, p16 = lax.optimization_barrier((send_core(part_other), p16))
    part = (part_own.astype(f32) + got.astype(f32)).astype(bf16)
    y, dq = outputs(seg_image, gate, p16, ds16, kv_used)
    part = part.reshape((4,) + part.shape[2:])
    if folded:
        parts = [part[0, 0]] + [send_xy(part[p, 0], p) for p in PEERS]
        line = part[0, 1:].astype(f32)
        for p in PEERS:
            line = line + send_xy(part[p, 1:], p).astype(f32)
        line, y = lax.optimization_barrier((line.astype(bf16), y))
        parts += [send_z(line[k - 1], k) for k in LINE]
    else:
        line = part[0, 0].astype(f32)
        for p in PEERS:
            line = line + send_xy(part[p, 0], p).astype(f32)
        grads, gates = line[:-GROWS].reshape(2 * KV_HEADS, cols, mine, hd), line[-GROWS:]
        grads = lax.psum_scatter(grads, "z", scatter_dimension=1, tiled=True)
        parts = [jnp.concatenate([grads.reshape(-1, hd), lax.psum(gates, "z")], axis=0)]
    return (y, dq, *finish(mine, g, parts))


def solution(mesh):
    section, mp = mesh.shape["section"], mesh.shape["mp"]
    fine = Mesh(mesh.devices.reshape(section // 2, 2, mp // 2, 2), AXES)
    rows = P(AXES, None)
    return jax.shard_map(
        local,
        mesh=fine,
        in_specs=(rows, rows, rows, P(AXES), P(), P(), rows),
        out_specs=(rows, rows, rows, rows, P()),
        check_vma=False,
    )
```

```python
import functools

import jax
import jax.numpy as jnp
from jax import lax
from jax.experimental import pallas as pl
from jax.experimental.pallas import tpu as pltpu
from jax.sharding import Mesh
from jax.sharding import PartitionSpec as P

KV_HEADS = 4
TILE_TOK = 64
IMG_TOK = 256
AXES = ("x", "core", "z", "y")
NEG = -1e30
LOG2E = 1.4426950408889634
GROWS = 16
GTOP = 8
STRIP = 32
LINE = PEERS = (1, 2, 3)

NT = (((1,), (1,)), ((), ()))
NN = (((1,), (0,)), ((), ()))


def mm(a, b, dims):
    return lax.dot_general(a, b, dims, preferred_element_type=jnp.float32)


def join_kernel(k_ref, v_ref, out, sems):
    width = k_ref.shape[1]
    copies = [
        pltpu.make_async_copy(src, out.at[:, pl.ds(i * width, width)], sems.at[i])
        for i, src in enumerate((k_ref, v_ref))
    ]
    for c in copies:
        c.start()
    for c in copies:
        c.wait()


def join(keys, values):
    rows, width = keys.shape
    hbm = pl.BlockSpec(memory_space=pl.ANY)
    return pl.pallas_call(
        join_kernel,
        in_specs=[hbm, hbm],
        out_specs=hbm,
        out_shape=jax.ShapeDtypeStruct((rows, 2 * width), keys.dtype),
        scratch_shapes=[pltpu.SemaphoreType.DMA((2,))],
        compiler_params=pltpu.CompilerParams(vmem_limit_bytes=60 * 1024 * 1024),
    )(keys, values)


def outputs_kernel(seg_s, gate_s, seg_v, p16, ds16, k_ref, v_ref, y_ref, dq_ref):
    tokens = y_ref.shape[0]
    hd = k_ref.shape[2]
    span = 2 * tokens
    in_a = seg_v[...] == seg_s[0]
    in_a2 = jnp.concatenate([in_a, in_a], axis=1)
    tg2 = jnp.tanh(jnp.full((1, span), gate_s[0], jnp.float32))
    kcat_t = jnp.concatenate([k_ref[0], k_ref[1]], axis=1).T
    vcat_t = jnp.concatenate([v_ref[0], v_ref[1]], axis=1).T
    for h in range(y_ref.shape[1] // hd // 2):
        rows = slice(h * span, (h + 1) * span)
        o = mm(vcat_t, p16[0, :, rows], NN)
        o = (tg2 * jnp.where(in_a2, o[:hd], o[hd:])).astype(jnp.bfloat16)
        dq = mm(kcat_t, ds16[0, :, rows], NN)
        dq = (tg2 * (1.0 / hd**0.5) * jnp.where(in_a2, dq[:hd], dq[hd:])).astype(jnp.bfloat16)
        for j in range(2):
            feats = slice((2 * h + j) * hd, (2 * h + j + 1) * hd)
            toks = slice(j * tokens, (j + 1) * tokens)
            y_ref[:, feats] = o[:, toks].T
            dq_ref[:, feats] = dq[:, toks].T


def outputs(seg, gate, p16, ds16, kv):
    tokens = seg.shape[0]
    slots, rows = p16.shape[1:]
    hd = kv.shape[2] // 2 // KV_HEADS
    block = rows // tokens * hd
    smem = pl.BlockSpec(memory_space=pltpu.SMEM)
    full = pl.BlockSpec((1, slots, rows), lambda i: (i, 0, 0))
    cut = pl.BlockSpec((tokens, block), lambda i: (0, i))
    shape = jax.ShapeDtypeStruct((tokens, KV_HEADS * block), jnp.bfloat16)
    return pl.pallas_call(
        outputs_kernel,
        grid=(KV_HEADS,),
        in_specs=[
            smem,
            smem,
            pl.BlockSpec((1, tokens), lambda i: (0, 0)),
            full,
            full,
            pl.BlockSpec((2, slots, hd), lambda i: (0, 0, i)),
            pl.BlockSpec((2, slots, hd), lambda i: (0, 0, KV_HEADS + i)),
        ],
        out_specs=[cut, cut],
        out_shape=[shape, shape],
        compiler_params=pltpu.CompilerParams(vmem_limit_bytes=16 * 1024 * 1024),
        cost_estimate=pl.CostEstimate(flops=5 * 10**9, bytes_accessed=12 * p16.size, transcendentals=0),
    )(seg, gate, seg.reshape(1, tokens), p16, ds16, kv, kv)


def scores_kernel(
    mine,
    cols,
    folded,
    seg_s,
    cnt_s,
    gate_s,
    seg_v,
    q_ref,
    dy_ref,
    own,
    other,
    p16,
    ds16,
    kv_out,
    part_own,
    part_other,
    g_ref,
    kv,
    acc,
    qc,
    dc,
    rowsel,
    sbuf,
    dbuf,
    bias,
    sems,
    fetched,
):
    step = pl.program_id(0)
    heads = pl.num_programs(0)
    tokens = seg_v.shape[1]
    slots, width = kv.shape[1], kv.shape[2] // 2
    half = slots // 2
    hd = width // heads
    group = qc.shape[0] // tokens
    scale = 1.0 / hd**0.5
    core, xpos = lax.axis_index("core"), lax.axis_index("x")
    ypos, zpos = lax.axis_index("y"), lax.axis_index("z")
    img_a, img_b = seg_s[0], seg_s[tokens - 1]

    def place(img):
        return img % 2, (img // 2) ^ xpos

    def fetch(head, start):
        for i, img in enumerate((img_a, img_b)):
            par, dx = place(img)
            for src, mask in ((own, par == core), (other, par != core)):

                @pl.when(mask)
                def _():
                    for h in range(2):
                        for lane in (head * hd, width + head * hd):
                            lanes = pl.ds(lane, hd)
                            c = pltpu.make_async_copy(
                                src.at[dx, h, :, lanes],
                                kv.at[i, pl.ds(h * half, half), lanes],
                                fetched.at[head],
                            )
                            c.start() if start else c.wait()

    in_a = seg_v[...] == img_a
    tg = jnp.tanh(jnp.full((1, hd), gate_s[0], jnp.float32))

    @pl.when(step == 0)
    def _():
        for h in range(KV_HEADS):
            fetch(h, True)
        acc[...] = jnp.zeros_like(acc)
        g_ref[...] = jnp.zeros_like(g_ref)
        n = lax.broadcasted_iota(jnp.int32, (slots, tokens), 0)
        z, y = n // mine % cols, (n // half) ^ ypos
        if folded:
            z = z ^ zpos
        tile = (z * (2 * mine) + y * mine + n % mine) // TILE_TOK
        bias[...] = jnp.where(tile < jnp.where(in_a, cnt_s[img_a], cnt_s[img_b]), 0.0, NEG)
        side_a = jnp.broadcast_to(in_a.astype(jnp.float32), (hd, tokens)).T
        rowsel[0] = side_a.astype(jnp.bfloat16)
        rowsel[1] = (1.0 - side_a).astype(jnp.bfloat16)
    for h in range(KV_HEADS):

        @pl.when(step == h)
        def _():
            fetch(h, False)

    @pl.when(step == heads - 1)
    def _():
        pltpu.make_async_copy(kv, kv_out, sems.at[2]).start()

    kcols = pl.ds(pl.multiple_of(step * hd, hd), hd)
    vcols = pl.ds(pl.multiple_of(width + step * hd, hd), hd)
    kcat = jnp.concatenate([kv[0, :, kcols], kv[1, :, kcols]], axis=1)
    vcat = jnp.concatenate([kv[0, :, vcols], kv[1, :, vcols]], axis=1)
    for g in range(group):
        feats = slice(g * hd, (g + 1) * hd)
        rows = slice(g * tokens, (g + 1) * tokens)
        q, dy = q_ref[:, feats], dy_ref[:, feats]
        for i in range(2):
            side = slice(i * hd, (i + 1) * hd)
            qc[rows, side] = q * rowsel[i]
            dc[rows, side] = dy * rowsel[i]

    span = 2 * tokens
    blocks = group // 2
    strips = [slice(i, i + STRIP) for i in range(0, slots, STRIP)]
    tg2 = jnp.concatenate([tg, tg], axis=1)

    def fold8(x):
        return jnp.sum(x.reshape(x.shape[0] // 8, 8, x.shape[1]), axis=0)

    def slot_grads(lo, hi):
        rows = slice(lo * span, hi * span)
        return mm(ds16[0, :, rows], qc[rows, :], NN), mm(p16[0, :, rows], dc[rows, :], NN)

    dk = dv = 0.0
    tops, invs, deltas = {}, {}, {}
    for t in range(blocks + 2):
        new, mid, old = t, t - 1, t - 2
        if new < blocks:
            rows = slice(new * span, (new + 1) * span)
            s = mm(kcat, qc[rows, :], NT)
            dbuf[new % 3] = mm(vcat, dc[rows, :], NT)
            top = jnp.full((8, span), NEG, jnp.float32)
        norm = dots = jnp.zeros((8, span), jnp.float32)
        for strip in strips:
            if old >= 0:
                rows = slice(old * span, (old + 1) * span)
                p = sbuf[old % 3, strip] * invs[old]
                p16[0, strip, rows] = p.astype(jnp.bfloat16)
                ds16[0, strip, rows] = (p * (dbuf[old % 3, strip] - deltas[old])).astype(jnp.bfloat16)
            if 0 <= mid < blocks:
                e = jnp.exp2(sbuf[mid % 3, strip] * (scale * LOG2E) - tops[mid])
                sbuf[mid % 3, strip] = e
                norm = norm + fold8(e)
                dots = dots + fold8(e * dbuf[mid % 3, strip])
            if new < blocks:
                x = s[strip] + jnp.concatenate([bias[strip], bias[strip]], axis=1)
                sbuf[new % 3, strip] = x
                top = jnp.maximum(top, jnp.max(x.reshape(STRIP // 8, 8, span), axis=0))
        if new < blocks:
            tops[new] = jnp.max(top, axis=0, keepdims=True) * (scale * LOG2E)
        if 0 <= mid < blocks:
            invs[mid] = 1.0 / jnp.sum(norm, axis=0, keepdims=True)
            deltas[mid] = invs[mid] * jnp.sum(dots, axis=0, keepdims=True)
        if old >= 0 and old % 2:
            more = slot_grads(old - 1, old + 1)
            dk, dv = dk + more[0], dv + more[1]
    dk = (scale * tg2 * dk).astype(jnp.bfloat16)
    g_ref[...] += fold8((dv * vcat.astype(jnp.float32))[:, :hd] + (dv * vcat.astype(jnp.float32))[:, hd:])
    dv = (tg2 * dv).astype(jnp.bfloat16)
    pieces = 2 * acc.shape[3]
    per = slots // pieces
    krows = pl.ds(pl.multiple_of(step * per, per), per)
    vrows = pl.ds(pl.multiple_of((heads + step) * per, per), per)
    for img, lanes in ((img_b, slice(hd, 2 * hd)), (img_a, slice(0, hd))):
        par, dx = place(img)
        for j in range(pieces):
            at = slice(j * per, (j + 1) * per)
            acc[par, dx, j // (pieces // 2), j % (pieces // 2), krows] = dk[at, lanes]
            acc[par, dx, j // (pieces // 2), j % (pieces // 2), vrows] = dv[at, lanes]

    def leave(rows, i):
        lay = slice(None), slice(None), slice(None), rows
        return (
            pltpu.make_async_copy(acc.at[(1 - core,) + lay], part_other.at[lay], sems.at[3 + 2 * i]),
            pltpu.make_async_copy(acc.at[(core,) + lay], part_own.at[lay], sems.at[4 + 2 * i]),
        )

    def head_rows(h):
        return pl.ds(h * per, per), pl.ds((heads + h) * per, per)

    for h in range(KV_HEADS):

        @pl.when(step == h)
        def _():
            for i, rows in enumerate(head_rows(h)):
                for c in leave(rows, 2 * h + i):
                    c.start()

    @pl.when(step == heads - 1)
    def _():
        left = jnp.broadcast_to(jnp.sum(g_ref[...], axis=0, keepdims=True), (GROWS, hd))
        line = lax.broadcasted_iota(jnp.int32, (GROWS, hd), 0)
        digits = jnp.zeros((GROWS, hd), jnp.float32)
        for i in range(GROWS):
            unit = 4.0 ** (GTOP - i)
            d = jnp.round(left * (1.0 / unit))
            left = left - d * unit
            digits = jnp.where(line == i, d, digits)
        digits = digits.astype(jnp.bfloat16)
        g_ref[...] = jnp.broadcast_to(1.0 - tg * tg, g_ref.shape)
        for i in range(8):
            for j in range(pieces // 2):
                acc[i // 4, i // 2 % 2, i % 2, j, 2 * heads * per :] = digits
        tail = leave(pl.ds(2 * KV_HEADS * per, GROWS), 2 * KV_HEADS)
        for c in tail:
            c.start()
        for h in range(KV_HEADS):
            for i, rows in enumerate(head_rows(h)):
                for c in leave(rows, 2 * h + i):
                    c.wait()
        for c in tail:
            c.wait()
        pltpu.make_async_copy(kv, kv_out, sems.at[2]).wait()


def scores(mine, cols, folded, seg, counts, gate, q, dy, own, other):
    tokens = seg.shape[0]
    slots, width2 = 2 * own.shape[2], own.shape[3]
    hd = width2 // 2 // KV_HEADS
    block = q.shape[1] // KV_HEADS
    rows = block // hd * tokens
    smem = pl.BlockSpec(memory_space=pltpu.SMEM)
    hbm = pl.BlockSpec(memory_space=pl.ANY)
    gspec = pl.BlockSpec((8, hd), lambda i: (0, 0))
    full = pl.BlockSpec((1, slots, rows), lambda i: (i, 0, 0))
    pieces = 8 if folded else 2
    part = (2, 2, pieces // 2, 2 * KV_HEADS * (slots // pieces) + GROWS, hd)
    return pl.pallas_call(
        functools.partial(scores_kernel, mine, cols, folded),
        grid=(KV_HEADS,),
        in_specs=[
            smem,
            smem,
            smem,
            pl.BlockSpec((1, tokens), lambda i: (0, 0)),
        ]
        + [pl.BlockSpec((tokens, block), lambda i: (0, i))] * 2
        + [hbm, hbm],
        out_specs=[full, full, hbm, hbm, hbm, gspec],
        out_shape=[
            jax.ShapeDtypeStruct((KV_HEADS, slots, rows), jnp.bfloat16),
            jax.ShapeDtypeStruct((KV_HEADS, slots, rows), jnp.bfloat16),
            jax.ShapeDtypeStruct((2, slots, width2), jnp.bfloat16),
            jax.ShapeDtypeStruct(part, jnp.bfloat16),
            jax.ShapeDtypeStruct(part, jnp.bfloat16),
            jax.ShapeDtypeStruct((8, hd), jnp.float32),
        ],
        scratch_shapes=[
            pltpu.VMEM((2, slots, width2), jnp.bfloat16),
            pltpu.VMEM((2,) + part, jnp.bfloat16),
            pltpu.VMEM((rows, 2 * hd), jnp.bfloat16),
            pltpu.VMEM((rows, 2 * hd), jnp.bfloat16),
            pltpu.VMEM((2, tokens, hd), jnp.bfloat16),
            pltpu.VMEM((3, slots, 2 * tokens), jnp.float32),
            pltpu.VMEM((3, slots, 2 * tokens), jnp.float32),
            pltpu.VMEM((slots, tokens), jnp.float32),
            pltpu.SemaphoreType.DMA((5 + 4 * KV_HEADS,)),
            pltpu.SemaphoreType.DMA((KV_HEADS,)),
        ],
        compiler_params=pltpu.CompilerParams(vmem_limit_bytes=28 * 1024 * 1024),
        cost_estimate=pl.CostEstimate(
            flops=8 * KV_HEADS * rows * slots * hd * 2,
            bytes_accessed=12 * KV_HEADS * rows * slots,
            transcendentals=KV_HEADS * rows * slots,
        ),
    )(seg, counts, gate, seg.reshape(1, tokens), q, dy, own, other)


def add_up(refs, at):
    total = refs[0][at].astype(jnp.float32)
    for r in refs[1:]:
        total = total + r[at].astype(jnp.float32)
    return total


def finish_kernel(mine, gate, *refs):
    ins, (dk_ref, dv_ref, g_ref) = refs[:-3], refs[-3:]
    hd = ins[0].shape[1]
    for h in range(2 * KV_HEADS):
        out = (dk_ref, dv_ref)[h // KV_HEADS]
        lanes = slice(h % KV_HEADS * hd, (h % KV_HEADS + 1) * hd)
        out[:, lanes] = add_up(ins, slice(h * mine, (h + 1) * mine))
    digits = add_up(ins, slice(2 * KV_HEADS * mine, None))
    line = lax.broadcasted_iota(jnp.int32, digits.shape, 0)
    units = jnp.zeros(digits.shape, jnp.float32)
    for i in range(GROWS):
        units = jnp.where(line == i, 4.0 ** (GTOP - i), units)
    g_ref[0] = jnp.sum(jnp.sum(digits * units, axis=0, keepdims=True) * gate[0:1, :])


def finish(mine, gate, parts):
    hd = parts[0].shape[1]
    smem = pl.BlockSpec(memory_space=pltpu.SMEM)
    vmem = pl.BlockSpec(memory_space=pltpu.VMEM)
    full = jax.ShapeDtypeStruct((mine, KV_HEADS * hd), jnp.float32)
    return pl.pallas_call(
        functools.partial(finish_kernel, mine),
        in_specs=[vmem] + [vmem] * len(parts),
        out_specs=[vmem, vmem, smem],
        out_shape=[full, full, jax.ShapeDtypeStruct((1,), jnp.float32)],
        compiler_params=pltpu.CompilerParams(vmem_limit_bytes=4 * 1024 * 1024),
    )(gate, *parts)


def local(queries, keys, values, seg_image, tile_counts, gate, cotangent):
    f32, bf16 = jnp.float32, jnp.bfloat16
    mine, width = keys.shape
    hd = width // KV_HEADS
    cols = lax.axis_size("z")
    folded = cols == 4
    half = cols * mine

    def send_z(x, k):
        return lax.ppermute(x, "z", [(i, i ^ k) for i in range(cols)])

    def send_xy(x, p):
        return lax.ppermute(x, ("x", "y"), [(i, i ^ p) for i in range(4)])

    def send_core(x):
        return lax.ppermute(x, "core", [(0, 1), (1, 0)])

    kv = join(keys, values) if folded else jnp.concatenate([keys, values], axis=1)
    if folded:
        near = [send_xy(kv, p) for p in (1, 2)]
        line = [send_z(kv, k) for k in LINE]
        line, near = lax.optimization_barrier((jnp.concatenate(line, axis=0), near))
        kv, line = lax.optimization_barrier((kv, line))
        block = jnp.concatenate([kv, line], axis=0)
        diag = send_xy(block, 3)
        own = [block, near[0], send_xy(line, 1), near[1], send_xy(line, 2), diag]
    else:
        line = lax.all_gather(kv, "z", axis=0, tiled=True)
        own = [line] + [send_xy(line, p) for p in PEERS]
    own = jnp.concatenate(own, axis=0).reshape(2, 2, half, 2 * width)
    other = send_core(own)
    p16, ds16, kv_used, part_own, part_other, g = scores(
        mine, cols, folded, seg_image, tile_counts, gate, queries, cotangent, own, other
    )

    got, p16 = lax.optimization_barrier((send_core(part_other), p16))
    part = (part_own.astype(f32) + got.astype(f32)).astype(bf16)
    y, dq = outputs(seg_image, gate, p16, ds16, kv_used)
    part = part.reshape((4,) + part.shape[2:])
    if folded:
        parts = [part[0, 0]] + [send_xy(part[p, 0], p) for p in PEERS]
        line = part[0, 1:].astype(f32)
        for p in PEERS:
            line = line + send_xy(part[p, 1:], p).astype(f32)
        line, y = lax.optimization_barrier((line.astype(bf16), y))
        parts += [send_z(line[k - 1], k) for k in LINE]
    else:
        line = part[0, 0].astype(f32)
        for p in PEERS:
            line = line + send_xy(part[p, 0], p).astype(f32)
        grads, gates = line[:-GROWS].reshape(2 * KV_HEADS, cols, mine, hd), line[-GROWS:]
        grads = lax.psum_scatter(grads, "z", scatter_dimension=1, tiled=True)
        parts = [jnp.concatenate([grads.reshape(-1, hd), lax.psum(gates, "z")], axis=0)]
    return (y, dq, *finish(mine, g, parts))


def solution(mesh):
    section, mp = mesh.shape["section"], mesh.shape["mp"]
    fine = Mesh(mesh.devices.reshape(section // 2, 2, mp // 2, 2), AXES)
    rows = P(AXES, None)
    return jax.shard_map(
        local,
        mesh=fine,
        in_specs=(rows, rows, rows, P(AXES), P(), P(), rows),
        out_specs=(rows, rows, rows, rows, P()),
        check_vma=False,
    )
```

```python
import functools

import jax
import jax.numpy as jnp
from jax import lax
from jax.experimental import pallas as pl
from jax.experimental.pallas import tpu as pltpu
from jax.sharding import Mesh
from jax.sharding import PartitionSpec as P

KV_HEADS = 4
TILE_TOK = 64
IMG_TOK = 256
AXES = ("x", "core", "z", "y")
NEG = -1e30
LOG2E = 1.4426950408889634
GROWS = 16
GTOP = 8
STRIP = 32
LINE = PEERS = (1, 2, 3)

NT = (((1,), (1,)), ((), ()))
NN = (((1,), (0,)), ((), ()))


def mm(a, b, dims):
    return lax.dot_general(a, b, dims, preferred_element_type=jnp.float32)


def outputs_kernel(seg_s, gate_s, seg_v, p16, ds16, k_ref, v_ref, y_ref, dq_ref):
    tokens = y_ref.shape[0]
    hd = k_ref.shape[2]
    span = 2 * tokens
    in_a = seg_v[...] == seg_s[0]
    in_a2 = jnp.concatenate([in_a, in_a], axis=1)
    tg2 = jnp.tanh(jnp.full((1, span), gate_s[0], jnp.float32))
    kcat_t = jnp.concatenate([k_ref[0], k_ref[1]], axis=1).T
    vcat_t = jnp.concatenate([v_ref[0], v_ref[1]], axis=1).T
    for h in range(y_ref.shape[1] // hd // 2):
        rows = slice(h * span, (h + 1) * span)
        o = mm(vcat_t, p16[0, :, rows], NN)
        o = (tg2 * jnp.where(in_a2, o[:hd], o[hd:])).astype(jnp.bfloat16)
        dq = mm(kcat_t, ds16[0, :, rows], NN)
        dq = (tg2 * (1.0 / hd**0.5) * jnp.where(in_a2, dq[:hd], dq[hd:])).astype(jnp.bfloat16)
        for j in range(2):
            feats = slice((2 * h + j) * hd, (2 * h + j + 1) * hd)
            toks = slice(j * tokens, (j + 1) * tokens)
            y_ref[:, feats] = o[:, toks].T
            dq_ref[:, feats] = dq[:, toks].T


def outputs(seg, gate, p16, ds16, kv):
    tokens = seg.shape[0]
    slots, rows = p16.shape[1:]
    hd = kv.shape[2] // 2 // KV_HEADS
    block = rows // tokens * hd
    smem = pl.BlockSpec(memory_space=pltpu.SMEM)
    full = pl.BlockSpec((1, slots, rows), lambda i: (i, 0, 0))
    cut = pl.BlockSpec((tokens, block), lambda i: (0, i))
    shape = jax.ShapeDtypeStruct((tokens, KV_HEADS * block), jnp.bfloat16)
    return pl.pallas_call(
        outputs_kernel,
        grid=(KV_HEADS,),
        in_specs=[
            smem,
            smem,
            pl.BlockSpec((1, tokens), lambda i: (0, 0)),
            full,
            full,
            pl.BlockSpec((2, slots, hd), lambda i: (0, 0, i)),
            pl.BlockSpec((2, slots, hd), lambda i: (0, 0, KV_HEADS + i)),
        ],
        out_specs=[cut, cut],
        out_shape=[shape, shape],
        compiler_params=pltpu.CompilerParams(vmem_limit_bytes=16 * 1024 * 1024),
        cost_estimate=pl.CostEstimate(flops=5 * 10**9, bytes_accessed=12 * p16.size, transcendentals=0),
    )(seg, gate, seg.reshape(1, tokens), p16, ds16, kv, kv)


def scores_kernel(
    mine,
    cols,
    folded,
    seg_s,
    cnt_s,
    gate_s,
    seg_v,
    q_ref,
    dy_ref,
    own,
    other,
    p16,
    ds16,
    kv_out,
    part_own,
    part_other,
    g_ref,
    kv,
    acc,
    qc,
    dc,
    rowsel,
    sbuf,
    dbuf,
    bias,
    sems,
    fetched,
):
    step = pl.program_id(0)
    heads = pl.num_programs(0)
    tokens = seg_v.shape[1]
    slots, width = kv.shape[1], kv.shape[2] // 2
    half = slots // 2
    hd = width // heads
    group = qc.shape[0] // tokens
    scale = 1.0 / hd**0.5
    core, xpos = lax.axis_index("core"), lax.axis_index("x")
    ypos, zpos = lax.axis_index("y"), lax.axis_index("z")
    img_a, img_b = seg_s[0], seg_s[tokens - 1]

    def place(img):
        return img % 2, (img // 2) ^ xpos

    def fetch(head, start):
        for i, img in enumerate((img_a, img_b)):
            par, dx = place(img)
            for src, mask in ((own, par == core), (other, par != core)):

                @pl.when(mask)
                def _():
                    for h in range(2):
                        for lane in (head * hd, width + head * hd):
                            lanes = pl.ds(lane, hd)
                            c = pltpu.make_async_copy(
                                src.at[dx, h, :, lanes],
                                kv.at[i, pl.ds(h * half, half), lanes],
                                fetched.at[head],
                            )
                            c.start() if start else c.wait()

    in_a = seg_v[...] == img_a
    tg = jnp.tanh(jnp.full((1, hd), gate_s[0], jnp.float32))

    @pl.when(step == 0)
    def _():
        for h in range(KV_HEADS):
            fetch(h, True)
        acc[...] = jnp.zeros_like(acc)
        g_ref[...] = jnp.zeros_like(g_ref)
        n = lax.broadcasted_iota(jnp.int32, (slots, tokens), 0)
        z, y = n // mine % cols, (n // half) ^ ypos
        if folded:
            z = z ^ zpos
        tile = (z * (2 * mine) + y * mine + n % mine) // TILE_TOK
        bias[...] = jnp.where(tile < jnp.where(in_a, cnt_s[img_a], cnt_s[img_b]), 0.0, NEG)
        side_a = jnp.broadcast_to(in_a.astype(jnp.float32), (hd, tokens)).T
        rowsel[0] = side_a.astype(jnp.bfloat16)
        rowsel[1] = (1.0 - side_a).astype(jnp.bfloat16)
    for h in range(KV_HEADS):

        @pl.when(step == h)
        def _():
            fetch(h, False)

    @pl.when(step == heads - 1)
    def _():
        pltpu.make_async_copy(kv, kv_out, sems.at[2]).start()

    kcols = pl.ds(pl.multiple_of(step * hd, hd), hd)
    vcols = pl.ds(pl.multiple_of(width + step * hd, hd), hd)
    kcat = jnp.concatenate([kv[0, :, kcols], kv[1, :, kcols]], axis=1)
    vcat = jnp.concatenate([kv[0, :, vcols], kv[1, :, vcols]], axis=1)
    for g in range(group):
        feats = slice(g * hd, (g + 1) * hd)
        rows = slice(g * tokens, (g + 1) * tokens)
        q, dy = q_ref[:, feats], dy_ref[:, feats]
        for i in range(2):
            side = slice(i * hd, (i + 1) * hd)
            qc[rows, side] = q * rowsel[i]
            dc[rows, side] = dy * rowsel[i]

    span = 2 * tokens
    blocks = group // 2
    strips = [slice(i, i + STRIP) for i in range(0, slots, STRIP)]
    tg2 = jnp.concatenate([tg, tg], axis=1)

    def fold8(x):
        return jnp.sum(x.reshape(x.shape[0] // 8, 8, x.shape[1]), axis=0)

    def slot_grads(lo, hi):
        rows = slice(lo * span, hi * span)
        return mm(ds16[0, :, rows], qc[rows, :], NN), mm(p16[0, :, rows], dc[rows, :], NN)

    dk = dv = 0.0
    tops, invs, deltas = {}, {}, {}
    for t in range(blocks + 2):
        new, mid, old = t, t - 1, t - 2
        if new < blocks:
            rows = slice(new * span, (new + 1) * span)
            s = mm(kcat, qc[rows, :], NT)
            dbuf[new % 3] = mm(vcat, dc[rows, :], NT)
            top = jnp.full((8, span), NEG, jnp.float32)
        norm = dots = jnp.zeros((8, span), jnp.float32)
        for strip in strips:
            if old >= 0:
                rows = slice(old * span, (old + 1) * span)
                p = sbuf[old % 3, strip] * invs[old]
                p16[0, strip, rows] = p.astype(jnp.bfloat16)
                ds16[0, strip, rows] = (p * (dbuf[old % 3, strip] - deltas[old])).astype(jnp.bfloat16)
            if 0 <= mid < blocks:
                e = jnp.exp2(sbuf[mid % 3, strip] * (scale * LOG2E) - tops[mid])
                sbuf[mid % 3, strip] = e
                norm = norm + fold8(e)
                dots = dots + fold8(e * dbuf[mid % 3, strip])
            if new < blocks:
                x = s[strip] + jnp.concatenate([bias[strip], bias[strip]], axis=1)
                sbuf[new % 3, strip] = x
                top = jnp.maximum(top, jnp.max(x.reshape(STRIP // 8, 8, span), axis=0))
        if new < blocks:
            tops[new] = jnp.max(top, axis=0, keepdims=True) * (scale * LOG2E)
        if 0 <= mid < blocks:
            invs[mid] = 1.0 / jnp.sum(norm, axis=0, keepdims=True)
            deltas[mid] = invs[mid] * jnp.sum(dots, axis=0, keepdims=True)
        if old >= 0 and old % 2:
            more = slot_grads(old - 1, old + 1)
            dk, dv = dk + more[0], dv + more[1]
    dk = (scale * tg2 * dk).astype(jnp.bfloat16)
    g_ref[...] += fold8((dv * vcat.astype(jnp.float32))[:, :hd] + (dv * vcat.astype(jnp.float32))[:, hd:])
    dv = (tg2 * dv).astype(jnp.bfloat16)
    pieces = 2 * acc.shape[3]
    per = slots // pieces
    krows = pl.ds(pl.multiple_of(step * per, per), per)
    vrows = pl.ds(pl.multiple_of((heads + step) * per, per), per)
    for img, lanes in ((img_b, slice(hd, 2 * hd)), (img_a, slice(0, hd))):
        par, dx = place(img)
        for j in range(pieces):
            at = slice(j * per, (j + 1) * per)
            acc[par, dx, j // (pieces // 2), j % (pieces // 2), krows] = dk[at, lanes]
            acc[par, dx, j // (pieces // 2), j % (pieces // 2), vrows] = dv[at, lanes]

    def leave(rows, i):
        lay = slice(None), slice(None), slice(None), rows
        return (
            pltpu.make_async_copy(acc.at[(1 - core,) + lay], part_other.at[lay], sems.at[3 + 2 * i]),
            pltpu.make_async_copy(acc.at[(core,) + lay], part_own.at[lay], sems.at[4 + 2 * i]),
        )

    def head_rows(h):
        return pl.ds(h * per, per), pl.ds((heads + h) * per, per)

    for h in range(KV_HEADS):

        @pl.when(step == h)
        def _():
            for i, rows in enumerate(head_rows(h)):
                for c in leave(rows, 2 * h + i):
                    c.start()

    @pl.when(step == heads - 1)
    def _():
        left = jnp.broadcast_to(jnp.sum(g_ref[...], axis=0, keepdims=True), (GROWS, hd))
        line = lax.broadcasted_iota(jnp.int32, (GROWS, hd), 0)
        digits = jnp.zeros((GROWS, hd), jnp.float32)
        for i in range(GROWS):
            unit = 4.0 ** (GTOP - i)
            d = jnp.round(left * (1.0 / unit))
            left = left - d * unit
            digits = jnp.where(line == i, d, digits)
        digits = digits.astype(jnp.bfloat16)
        g_ref[...] = jnp.broadcast_to(1.0 - tg * tg, g_ref.shape)
        for i in range(8):
            for j in range(pieces // 2):
                acc[i // 4, i // 2 % 2, i % 2, j, 2 * heads * per :] = digits
        tail = leave(pl.ds(2 * KV_HEADS * per, GROWS), 2 * KV_HEADS)
        for c in tail:
            c.start()
        for h in range(KV_HEADS):
            for i, rows in enumerate(head_rows(h)):
                for c in leave(rows, 2 * h + i):
                    c.wait()
        for c in tail:
            c.wait()
        pltpu.make_async_copy(kv, kv_out, sems.at[2]).wait()


def scores(mine, cols, folded, seg, counts, gate, q, dy, own, other):
    tokens = seg.shape[0]
    slots, width2 = 2 * own.shape[2], own.shape[3]
    hd = width2 // 2 // KV_HEADS
    block = q.shape[1] // KV_HEADS
    rows = block // hd * tokens
    smem = pl.BlockSpec(memory_space=pltpu.SMEM)
    hbm = pl.BlockSpec(memory_space=pl.ANY)
    gspec = pl.BlockSpec((8, hd), lambda i: (0, 0))
    full = pl.BlockSpec((1, slots, rows), lambda i: (i, 0, 0))
    pieces = 8 if folded else 2
    part = (2, 2, pieces // 2, 2 * KV_HEADS * (slots // pieces) + GROWS, hd)
    return pl.pallas_call(
        functools.partial(scores_kernel, mine, cols, folded),
        grid=(KV_HEADS,),
        in_specs=[
            smem,
            smem,
            smem,
            pl.BlockSpec((1, tokens), lambda i: (0, 0)),
        ]
        + [pl.BlockSpec((tokens, block), lambda i: (0, i))] * 2
        + [hbm, hbm],
        out_specs=[full, full, hbm, hbm, hbm, gspec],
        out_shape=[
            jax.ShapeDtypeStruct((KV_HEADS, slots, rows), jnp.bfloat16),
            jax.ShapeDtypeStruct((KV_HEADS, slots, rows), jnp.bfloat16),
            jax.ShapeDtypeStruct((2, slots, width2), jnp.bfloat16),
            jax.ShapeDtypeStruct(part, jnp.bfloat16),
            jax.ShapeDtypeStruct(part, jnp.bfloat16),
            jax.ShapeDtypeStruct((8, hd), jnp.float32),
        ],
        scratch_shapes=[
            pltpu.VMEM((2, slots, width2), jnp.bfloat16),
            pltpu.VMEM((2,) + part, jnp.bfloat16),
            pltpu.VMEM((rows, 2 * hd), jnp.bfloat16),
            pltpu.VMEM((rows, 2 * hd), jnp.bfloat16),
            pltpu.VMEM((2, tokens, hd), jnp.bfloat16),
            pltpu.VMEM((3, slots, 2 * tokens), jnp.float32),
            pltpu.VMEM((3, slots, 2 * tokens), jnp.float32),
            pltpu.VMEM((slots, tokens), jnp.float32),
            pltpu.SemaphoreType.DMA((5 + 4 * KV_HEADS,)),
            pltpu.SemaphoreType.DMA((KV_HEADS,)),
        ],
        compiler_params=pltpu.CompilerParams(vmem_limit_bytes=28 * 1024 * 1024),
        cost_estimate=pl.CostEstimate(
            flops=8 * KV_HEADS * rows * slots * hd * 2,
            bytes_accessed=12 * KV_HEADS * rows * slots,
            transcendentals=KV_HEADS * rows * slots,
        ),
    )(seg, counts, gate, seg.reshape(1, tokens), q, dy, own, other)


def add_up(refs, at):
    total = refs[0][at].astype(jnp.float32)
    for r in refs[1:]:
        total = total + r[at].astype(jnp.float32)
    return total


def finish_kernel(mine, gate, *refs):
    ins, (dk_ref, dv_ref, g_ref) = refs[:-3], refs[-3:]
    hd = ins[0].shape[1]
    for h in range(2 * KV_HEADS):
        out = (dk_ref, dv_ref)[h // KV_HEADS]
        lanes = slice(h % KV_HEADS * hd, (h % KV_HEADS + 1) * hd)
        out[:, lanes] = add_up(ins, slice(h * mine, (h + 1) * mine))
    digits = add_up(ins, slice(2 * KV_HEADS * mine, None))
    line = lax.broadcasted_iota(jnp.int32, digits.shape, 0)
    units = jnp.zeros(digits.shape, jnp.float32)
    for i in range(GROWS):
        units = jnp.where(line == i, 4.0 ** (GTOP - i), units)
    g_ref[0] = jnp.sum(jnp.sum(digits * units, axis=0, keepdims=True) * gate[0:1, :])


def finish(mine, gate, parts):
    hd = parts[0].shape[1]
    smem = pl.BlockSpec(memory_space=pltpu.SMEM)
    vmem = pl.BlockSpec(memory_space=pltpu.VMEM)
    full = jax.ShapeDtypeStruct((mine, KV_HEADS * hd), jnp.float32)
    return pl.pallas_call(
        functools.partial(finish_kernel, mine),
        in_specs=[vmem] + [vmem] * len(parts),
        out_specs=[vmem, vmem, smem],
        out_shape=[full, full, jax.ShapeDtypeStruct((1,), jnp.float32)],
        compiler_params=pltpu.CompilerParams(vmem_limit_bytes=4 * 1024 * 1024),
    )(gate, *parts)


def local(queries, keys, values, seg_image, tile_counts, gate, cotangent):
    f32, bf16 = jnp.float32, jnp.bfloat16
    mine, width = keys.shape
    hd = width // KV_HEADS
    cols = lax.axis_size("z")
    folded = cols == 4
    half = cols * mine

    def send_z(x, k):
        return lax.ppermute(x, "z", [(i, i ^ k) for i in range(cols)])

    def send_xy(x, p):
        return lax.ppermute(x, ("x", "y"), [(i, i ^ p) for i in range(4)])

    def send_core(x):
        return lax.ppermute(x, "core", [(0, 1), (1, 0)])

    kv = jnp.concatenate([keys, values], axis=1)
    if folded:
        near = [send_xy(kv, p) for p in (1, 2)]
        line = [send_z(kv, k) for k in LINE]
        line, near = lax.optimization_barrier((jnp.concatenate(line, axis=0), near))
        kv, line = lax.optimization_barrier((kv, line))
        block = jnp.concatenate([kv, line], axis=0)
        diag = send_xy(block, 3)
        own = [block, near[0], send_xy(line, 1), near[1], send_xy(line, 2), diag]
    else:
        line = lax.all_gather(kv, "z", axis=0, tiled=True)
        own = [line] + [send_xy(line, p) for p in PEERS]
    own = jnp.concatenate(own, axis=0).reshape(2, 2, half, 2 * width)
    other = send_core(own)
    p16, ds16, kv_used, part_own, part_other, g = scores(
        mine, cols, folded, seg_image, tile_counts, gate, queries, cotangent, own, other
    )

    got, p16 = lax.optimization_barrier((send_core(part_other), p16))
    part = (part_own.astype(f32) + got.astype(f32)).astype(bf16)
    y, dq = outputs(seg_image, gate, p16, ds16, kv_used)
    part = part.reshape((4,) + part.shape[2:])
    if folded:
        parts = [part[0, 0]] + [send_xy(part[p, 0], p) for p in PEERS]
        line = part[0, 1:].astype(f32)
        for p in PEERS:
            line = line + send_xy(part[p, 1:], p).astype(f32)
        line, y = lax.optimization_barrier((line.astype(bf16), y))
        parts += [send_z(line[k - 1], k) for k in LINE[::-1]]
    else:
        line = part[0, 0].astype(f32)
        for p in PEERS:
            line = line + send_xy(part[p, 0], p).astype(f32)
        grads, gates = line[:-GROWS].reshape(2 * KV_HEADS, cols, mine, hd), line[-GROWS:]
        grads = lax.psum_scatter(grads, "z", scatter_dimension=1, tiled=True)
        parts = [jnp.concatenate([grads.reshape(-1, hd), lax.psum(gates, "z")], axis=0)]
    return (y, dq, *finish(mine, g, parts))


def solution(mesh):
    section, mp = mesh.shape["section"], mesh.shape["mp"]
    fine = Mesh(mesh.devices.reshape(section // 2, 2, mp // 2, 2), AXES)
    rows = P(AXES, None)
    return jax.shard_map(
        local,
        mesh=fine,
        in_specs=(rows, rows, rows, P(AXES), P(), P(), rows),
        out_specs=(rows, rows, rows, rows, P()),
        check_vma=False,
    )
```

```python
import functools

import jax
import jax.numpy as jnp
from jax import lax
from jax.experimental import pallas as pl
from jax.experimental.pallas import tpu as pltpu
from jax.sharding import Mesh
from jax.sharding import PartitionSpec as P

KV_HEADS = 4
TILE_TOK = 64
IMG_TOK = 256
AXES = ("x", "core", "z", "y")
NEG = -1e30
LOG2E = 1.4426950408889634
GROWS = 16
GTOP = 8
STRIP = 32
LINE = PEERS = (1, 2, 3)

NT = (((1,), (1,)), ((), ()))
NN = (((1,), (0,)), ((), ()))


def mm(a, b, dims):
    return lax.dot_general(a, b, dims, preferred_element_type=jnp.float32)


def outputs_kernel(seg_s, gate_s, seg_v, p16, ds16, k_ref, v_ref, y_ref, dq_ref):
    tokens = y_ref.shape[0]
    hd = k_ref.shape[2]
    span = 2 * tokens
    in_a = seg_v[...] == seg_s[0]
    in_a2 = jnp.concatenate([in_a, in_a], axis=1)
    tg2 = jnp.tanh(jnp.full((1, span), gate_s[0], jnp.float32))
    kcat_t = jnp.concatenate([k_ref[0], k_ref[1]], axis=1).T
    vcat_t = jnp.concatenate([v_ref[0], v_ref[1]], axis=1).T
    for h in range(y_ref.shape[1] // hd // 2):
        rows = slice(h * span, (h + 1) * span)
        o = mm(vcat_t, p16[0, :, rows], NN)
        o = (tg2 * jnp.where(in_a2, o[:hd], o[hd:])).astype(jnp.bfloat16)
        dq = mm(kcat_t, ds16[0, :, rows], NN)
        dq = (tg2 * (1.0 / hd**0.5) * jnp.where(in_a2, dq[:hd], dq[hd:])).astype(jnp.bfloat16)
        for j in range(2):
            feats = slice((2 * h + j) * hd, (2 * h + j + 1) * hd)
            toks = slice(j * tokens, (j + 1) * tokens)
            y_ref[:, feats] = o[:, toks].T
            dq_ref[:, feats] = dq[:, toks].T


def outputs(seg, gate, p16, ds16, kv):
    tokens = seg.shape[0]
    slots, rows = p16.shape[1:]
    hd = kv.shape[2] // 2 // KV_HEADS
    block = rows // tokens * hd
    smem = pl.BlockSpec(memory_space=pltpu.SMEM)
    full = pl.BlockSpec((1, slots, rows), lambda i: (i, 0, 0))
    cut = pl.BlockSpec((tokens, block), lambda i: (0, i))
    shape = jax.ShapeDtypeStruct((tokens, KV_HEADS * block), jnp.bfloat16)
    return pl.pallas_call(
        outputs_kernel,
        grid=(KV_HEADS,),
        in_specs=[
            smem,
            smem,
            pl.BlockSpec((1, tokens), lambda i: (0, 0)),
            full,
            full,
            pl.BlockSpec((2, slots, hd), lambda i: (0, 0, i)),
            pl.BlockSpec((2, slots, hd), lambda i: (0, 0, KV_HEADS + i)),
        ],
        out_specs=[cut, cut],
        out_shape=[shape, shape],
        compiler_params=pltpu.CompilerParams(vmem_limit_bytes=16 * 1024 * 1024),
        cost_estimate=pl.CostEstimate(flops=5 * 10**9, bytes_accessed=12 * p16.size, transcendentals=0),
    )(seg, gate, seg.reshape(1, tokens), p16, ds16, kv, kv)


def scores_kernel(
    mine,
    cols,
    folded,
    seg_s,
    cnt_s,
    gate_s,
    seg_v,
    q_ref,
    dy_ref,
    own,
    other,
    p16,
    ds16,
    kv_out,
    part_own,
    part_other,
    g_ref,
    kv,
    acc,
    qc,
    dc,
    rowsel,
    sbuf,
    dbuf,
    bias,
    sems,
    fetched,
):
    step = pl.program_id(0)
    heads = pl.num_programs(0)
    tokens = seg_v.shape[1]
    slots, width = kv.shape[1], kv.shape[2] // 2
    half = slots // 2
    hd = width // heads
    group = qc.shape[0] // tokens
    scale = 1.0 / hd**0.5
    core, xpos = lax.axis_index("core"), lax.axis_index("x")
    ypos, zpos = lax.axis_index("y"), lax.axis_index("z")
    img_a, img_b = seg_s[0], seg_s[tokens - 1]

    def place(img):
        return img % 2, (img // 2) ^ xpos

    def fetch(head, start):
        for i, img in enumerate((img_a, img_b)):
            par, dx = place(img)
            for src, mask in ((own, par == core), (other, par != core)):

                @pl.when(mask)
                def _():
                    for h in range(2):
                        for lane in (head * hd, width + head * hd):
                            lanes = pl.ds(lane, hd)
                            c = pltpu.make_async_copy(
                                src.at[dx, h, :, lanes],
                                kv.at[i, pl.ds(h * half, half), lanes],
                                fetched.at[head],
                            )
                            c.start() if start else c.wait()

    in_a = seg_v[...] == img_a
    tg = jnp.tanh(jnp.full((1, hd), gate_s[0], jnp.float32))

    @pl.when(step == 0)
    def _():
        for h in range(KV_HEADS):
            fetch(h, True)
        acc[...] = jnp.zeros_like(acc)
        g_ref[...] = jnp.zeros_like(g_ref)
        n = lax.broadcasted_iota(jnp.int32, (slots, tokens), 0)
        z, y = n // mine % cols, (n // half) ^ ypos
        if folded:
            z = z ^ zpos
        tile = (z * (2 * mine) + y * mine + n % mine) // TILE_TOK
        bias[...] = jnp.where(tile < jnp.where(in_a, cnt_s[img_a], cnt_s[img_b]), 0.0, NEG)
        side_a = jnp.broadcast_to(in_a.astype(jnp.float32), (hd, tokens)).T
        rowsel[0] = side_a.astype(jnp.bfloat16)
        rowsel[1] = (1.0 - side_a).astype(jnp.bfloat16)
    for h in range(KV_HEADS):

        @pl.when(step == h)
        def _():
            fetch(h, False)

    @pl.when(step == heads - 1)
    def _():
        pltpu.make_async_copy(kv, kv_out, sems.at[2]).start()

    kcols = pl.ds(pl.multiple_of(step * hd, hd), hd)
    vcols = pl.ds(pl.multiple_of(width + step * hd, hd), hd)
    kcat = jnp.concatenate([kv[0, :, kcols], kv[1, :, kcols]], axis=1)
    vcat = jnp.concatenate([kv[0, :, vcols], kv[1, :, vcols]], axis=1)
    for g in range(group):
        feats = slice(g * hd, (g + 1) * hd)
        rows = slice(g * tokens, (g + 1) * tokens)
        q, dy = q_ref[:, feats], dy_ref[:, feats]
        for i in range(2):
            side = slice(i * hd, (i + 1) * hd)
            qc[rows, side] = q * rowsel[i]
            dc[rows, side] = dy * rowsel[i]

    span = 2 * tokens
    blocks = group // 2
    strips = [slice(i, i + STRIP) for i in range(0, slots, STRIP)]
    tg2 = jnp.concatenate([tg, tg], axis=1)

    def fold8(x):
        return jnp.sum(x.reshape(x.shape[0] // 8, 8, x.shape[1]), axis=0)

    def slot_grads(lo, hi):
        rows = slice(lo * span, hi * span)
        return mm(ds16[0, :, rows], qc[rows, :], NN), mm(p16[0, :, rows], dc[rows, :], NN)

    dk = dv = 0.0
    tops, invs, deltas = {}, {}, {}
    for t in range(blocks + 2):
        new, mid, old = t, t - 1, t - 2
        if new < blocks:
            rows = slice(new * span, (new + 1) * span)
            s = mm(kcat, qc[rows, :], NT)
            dbuf[new % 3] = mm(vcat, dc[rows, :], NT)
            top = jnp.full((8, span), NEG, jnp.float32)
        norm = dots = jnp.zeros((8, span), jnp.float32)
        for strip in strips:
            if old >= 0:
                rows = slice(old * span, (old + 1) * span)
                p = sbuf[old % 3, strip] * invs[old]
                p16[0, strip, rows] = p.astype(jnp.bfloat16)
                ds16[0, strip, rows] = (p * (dbuf[old % 3, strip] - deltas[old])).astype(jnp.bfloat16)
            if 0 <= mid < blocks:
                e = jnp.exp2(sbuf[mid % 3, strip] * (scale * LOG2E) - tops[mid])
                sbuf[mid % 3, strip] = e
                norm = norm + fold8(e)
                dots = dots + fold8(e * dbuf[mid % 3, strip])
            if new < blocks:
                x = s[strip] + jnp.concatenate([bias[strip], bias[strip]], axis=1)
                sbuf[new % 3, strip] = x
                top = jnp.maximum(top, jnp.max(x.reshape(STRIP // 8, 8, span), axis=0))
        if new < blocks:
            tops[new] = jnp.max(top, axis=0, keepdims=True) * (scale * LOG2E)
        if 0 <= mid < blocks:
            invs[mid] = 1.0 / jnp.sum(norm, axis=0, keepdims=True)
            deltas[mid] = invs[mid] * jnp.sum(dots, axis=0, keepdims=True)
        if old >= 0 and old % 2:
            more = slot_grads(old - 1, old + 1)
            dk, dv = dk + more[0], dv + more[1]
    dk = (scale * tg2 * dk).astype(jnp.bfloat16)
    g_ref[...] += fold8((dv * vcat.astype(jnp.float32))[:, :hd] + (dv * vcat.astype(jnp.float32))[:, hd:])
    dv = (tg2 * dv).astype(jnp.bfloat16)
    pieces = 2 * acc.shape[3]
    per = slots // pieces
    krows = pl.ds(pl.multiple_of(step * per, per), per)
    vrows = pl.ds(pl.multiple_of((heads + step) * per, per), per)
    for img, lanes in ((img_b, slice(hd, 2 * hd)), (img_a, slice(0, hd))):
        par, dx = place(img)
        for j in range(pieces):
            at = slice(j * per, (j + 1) * per)
            acc[par, dx, j // (pieces // 2), j % (pieces // 2), krows] = dk[at, lanes]
            acc[par, dx, j // (pieces // 2), j % (pieces // 2), vrows] = dv[at, lanes]

    def leave(rows, i):
        lay = slice(None), slice(None), slice(None), rows
        return (
            pltpu.make_async_copy(acc.at[(1 - core,) + lay], part_other.at[lay], sems.at[3 + 2 * i]),
            pltpu.make_async_copy(acc.at[(core,) + lay], part_own.at[lay], sems.at[4 + 2 * i]),
        )

    def head_rows(h):
        return pl.ds(h * per, per), pl.ds((heads + h) * per, per)

    for h in range(KV_HEADS):

        @pl.when(step == h)
        def _():
            for i, rows in enumerate(head_rows(h)):
                for c in leave(rows, 2 * h + i):
                    c.start()

    @pl.when(step == heads - 1)
    def _():
        left = jnp.broadcast_to(jnp.sum(g_ref[...], axis=0, keepdims=True), (GROWS, hd))
        line = lax.broadcasted_iota(jnp.int32, (GROWS, hd), 0)
        digits = jnp.zeros((GROWS, hd), jnp.float32)
        for i in range(GROWS):
            unit = 4.0 ** (GTOP - i)
            d = jnp.round(left * (1.0 / unit))
            left = left - d * unit
            digits = jnp.where(line == i, d, digits)
        digits = digits.astype(jnp.bfloat16)
        g_ref[...] = jnp.broadcast_to(1.0 - tg * tg, g_ref.shape)
        for i in range(8):
            for j in range(pieces // 2):
                acc[i // 4, i // 2 % 2, i % 2, j, 2 * heads * per :] = digits
        tail = leave(pl.ds(2 * KV_HEADS * per, GROWS), 2 * KV_HEADS)
        for c in tail:
            c.start()
        for h in range(KV_HEADS):
            for i, rows in enumerate(head_rows(h)):
                for c in leave(rows, 2 * h + i):
                    c.wait()
        for c in tail:
            c.wait()
        pltpu.make_async_copy(kv, kv_out, sems.at[2]).wait()


def scores(mine, cols, folded, seg, counts, gate, q, dy, own, other):
    tokens = seg.shape[0]
    slots, width2 = 2 * own.shape[2], own.shape[3]
    hd = width2 // 2 // KV_HEADS
    block = q.shape[1] // KV_HEADS
    rows = block // hd * tokens
    smem = pl.BlockSpec(memory_space=pltpu.SMEM)
    hbm = pl.BlockSpec(memory_space=pl.ANY)
    gspec = pl.BlockSpec((8, hd), lambda i: (0, 0))
    full = pl.BlockSpec((1, slots, rows), lambda i: (i, 0, 0))
    pieces = 8 if folded else 2
    part = (2, 2, pieces // 2, 2 * KV_HEADS * (slots // pieces) + GROWS, hd)
    return pl.pallas_call(
        functools.partial(scores_kernel, mine, cols, folded),
        grid=(KV_HEADS,),
        in_specs=[
            smem,
            smem,
            smem,
            pl.BlockSpec((1, tokens), lambda i: (0, 0)),
        ]
        + [pl.BlockSpec((tokens, block), lambda i: (0, i))] * 2
        + [hbm, hbm],
        out_specs=[full, full, hbm, hbm, hbm, gspec],
        out_shape=[
            jax.ShapeDtypeStruct((KV_HEADS, slots, rows), jnp.bfloat16),
            jax.ShapeDtypeStruct((KV_HEADS, slots, rows), jnp.bfloat16),
            jax.ShapeDtypeStruct((2, slots, width2), jnp.bfloat16),
            jax.ShapeDtypeStruct(part, jnp.bfloat16),
            jax.ShapeDtypeStruct(part, jnp.bfloat16),
            jax.ShapeDtypeStruct((8, hd), jnp.float32),
        ],
        scratch_shapes=[
            pltpu.VMEM((2, slots, width2), jnp.bfloat16),
            pltpu.VMEM((2,) + part, jnp.bfloat16),
            pltpu.VMEM((rows, 2 * hd), jnp.bfloat16),
            pltpu.VMEM((rows, 2 * hd), jnp.bfloat16),
            pltpu.VMEM((2, tokens, hd), jnp.bfloat16),
            pltpu.VMEM((3, slots, 2 * tokens), jnp.float32),
            pltpu.VMEM((3, slots, 2 * tokens), jnp.float32),
            pltpu.VMEM((slots, tokens), jnp.float32),
            pltpu.SemaphoreType.DMA((5 + 4 * KV_HEADS,)),
            pltpu.SemaphoreType.DMA((KV_HEADS,)),
        ],
        compiler_params=pltpu.CompilerParams(vmem_limit_bytes=28 * 1024 * 1024),
        cost_estimate=pl.CostEstimate(
            flops=8 * KV_HEADS * rows * slots * hd * 2,
            bytes_accessed=12 * KV_HEADS * rows * slots,
            transcendentals=KV_HEADS * rows * slots,
        ),
    )(seg, counts, gate, seg.reshape(1, tokens), q, dy, own, other)


def add_up(refs, at):
    total = refs[0][at].astype(jnp.float32)
    for r in refs[1:]:
        total = total + r[at].astype(jnp.float32)
    return total


def finish_kernel(mine, gate, *refs):
    ins, (dk_ref, dv_ref, g_ref) = refs[:-3], refs[-3:]
    hd = ins[0].shape[1]
    for h in range(2 * KV_HEADS):
        out = (dk_ref, dv_ref)[h // KV_HEADS]
        lanes = slice(h % KV_HEADS * hd, (h % KV_HEADS + 1) * hd)
        out[:, lanes] = add_up(ins, slice(h * mine, (h + 1) * mine))
    digits = add_up(ins, slice(2 * KV_HEADS * mine, None))
    line = lax.broadcasted_iota(jnp.int32, digits.shape, 0)
    units = jnp.zeros(digits.shape, jnp.float32)
    for i in range(GROWS):
        units = jnp.where(line == i, 4.0 ** (GTOP - i), units)
    g_ref[0] = jnp.sum(jnp.sum(digits * units, axis=0, keepdims=True) * gate[0:1, :])


def finish(mine, gate, parts):
    hd = parts[0].shape[1]
    smem = pl.BlockSpec(memory_space=pltpu.SMEM)
    vmem = pl.BlockSpec(memory_space=pltpu.VMEM)
    full = jax.ShapeDtypeStruct((mine, KV_HEADS * hd), jnp.float32)
    return pl.pallas_call(
        functools.partial(finish_kernel, mine),
        in_specs=[vmem] + [vmem] * len(parts),
        out_specs=[vmem, vmem, smem],
        out_shape=[full, full, jax.ShapeDtypeStruct((1,), jnp.float32)],
        compiler_params=pltpu.CompilerParams(vmem_limit_bytes=4 * 1024 * 1024),
    )(gate, *parts)


def local(queries, keys, values, seg_image, tile_counts, gate, cotangent):
    f32, bf16 = jnp.float32, jnp.bfloat16
    mine, width = keys.shape
    hd = width // KV_HEADS
    cols = lax.axis_size("z")
    folded = cols == 4
    half = cols * mine

    def send_z(x, k):
        return lax.ppermute(x, "z", [(i, i ^ k) for i in range(cols)])

    def send_xy(x, p):
        return lax.ppermute(x, ("x", "y"), [(i, i ^ p) for i in range(4)])

    def send_core(x):
        return lax.ppermute(x, "core", [(0, 1), (1, 0)])

    kv = jnp.concatenate([keys, values], axis=1)
    if folded:
        near = [send_xy(kv, p) for p in (2, 3)]
        line = [send_z(kv, k) for k in LINE]
        line, near = lax.optimization_barrier((jnp.concatenate(line, axis=0), near))
        kv, line = lax.optimization_barrier((kv, line))
        block = jnp.concatenate([kv, line], axis=0)
        own = [block, send_xy(block, 1), near[0], send_xy(line, 2), near[1], send_xy(line, 3)]
    else:
        line = lax.all_gather(kv, "z", axis=0, tiled=True)
        own = [line] + [send_xy(line, p) for p in PEERS]
    own = jnp.concatenate(own, axis=0).reshape(2, 2, half, 2 * width)
    other = send_core(own)
    p16, ds16, kv_used, part_own, part_other, g = scores(
        mine, cols, folded, seg_image, tile_counts, gate, queries, cotangent, own, other
    )

    got, p16 = lax.optimization_barrier((send_core(part_other), p16))
    part = (part_own.astype(f32) + got.astype(f32)).astype(bf16)
    y, dq = outputs(seg_image, gate, p16, ds16, kv_used)
    part = part.reshape((4,) + part.shape[2:])
    if folded:
        parts = [part[0, 0]] + [send_xy(part[p, 0], p) for p in PEERS]
        line = part[0, 1:].astype(f32)
        for p in PEERS:
            line = line + send_xy(part[p, 1:], p).astype(f32)
        line, y = lax.optimization_barrier((line.astype(bf16), y))
        parts += [send_z(line[k - 1], k) for k in LINE[::-1]]
    else:
        line = part[0, 0].astype(f32)
        for p in PEERS:
            line = line + send_xy(part[p, 0], p).astype(f32)
        grads, gates = line[:-GROWS].reshape(2 * KV_HEADS, cols, mine, hd), line[-GROWS:]
        grads = lax.psum_scatter(grads, "z", scatter_dimension=1, tiled=True)
        parts = [jnp.concatenate([grads.reshape(-1, hd), lax.psum(gates, "z")], axis=0)]
    return (y, dq, *finish(mine, g, parts))


def solution(mesh):
    section, mp = mesh.shape["section"], mesh.shape["mp"]
    fine = Mesh(mesh.devices.reshape(section // 2, 2, mp // 2, 2), AXES)
    rows = P(AXES, None)
    return jax.shard_map(
        local,
        mesh=fine,
        in_specs=(rows, rows, rows, P(AXES), P(), P(), rows),
        out_specs=(rows, rows, rows, rows, P()),
        check_vma=False,
    )
```

```python
import functools

import jax
import jax.numpy as jnp
from jax import lax
from jax.experimental import pallas as pl
from jax.experimental.pallas import tpu as pltpu
from jax.sharding import Mesh
from jax.sharding import PartitionSpec as P

KV_HEADS = 4
TILE_TOK = 64
IMG_TOK = 256
AXES = ("x", "core", "z", "y")
NEG = -1e30
LOG2E = 1.4426950408889634
GROWS = 16
GTOP = 8
STRIP = 16
LINE = PEERS = (1, 2, 3)

NT = (((1,), (1,)), ((), ()))
NN = (((1,), (0,)), ((), ()))


def mm(a, b, dims):
    return lax.dot_general(a, b, dims, preferred_element_type=jnp.float32)


def outputs_kernel(seg_s, gate_s, seg_v, p16, ds16, k_ref, v_ref, y_ref, dq_ref):
    tokens = y_ref.shape[0]
    hd = k_ref.shape[2]
    span = 2 * tokens
    in_a = seg_v[...] == seg_s[0]
    in_a2 = jnp.concatenate([in_a, in_a], axis=1)
    tg2 = jnp.tanh(jnp.full((1, span), gate_s[0], jnp.float32))
    kcat_t = jnp.concatenate([k_ref[0], k_ref[1]], axis=1).T
    vcat_t = jnp.concatenate([v_ref[0], v_ref[1]], axis=1).T
    for h in range(y_ref.shape[1] // hd // 2):
        rows = slice(h * span, (h + 1) * span)
        o = mm(vcat_t, p16[0, :, rows], NN)
        o = (tg2 * jnp.where(in_a2, o[:hd], o[hd:])).astype(jnp.bfloat16)
        dq = mm(kcat_t, ds16[0, :, rows], NN)
        dq = (tg2 * (1.0 / hd**0.5) * jnp.where(in_a2, dq[:hd], dq[hd:])).astype(jnp.bfloat16)
        for j in range(2):
            feats = slice((2 * h + j) * hd, (2 * h + j + 1) * hd)
            toks = slice(j * tokens, (j + 1) * tokens)
            y_ref[:, feats] = o[:, toks].T
            dq_ref[:, feats] = dq[:, toks].T


def outputs(seg, gate, p16, ds16, kv):
    tokens = seg.shape[0]
    slots, rows = p16.shape[1:]
    hd = kv.shape[2] // 2 // KV_HEADS
    block = rows // tokens * hd
    smem = pl.BlockSpec(memory_space=pltpu.SMEM)
    full = pl.BlockSpec((1, slots, rows), lambda i: (i, 0, 0))
    cut = pl.BlockSpec((tokens, block), lambda i: (0, i))
    shape = jax.ShapeDtypeStruct((tokens, KV_HEADS * block), jnp.bfloat16)
    return pl.pallas_call(
        outputs_kernel,
        grid=(KV_HEADS,),
        in_specs=[
            smem,
            smem,
            pl.BlockSpec((1, tokens), lambda i: (0, 0)),
            full,
            full,
            pl.BlockSpec((2, slots, hd), lambda i: (0, 0, i)),
            pl.BlockSpec((2, slots, hd), lambda i: (0, 0, KV_HEADS + i)),
        ],
        out_specs=[cut, cut],
        out_shape=[shape, shape],
        compiler_params=pltpu.CompilerParams(vmem_limit_bytes=16 * 1024 * 1024),
        cost_estimate=pl.CostEstimate(flops=5 * 10**9, bytes_accessed=12 * p16.size, transcendentals=0),
    )(seg, gate, seg.reshape(1, tokens), p16, ds16, kv, kv)


def scores_kernel(
    mine,
    cols,
    folded,
    seg_s,
    cnt_s,
    gate_s,
    seg_v,
    q_ref,
    dy_ref,
    own,
    other,
    p16,
    ds16,
    kv_out,
    part_own,
    part_other,
    g_ref,
    kv,
    acc,
    qc,
    dc,
    rowsel,
    sbuf,
    dbuf,
    bias,
    sems,
    fetched,
):
    step = pl.program_id(0)
    heads = pl.num_programs(0)
    tokens = seg_v.shape[1]
    slots, width = kv.shape[1], kv.shape[2] // 2
    half = slots // 2
    hd = width // heads
    group = qc.shape[0] // tokens
    scale = 1.0 / hd**0.5
    core, xpos = lax.axis_index("core"), lax.axis_index("x")
    ypos, zpos = lax.axis_index("y"), lax.axis_index("z")
    img_a, img_b = seg_s[0], seg_s[tokens - 1]

    def place(img):
        return img % 2, (img // 2) ^ xpos

    def fetch(head, start):
        for i, img in enumerate((img_a, img_b)):
            par, dx = place(img)
            for src, mask in ((own, par == core), (other, par != core)):

                @pl.when(mask)
                def _():
                    for h in range(2):
                        for lane in (head * hd, width + head * hd):
                            lanes = pl.ds(lane, hd)
                            c = pltpu.make_async_copy(
                                src.at[dx, h, :, lanes],
                                kv.at[i, pl.ds(h * half, half), lanes],
                                fetched.at[head],
                            )
                            c.start() if start else c.wait()

    in_a = seg_v[...] == img_a
    tg = jnp.tanh(jnp.full((1, hd), gate_s[0], jnp.float32))

    @pl.when(step == 0)
    def _():
        for h in range(KV_HEADS):
            fetch(h, True)
        acc[...] = jnp.zeros_like(acc)
        g_ref[...] = jnp.zeros_like(g_ref)
        n = lax.broadcasted_iota(jnp.int32, (slots, tokens), 0)
        z, y = n // mine % cols, (n // half) ^ ypos
        if folded:
            z = z ^ zpos
        tile = (z * (2 * mine) + y * mine + n % mine) // TILE_TOK
        bias[...] = jnp.where(tile < jnp.where(in_a, cnt_s[img_a], cnt_s[img_b]), 0.0, NEG)
        side_a = jnp.broadcast_to(in_a.astype(jnp.float32), (hd, tokens)).T
        rowsel[0] = side_a.astype(jnp.bfloat16)
        rowsel[1] = (1.0 - side_a).astype(jnp.bfloat16)
    for h in range(KV_HEADS):

        @pl.when(step == h)
        def _():
            fetch(h, False)

    @pl.when(step == heads - 1)
    def _():
        pltpu.make_async_copy(kv, kv_out, sems.at[2]).start()

    kcols = pl.ds(pl.multiple_of(step * hd, hd), hd)
    vcols = pl.ds(pl.multiple_of(width + step * hd, hd), hd)
    kcat = jnp.concatenate([kv[0, :, kcols], kv[1, :, kcols]], axis=1)
    vcat = jnp.concatenate([kv[0, :, vcols], kv[1, :, vcols]], axis=1)
    for g in range(group):
        feats = slice(g * hd, (g + 1) * hd)
        rows = slice(g * tokens, (g + 1) * tokens)
        q, dy = q_ref[:, feats], dy_ref[:, feats]
        for i in range(2):
            side = slice(i * hd, (i + 1) * hd)
            qc[rows, side] = q * rowsel[i]
            dc[rows, side] = dy * rowsel[i]

    span = 4 * tokens
    blocks = group // 4
    strips = [slice(i, i + STRIP) for i in range(0, slots, STRIP)]
    tg2 = jnp.concatenate([tg, tg], axis=1)

    def fold8(x):
        return jnp.sum(x.reshape(x.shape[0] // 8, 8, x.shape[1]), axis=0)

    def slot_grads(lo, hi):
        rows = slice(lo * span, hi * span)
        return mm(ds16[0, :, rows], qc[rows, :], NN), mm(p16[0, :, rows], dc[rows, :], NN)

    dk = dv = 0.0
    tops, invs, deltas = {}, {}, {}
    for t in range(blocks + 2):
        new, mid, old = t, t - 1, t - 2
        if new < blocks:
            rows = slice(new * span, (new + 1) * span)
            s = mm(kcat, qc[rows, :], NT)
            dbuf[new % 3] = mm(vcat, dc[rows, :], NT)
            top = jnp.full((8, span), NEG, jnp.float32)
        norm = dots = jnp.zeros((8, span), jnp.float32)
        for strip in strips:
            if old >= 0:
                rows = slice(old * span, (old + 1) * span)
                p = sbuf[old % 3, strip] * invs[old]
                p16[0, strip, rows] = p.astype(jnp.bfloat16)
                ds16[0, strip, rows] = (p * (dbuf[old % 3, strip] - deltas[old])).astype(jnp.bfloat16)
            if 0 <= mid < blocks:
                e = jnp.exp2(sbuf[mid % 3, strip] * (scale * LOG2E) - tops[mid])
                sbuf[mid % 3, strip] = e
                norm = norm + fold8(e)
                dots = dots + fold8(e * dbuf[mid % 3, strip])
            if new < blocks:
                x = s[strip] + jnp.concatenate([bias[strip]] * 4, axis=1)
                sbuf[new % 3, strip] = x
                top = jnp.maximum(top, jnp.max(x.reshape(STRIP // 8, 8, span), axis=0))
        if new < blocks:
            tops[new] = jnp.max(top, axis=0, keepdims=True) * (scale * LOG2E)
        if 0 <= mid < blocks:
            invs[mid] = 1.0 / jnp.sum(norm, axis=0, keepdims=True)
            deltas[mid] = invs[mid] * jnp.sum(dots, axis=0, keepdims=True)
        if old >= 0:
            more = slot_grads(old, old + 1)
            dk, dv = dk + more[0], dv + more[1]
    dk = (scale * tg2 * dk).astype(jnp.bfloat16)
    g_ref[...] += fold8((dv * vcat.astype(jnp.float32))[:, :hd] + (dv * vcat.astype(jnp.float32))[:, hd:])
    dv = (tg2 * dv).astype(jnp.bfloat16)
    pieces = 2 * acc.shape[3]
    per = slots // pieces
    krows = pl.ds(pl.multiple_of(step * per, per), per)
    vrows = pl.ds(pl.multiple_of((heads + step) * per, per), per)
    for img, lanes in ((img_b, slice(hd, 2 * hd)), (img_a, slice(0, hd))):
        par, dx = place(img)
        for j in range(pieces):
            at = slice(j * per, (j + 1) * per)
            acc[par, dx, j // (pieces // 2), j % (pieces // 2), krows] = dk[at, lanes]
            acc[par, dx, j // (pieces // 2), j % (pieces // 2), vrows] = dv[at, lanes]

    def leave(rows, i):
        lay = slice(None), slice(None), slice(None), rows
        return (
            pltpu.make_async_copy(acc.at[(1 - core,) + lay], part_other.at[lay], sems.at[3 + 2 * i]),
            pltpu.make_async_copy(acc.at[(core,) + lay], part_own.at[lay], sems.at[4 + 2 * i]),
        )

    def head_rows(h):
        return pl.ds(h * per, per), pl.ds((heads + h) * per, per)

    for h in range(KV_HEADS):

        @pl.when(step == h)
        def _():
            for i, rows in enumerate(head_rows(h)):
                for c in leave(rows, 2 * h + i):
                    c.start()

    @pl.when(step == heads - 1)
    def _():
        left = jnp.broadcast_to(jnp.sum(g_ref[...], axis=0, keepdims=True), (GROWS, hd))
        line = lax.broadcasted_iota(jnp.int32, (GROWS, hd), 0)
        digits = jnp.zeros((GROWS, hd), jnp.float32)
        for i in range(GROWS):
            unit = 4.0 ** (GTOP - i)
            d = jnp.round(left * (1.0 / unit))
            left = left - d * unit
            digits = jnp.where(line == i, d, digits)
        digits = digits.astype(jnp.bfloat16)
        g_ref[...] = jnp.broadcast_to(1.0 - tg * tg, g_ref.shape)
        for i in range(8):
            for j in range(pieces // 2):
                acc[i // 4, i // 2 % 2, i % 2, j, 2 * heads * per :] = digits
        tail = leave(pl.ds(2 * KV_HEADS * per, GROWS), 2 * KV_HEADS)
        for c in tail:
            c.start()
        for h in range(KV_HEADS):
            for i, rows in enumerate(head_rows(h)):
                for c in leave(rows, 2 * h + i):
                    c.wait()
        for c in tail:
            c.wait()
        pltpu.make_async_copy(kv, kv_out, sems.at[2]).wait()


def scores(mine, cols, folded, seg, counts, gate, q, dy, own, other):
    tokens = seg.shape[0]
    slots, width2 = 2 * own.shape[2], own.shape[3]
    hd = width2 // 2 // KV_HEADS
    block = q.shape[1] // KV_HEADS
    rows = block // hd * tokens
    smem = pl.BlockSpec(memory_space=pltpu.SMEM)
    hbm = pl.BlockSpec(memory_space=pl.ANY)
    gspec = pl.BlockSpec((8, hd), lambda i: (0, 0))
    full = pl.BlockSpec((1, slots, rows), lambda i: (i, 0, 0))
    pieces = 8 if folded else 2
    part = (2, 2, pieces // 2, 2 * KV_HEADS * (slots // pieces) + GROWS, hd)
    return pl.pallas_call(
        functools.partial(scores_kernel, mine, cols, folded),
        grid=(KV_HEADS,),
        in_specs=[
            smem,
            smem,
            smem,
            pl.BlockSpec((1, tokens), lambda i: (0, 0)),
        ]
        + [pl.BlockSpec((tokens, block), lambda i: (0, i))] * 2
        + [hbm, hbm],
        out_specs=[full, full, hbm, hbm, hbm, gspec],
        out_shape=[
            jax.ShapeDtypeStruct((KV_HEADS, slots, rows), jnp.bfloat16),
            jax.ShapeDtypeStruct((KV_HEADS, slots, rows), jnp.bfloat16),
            jax.ShapeDtypeStruct((2, slots, width2), jnp.bfloat16),
            jax.ShapeDtypeStruct(part, jnp.bfloat16),
            jax.ShapeDtypeStruct(part, jnp.bfloat16),
            jax.ShapeDtypeStruct((8, hd), jnp.float32),
        ],
        scratch_shapes=[
            pltpu.VMEM((2, slots, width2), jnp.bfloat16),
            pltpu.VMEM((2,) + part, jnp.bfloat16),
            pltpu.VMEM((rows, 2 * hd), jnp.bfloat16),
            pltpu.VMEM((rows, 2 * hd), jnp.bfloat16),
            pltpu.VMEM((2, tokens, hd), jnp.bfloat16),
            pltpu.VMEM((3, slots, 4 * tokens), jnp.float32),
            pltpu.VMEM((3, slots, 4 * tokens), jnp.float32),
            pltpu.VMEM((slots, tokens), jnp.float32),
            pltpu.SemaphoreType.DMA((5 + 4 * KV_HEADS,)),
            pltpu.SemaphoreType.DMA((KV_HEADS,)),
        ],
        compiler_params=pltpu.CompilerParams(vmem_limit_bytes=28 * 1024 * 1024),
        cost_estimate=pl.CostEstimate(
            flops=8 * KV_HEADS * rows * slots * hd * 2,
            bytes_accessed=12 * KV_HEADS * rows * slots,
            transcendentals=KV_HEADS * rows * slots,
        ),
    )(seg, counts, gate, seg.reshape(1, tokens), q, dy, own, other)


def add_up(refs, at):
    total = refs[0][at].astype(jnp.float32)
    for r in refs[1:]:
        total = total + r[at].astype(jnp.float32)
    return total


def finish_kernel(mine, gate, *refs):
    ins, (dk_ref, dv_ref, g_ref) = refs[:-3], refs[-3:]
    hd = ins[0].shape[1]
    for h in range(2 * KV_HEADS):
        out = (dk_ref, dv_ref)[h // KV_HEADS]
        lanes = slice(h % KV_HEADS * hd, (h % KV_HEADS + 1) * hd)
        out[:, lanes] = add_up(ins, slice(h * mine, (h + 1) * mine))
    digits = add_up(ins, slice(2 * KV_HEADS * mine, None))
    line = lax.broadcasted_iota(jnp.int32, digits.shape, 0)
    units = jnp.zeros(digits.shape, jnp.float32)
    for i in range(GROWS):
        units = jnp.where(line == i, 4.0 ** (GTOP - i), units)
    g_ref[0] = jnp.sum(jnp.sum(digits * units, axis=0, keepdims=True) * gate[0:1, :])


def finish(mine, gate, parts):
    hd = parts[0].shape[1]
    smem = pl.BlockSpec(memory_space=pltpu.SMEM)
    vmem = pl.BlockSpec(memory_space=pltpu.VMEM)
    full = jax.ShapeDtypeStruct((mine, KV_HEADS * hd), jnp.float32)
    return pl.pallas_call(
        functools.partial(finish_kernel, mine),
        in_specs=[vmem] + [vmem] * len(parts),
        out_specs=[vmem, vmem, smem],
        out_shape=[full, full, jax.ShapeDtypeStruct((1,), jnp.float32)],
        compiler_params=pltpu.CompilerParams(vmem_limit_bytes=4 * 1024 * 1024),
    )(gate, *parts)


def local(queries, keys, values, seg_image, tile_counts, gate, cotangent):
    f32, bf16 = jnp.float32, jnp.bfloat16
    mine, width = keys.shape
    hd = width // KV_HEADS
    cols = lax.axis_size("z")
    folded = cols == 4
    half = cols * mine

    def send_z(x, k):
        return lax.ppermute(x, "z", [(i, i ^ k) for i in range(cols)])

    def send_xy(x, p):
        return lax.ppermute(x, ("x", "y"), [(i, i ^ p) for i in range(4)])

    def send_core(x):
        return lax.ppermute(x, "core", [(0, 1), (1, 0)])

    kv = jnp.concatenate([keys, values], axis=1)
    if folded:
        near = [send_xy(kv, p) for p in (1, 2)]
        line = [send_z(kv, k) for k in LINE]
        line, near = lax.optimization_barrier((jnp.concatenate(line, axis=0), near))
        kv, line = lax.optimization_barrier((kv, line))
        block = jnp.concatenate([kv, line], axis=0)
        diag = send_xy(block, 3)
        own = [block, near[0], send_xy(line, 1), near[1], send_xy(line, 2), diag]
    else:
        line = lax.all_gather(kv, "z", axis=0, tiled=True)
        own = [line] + [send_xy(line, p) for p in PEERS]
    own = jnp.concatenate(own, axis=0).reshape(2, 2, half, 2 * width)
    other = send_core(own)
    p16, ds16, kv_used, part_own, part_other, g = scores(
        mine, cols, folded, seg_image, tile_counts, gate, queries, cotangent, own, other
    )

    got, p16 = lax.optimization_barrier((send_core(part_other), p16))
    part = (part_own.astype(f32) + got.astype(f32)).astype(bf16)
    y, dq = outputs(seg_image, gate, p16, ds16, kv_used)
    part = part.reshape((4,) + part.shape[2:])
    if folded:
        parts = [part[0, 0]] + [send_xy(part[p, 0], p) for p in PEERS]
        line = part[0, 1:].astype(f32)
        for p in PEERS:
            line = line + send_xy(part[p, 1:], p).astype(f32)
        line, y = lax.optimization_barrier((line.astype(bf16), y))
        parts += [send_z(line[k - 1], k) for k in LINE[::-1]]
    else:
        line = part[0, 0].astype(f32)
        for p in PEERS:
            line = line + send_xy(part[p, 0], p).astype(f32)
        grads, gates = line[:-GROWS].reshape(2 * KV_HEADS, cols, mine, hd), line[-GROWS:]
        grads = lax.psum_scatter(grads, "z", scatter_dimension=1, tiled=True)
        parts = [jnp.concatenate([grads.reshape(-1, hd), lax.psum(gates, "z")], axis=0)]
    return (y, dq, *finish(mine, g, parts))


def solution(mesh):
    section, mp = mesh.shape["section"], mesh.shape["mp"]
    fine = Mesh(mesh.devices.reshape(section // 2, 2, mp // 2, 2), AXES)
    rows = P(AXES, None)
    return jax.shard_map(
        local,
        mesh=fine,
        in_specs=(rows, rows, rows, P(AXES), P(), P(), rows),
        out_specs=(rows, rows, rows, rows, P()),
        check_vma=False,
    )
```
